128 devices in a mesh: replica: 8 (over x, y_hi), fsdp: 16 (over z, y_lo, core).
Axes of the slice: x: 4, y: 4 (y_hi: 2, y_lo: 2; y = y_hi * 2 + y_lo), z: 4, core: 2. Of those that a mesh axis runs over, the one named last changes fastest.
Arguments:
- hidden_in: bfloat16 [8, 8192, 8192], P('replica', 'fsdp'), may hold values from -6 to 6
- value_cot: bfloat16 [8, 8192, 1024], P('replica', 'fsdp'), may hold values from -6 to 6
- proj_weight: bfloat16 [8, 8192, 1024], P('replica', 'fsdp'), may hold values from -0.0625 to 0.0625
- norm_gain: float32 [8, 8192], P('replica'), may hold values from 0.5 to 1.5
- anchor: float32 [8, 16, 512, 128], P(None, 'fsdp', 'replica'), may hold values from -0.0625 to 0.0625
- momentum: float32 [8, 16, 512, 128], P(None, 'fsdp', 'replica'), may hold values from -0.078125 to 0.078125
- excluded: int32 [8, 1024], P('replica'), may hold values from 0 to 8191
- fragment: int32 [1], replicated, may hold values from 0 to 7
Outputs:
- values_out: bfloat16 [8, 8192, 1024], P('replica', 'fsdp')
- hidden_grad: bfloat16 [8, 8192, 8192], P('replica', 'fsdp')
- weight_out: bfloat16 [8, 8192, 1024], P('replica', 'fsdp')
- gain_out: float32 [8, 8192], P('replica')
- anchor_out: float32 [8, 16, 512, 128], P(None, 'fsdp', 'replica')
- momentum_out: float32 [8, 16, 512, 128], P(None, 'fsdp', 'replica')
The draws below stay inside these ranges and needn't reach their ends.
Inputs may be any that keep to these rules, and one draw needn't show every extreme that they name: `excluded`: row indices within the replica's batch of 8192 rows; an index may repeat.
All inputs are finite; a program needn't handle non-finite values.
Results may differ from the reference program's by a relative error of at most 0.023.
Values may be sent and summed in bfloat16 or wider, within the bound.
No kernel may reach another device: no remote copies, remote signals or barrier semaphores. Data moves between devices by JAX's collectives and lax.ppermute only.
A program may use at most 192 MiB of HBM per device.

```python
import jax
import jax.numpy as jnp
from jax import lax

D = 8192
KV = 1024
FRAGS = 8
TOK_DEV = 512
TOKENS = 8192
FC = 128
EXCL = 1024
N_REPLICA = 8
N_FSDP = 16


def with_ends(drawn, key, least, largest):
    place = [jax.random.randint(jax.random.fold_in(key, axis), (), 0, length) for axis, length in enumerate(drawn.shape)]
    widest = drawn.shape.index(max(drawn.shape))
    neighbour = place[:widest] + [(place[widest] + 1) % drawn.shape[widest]] + place[widest + 1:]
    return drawn.at[tuple(place)].set(least).at[tuple(neighbour)].set(largest)


def shard_levels(key, dims, shards, smallest, high):
    level, own = 1.0, jax.random.fold_in(key, 6)
    for dim, parts in shards:
        heights = jnp.exp(jax.random.uniform(jax.random.fold_in(own, dim), (parts,), jnp.float32, smallest / len(shards), high / len(shards)))
        level = level * jnp.repeat(heights, dims[dim] // parts).reshape([-1 if axis == dim else 1 for axis in range(len(dims))])
    return level


def noise(key, dims, scale, reach, cuts=(), kind=jnp.bfloat16):
    entries = jax.random.normal(key, dims, jnp.float32) * scale
    if len(cuts) > 0:
        entries = shard_levels(key, dims, cuts, -0.22, 0.18) * entries
    return jnp.clip(entries, min=-reach, max=reach).astype(kind)


def setup_inputs(seed: int = 0) -> dict:
    key_of = jax.random.split(jax.random.key(seed), 9)
    hidden_in = noise(key_of[0], (N_REPLICA, TOKENS, D), 1.0, 6.0, ((0, 8), (1, 16)))
    value_cot = noise(key_of[1], (N_REPLICA, TOKENS, KV), 1.0, 6.0, ((0, 8), (1, 16)))
    proj_weight = noise(key_of[2], (N_REPLICA, D, KV), D ** -0.5, 0.0625, ((0, 8), (1, 16)))
    norm_gain = jnp.clip(1.0 + 0.1 * jax.random.normal(key_of[3], (N_REPLICA, D), jnp.float32), 0.5, 1.5)
    anchor = noise(key_of[4], (FRAGS, N_FSDP, D // N_FSDP, FC), D ** -0.5, 0.0625, ((1, 16), (2, 8)), jnp.float32)
    momentum = noise(key_of[5], (FRAGS, N_FSDP, D // N_FSDP, FC), 0.005, 0.078125, ((1, 16), (2, 8)), jnp.float32)
    excluded = with_ends(jax.random.randint(key_of[6], (N_REPLICA, EXCL), 0, TOKENS), jax.random.fold_in(key_of[6], 1), 0, TOKENS - 1).astype(jnp.int32)
    fragment = jax.random.randint(key_of[7], (1,), 0, FRAGS).astype(jnp.int32)
    return dict(hidden_in=hidden_in, value_cot=value_cot, proj_weight=proj_weight, norm_gain=norm_gain, anchor=anchor, momentum=momentum, excluded=excluded, fragment=fragment)


outer_momentum = 0.9
outer_rate = 0.7
mix_weight = 0.5

def one_replica(hidden_rows, cot_rows, weight, gain, excluded_rows):
    inner_rate = 0.01 / TOK_DEV ** 0.5
    gain_rate = 0.1 / TOK_DEV ** 0.5
    positions = jnp.arange(TOKENS, dtype=jnp.int32)
    hit = jnp.any(positions[:, None] == excluded_rows[None, :], axis=1)
    kept_rows = jnp.where(hit, 0.0, 1.0).astype(jnp.float32)
    values = hidden_rows.astype(jnp.float32)
    inverse = lax.rsqrt(lax.optimization_barrier(jnp.mean(values * values, axis=1, keepdims=True)) + 1e-05)
    normed = values * inverse
    scaled = (normed * gain[None, :]).astype(jnp.bfloat16)
    masked = (cot_rows.astype(jnp.float32) * kept_rows[:, None]).astype(jnp.bfloat16)
    projected = jnp.dot(scaled, weight, preferred_element_type=jnp.float32).astype(jnp.bfloat16)
    norm_grad = lax.dot_general(masked, weight, (((1,), (1,)), ((), ())), preferred_element_type=jnp.float32)
    gain_grad = lax.optimization_barrier(jnp.sum(norm_grad * normed, axis=0))
    weighted = norm_grad * gain[None, :]
    hidden_grad = ((weighted - normed * lax.optimization_barrier(jnp.mean(weighted * normed, axis=1, keepdims=True))) * inverse).astype(jnp.bfloat16)
    blocks_scaled = scaled.reshape(N_FSDP, TOK_DEV, D)
    blocks_masked = masked.reshape(N_FSDP, TOK_DEV, KV)

    def add_block(total, pair):
        term = lax.dot_general(pair[0], pair[1], (((0,), (0,)), ((), ())), preferred_element_type=jnp.float32)
        rounded = lax.optimization_barrier(term.astype(jnp.bfloat16))
        return (total + rounded.astype(jnp.float32), None)
    weight_grad, unused = lax.scan(add_block, jnp.zeros((D, KV), jnp.float32), (blocks_scaled, blocks_masked))
    updated = weight.astype(jnp.float32) - inner_rate * weight_grad
    new_gain = gain - gain_rate * gain_grad
    return (projected, hidden_grad, updated, new_gain)

def reference(hidden_in, value_cot, proj_weight, norm_gain, anchor, momentum, excluded, fragment):
    frag = fragment[0]
    anchor_all = anchor.reshape(FRAGS, D, FC)
    momentum_all = momentum.reshape(FRAGS, D, FC)
    anchor_frag = lax.dynamic_index_in_dim(anchor_all, frag, 0, keepdims=False)
    momentum_frag = lax.dynamic_index_in_dim(momentum_all, frag, 0, keepdims=False)
    weight_total = jnp.zeros((D, FC), jnp.float32)
    for member in range(N_REPLICA):
        weight_total = weight_total + lax.dynamic_slice_in_dim(proj_weight[member], frag * FC, FC, 1).astype(jnp.float32)
    delta = anchor_frag - weight_total / N_REPLICA
    momentum_new = outer_momentum * momentum_frag + delta
    anchor_new = anchor_frag - outer_rate * (delta + outer_momentum * momentum_new)
    values_list, grads_list, weights_list, gains_list = ([], [], [], [])
    for member in range(N_REPLICA):
        projected, hidden_grad, updated, new_gain = one_replica(hidden_in[member], value_cot[member], proj_weight[member], norm_gain[member], excluded[member])
        columns = lax.dynamic_slice_in_dim(updated, frag * FC, FC, 1)
        merged = mix_weight * anchor_new + (1.0 - mix_weight) * columns
        new_weight = lax.dynamic_update_slice_in_dim(updated, merged, frag * FC, 1).astype(jnp.bfloat16)
        values_list.append(projected)
        grads_list.append(hidden_grad)
        weights_list.append(new_weight)
        gains_list.append(new_gain)
    anchor_out = lax.dynamic_update_index_in_dim(anchor_all, anchor_new, frag, 0).reshape(FRAGS, N_FSDP, D // N_FSDP, FC)
    momentum_out = lax.dynamic_update_index_in_dim(momentum_all, momentum_new, frag, 0).reshape(FRAGS, N_FSDP, D // N_FSDP, FC)
    return (jnp.stack(values_list), jnp.stack(grads_list), jnp.stack(weights_list), jnp.stack(gains_list), anchor_out, momentum_out)
```

```python
import functools

import jax
import jax.numpy as jnp
from jax import lax
from jax.experimental import pallas as pl
from jax.experimental.pallas import tpu as pltpu
from jax.sharding import PartitionSpec as P

outer_momentum = 0.9
outer_rate = 0.7
mix_weight = 0.5

ROWS = 512
D = 8192
KV = 1024
HALF = D // 2
WIDE = HALF + KV
VMEM = 56 * 1024 * 1024
NZ, NY, NC = 4, 2, 2
bf16, f32 = jnp.bfloat16, jnp.float32


def params(n):
    return pltpu.CompilerParams(dimension_semantics=("arbitrary",) * n, vmem_limit_bytes=VMEM)


def cost(microseconds):
    return pl.CostEstimate(flops=0, bytes_accessed=int(microseconds * 3.3e6), transcendentals=0)


def shift(x, dz, dy, dc, name="x"):
    pairs = []
    for z in range(NZ):
        for y in range(NY):
            for c in range(NC):
                to = ((z + dz) % NZ, (y + dy) % NY, (c + dc) % NC)
                pairs.append(((z * NY + y) * NC + c, (to[0] * NY + to[1]) * NC + to[2]))
    with jax.named_scope(name):
        return lax.ppermute(x, "fsdp", pairs)


def flip_z(x, mask):
    pairs = [(i, i ^ (mask * NY * NC)) for i in range(NZ * NY * NC)]
    return lax.ppermute(x, "fsdp", pairs)


def flip_replica(x, mask):
    return lax.ppermute(x, "replica", [(i, i ^ mask) for i in range(8)])


Z, Y, CORE, FIRST, FRAG, REPLICA = range(6)
PAIR = 2 * ROWS


def pick(step, values):
    found = values[-1]
    for k, value in enumerate(values[:-1]):
        found = jnp.where(step == k, value, found)
    return found


def block_of(s, step, places):
    dz, dy = pick(step, [p[0] for p in places]), pick(step, [p[1] for p in places])
    return lax.rem(s[Z] + dz, NZ) * NY + lax.rem(s[Y] + dy, NY)


def pair_of(s, step, depths):
    return lax.rem(s[Z] + pick(step, depths), NZ)


def lanes(v, k):
    return v[:, k * 128 : (k + 1) * 128]


def norm_kernel(s_ref, x_ref, cot_ref, gain_ref, excl_ref, mine_ref, send_ref, inv_ref):
    core = s_ref[CORE]
    rows = x_ref.shape[0]
    position = s_ref[FIRST] + pl.program_id(0) * rows
    position = position + lax.broadcasted_iota(jnp.int32, (rows, 1), 0)
    hits = jnp.where(position == excl_ref[...], 1.0, 0.0)
    kept = 1.0 - jnp.max(hits, axis=1, keepdims=True)
    masked = (cot_ref[...].astype(f32) * kept).astype(bf16)
    mine_ref[:, HALF:] = masked
    send_ref[:, HALF:] = masked
    total = jnp.zeros((rows, 128), f32)
    for b in range(D // 128):
        v = x_ref[:, b * 128 : (b + 1) * 128].astype(f32)
        total = total + v * v
    total = jnp.sum(total, axis=1, keepdims=True)
    inverse = jnp.broadcast_to(lax.rsqrt(total / D + 1e-05), inv_ref.shape)
    inv_ref[...] = inverse
    for j in range(HALF // ROWS):
        for parity, out in ((core, mine_ref), (1 - core, send_ref)):
            at = pl.multiple_of((2 * j + parity) * ROWS, ROWS)
            x = x_ref[:, pl.ds(at, ROWS)].astype(f32)
            gain = gain_ref[:, pl.ds(at, ROWS)]
            for k in range(ROWS // 128):
                v = lanes(x, k) * inverse * lanes(gain, k)
                out[:, j * ROWS + k * 128 : j * ROWS + (k + 1) * 128] = v.astype(bf16)


def norm_call(scalars, hidden, cot, gain, excl):
    tile = 128
    return pl.pallas_call(
        norm_kernel,
        grid_spec=pltpu.PrefetchScalarGridSpec(
            num_scalar_prefetch=1,
            grid=(ROWS // tile,),
            in_specs=[
                pl.BlockSpec((tile, D), lambda t, s: (t, 0)),
                pl.BlockSpec((tile, KV), lambda t, s: (t, 0)),
                pl.BlockSpec((1, D), lambda t, s: (0, 0)),
                pl.BlockSpec((1, 1024), lambda t, s: (0, 0)),
            ],
            out_specs=[
                pl.BlockSpec((tile, WIDE), lambda t, s: (t, 0)),
                pl.BlockSpec((tile, WIDE), lambda t, s: (t, 0)),
                pl.BlockSpec((tile, 128), lambda t, s: (t, 0)),
            ],
        ),
        out_shape=[
            jax.ShapeDtypeStruct((ROWS, WIDE), bf16),
            jax.ShapeDtypeStruct((ROWS, WIDE), bf16),
            jax.ShapeDtypeStruct((ROWS, 128), f32),
        ],
        compiler_params=params(1),
        cost_estimate=cost(8),
        name="norm",
    )(scalars, hidden, cot, gain, excl)


def grad_kernel(count, s_ref, x0_ref, x1_ref, c0_ref, c1_ref, *rest):
    outs, (held, sems) = rest[:count], rest[count:]
    step = pl.program_id(0)
    dims = (((0,), (0,)), ((), ()))
    total = lax.dot_general(x0_ref[...], c0_ref[...], dims, preferred_element_type=f32)
    total = total + lax.dot_general(x1_ref[...], c1_ref[...], dims, preferred_element_type=f32)
    total = total.astype(bf16)
    copies = [pltpu.make_async_copy(held.at[k % 2], outs[k], sems.at[k % 2]) for k in range(count)]
    for k in range(count):

        @pl.when(step == k)
        def _(k=k):
            if k >= 2:
                copies[k - 2].wait()
            held[k % 2] = total
            copies[k].start()
            if k == count - 1:
                for copy in copies[max(k - 1, 0) :]:
                    copy.wait()


def grad_call(places, scalars, mine, recv, estimate):
    count = len(places)
    x = pl.BlockSpec((ROWS, ROWS), lambda t, s: (0, block_of(s, t, places)))
    c = pl.BlockSpec((ROWS, KV), lambda t, s: (0, HALF // KV))
    return pl.pallas_call(
        functools.partial(grad_kernel, count),
        grid_spec=pltpu.PrefetchScalarGridSpec(
            num_scalar_prefetch=1,
            grid=(count,),
            in_specs=[x, x, c, c],
            out_specs=[pl.BlockSpec(memory_space=pl.ANY)] * count,
            scratch_shapes=[pltpu.VMEM((2, ROWS, KV), bf16), pltpu.SemaphoreType.DMA((2,))],
        ),
        out_shape=[jax.ShapeDtypeStruct((ROWS, KV), bf16)] * count,
        compiler_params=params(1),
        cost_estimate=cost(estimate),
        name="weight_grad_blocks",
    )(scalars, mine, recv, mine, recv)


def weight_copies(depths, s_ref, weights, held, sems):
    copies = []
    for k in range(len(depths)):
        for dy in range(NY):
            at = pl.multiple_of(lax.rem(s_ref[Y] + dy, NY) * ROWS, ROWS)
            n = NY * k + dy
            copies.append(
                pltpu.make_async_copy(weights[n], held.at[k, pl.ds(at, ROWS)], sems.at[n])
            )
    return copies


def half_kernel(depths, s_ref, x_ref, c_ref, gain_ref, *rest):
    count = len(depths)
    weights, rest = rest[: NY * count], rest[NY * count :]
    outs, (held, sems, values, made, out_sems) = rest[: count + 1], rest[count + 1 :]
    step = pl.program_id(0)
    copies = weight_copies(depths, s_ref, weights, held, sems)
    back = [
        pltpu.make_async_copy(made.at[k % 2], outs[k], out_sems.at[k % 2]) for k in range(count + 1)
    ]

    @pl.when(step == 0)
    def _():
        for copy in copies:
            copy.start()

    for k in range(count):

        @pl.when(step == k)
        def _(k=k):
            copies[NY * k].wait()
            copies[NY * k + 1].wait()
            if k >= 2:
                back[k - 2].wait()

    w = held[step]
    part = jnp.dot(x_ref[...], w, preferred_element_type=f32)

    @pl.when(step == 0)
    def _():
        values[...] = part

    @pl.when(step > 0)
    def _():
        values[...] += part

    grad = lax.dot_general(c_ref[...], w, (((1,), (1,)), ((), ())), preferred_element_type=f32)
    first = lax.rem(s_ref[Z] + pick(step, depths), NZ) * NY
    slot = lax.rem(step, 2)
    for k in range(NY):
        at = pl.multiple_of((2 * (first + k) + s_ref[CORE]) * ROWS, ROWS)
        cols = slice(k * ROWS, (k + 1) * ROWS)
        made[slot, :, cols] = (grad[:, cols] * gain_ref[:, pl.ds(at, ROWS)]).astype(bf16)

    for k in range(count):

        @pl.when(step == k)
        def _(k=k):
            back[k].start()
            if k == count - 1:
                if count >= 2:
                    back[count - 2].wait()
                made[count % 2] = values[...].astype(bf16)
                back[count].start()
                back[count - 1].wait()
                back[count].wait()


def half_call(depths, scalars, x, gain, w, name, estimate):
    count = len(depths)
    weights = [w[dz, dy] for dz in depths for dy in range(NY)]
    return pl.pallas_call(
        functools.partial(half_kernel, depths),
        grid_spec=pltpu.PrefetchScalarGridSpec(
            num_scalar_prefetch=1,
            grid=(count,),
            in_specs=[
                pl.BlockSpec((ROWS, PAIR), lambda t, s: (0, pair_of(s, t, depths))),
                pl.BlockSpec((ROWS, KV), lambda t, s: (0, HALF // KV)),
                pl.BlockSpec((1, D), lambda t, s: (0, 0)),
            ]
            + [pl.BlockSpec(memory_space=pl.ANY)] * len(weights),
            out_specs=[pl.BlockSpec(memory_space=pl.ANY)] * (count + 1),
            scratch_shapes=[
                pltpu.VMEM((count, PAIR, KV), bf16),
                pltpu.SemaphoreType.DMA((NY * count,)),
                pltpu.VMEM((ROWS, KV), f32),
                pltpu.VMEM((2, ROWS, PAIR), bf16),
                pltpu.SemaphoreType.DMA((2,)),
            ],
        ),
        out_shape=[jax.ShapeDtypeStruct((ROWS, PAIR), bf16)] * (count + 1),
        compiler_params=params(1),
        cost_estimate=cost(estimate),
        name=name,
    )(scalars, x, x, gain, *weights)


def hidden_kernel(depths, s_ref, x_ref, c_ref, gain_ref, inv_ref, h_ref, *rest):
    step, count = pl.program_id(0), len(depths)
    gots, weights, rest = rest[: count + 2], rest[count + 2 : 3 * count + 2], rest[3 * count + 2 :]
    values_ref, out_ref, held, sems, values, mean, got, got_sems = rest
    received = [
        pltpu.make_async_copy(ref, got.at[k], got_sems.at[k]) for k, ref in enumerate(gots)
    ]
    copies = weight_copies(depths, s_ref, weights, held, sems)

    @pl.when(step == 0)
    def _():
        for copy in copies:
            copy.start()
        for copy in (*received[count:], *received[:count]):
            copy.start()

    for k in range(count):

        @pl.when(step == k)
        def _(k=k):
            copies[NY * k].wait()
            copies[NY * k + 1].wait()

        @pl.when(step == count + k)
        def _(k=k):
            received[k].wait()

    @pl.when(step < count)
    def _():
        part = jnp.dot(x_ref[...], held[step], preferred_element_type=f32)

        @pl.when(step == 0)
        def _():
            values[...] = part

        @pl.when(step > 0)
        def _():
            values[...] += part

    @pl.when(step == count)
    def _():
        for k in (count, count + 1):
            received[k].wait()
            values[...] += got[k].astype(f32)
        values_ref[...] = values[...].astype(bf16)
        dots = jnp.sum(values[...] * c_ref[...].astype(f32), axis=1, keepdims=True) / D
        mean[...] = jnp.broadcast_to(dots, mean.shape) * inv_ref[...]

    def finish(weighted, at):
        for n in range(ROWS // 128):
            cols = pl.ds(at + n * 128, 128)
            v = lanes(weighted, n) - h_ref[:, cols].astype(f32) * mean[...]
            out_ref[:, cols] = (v * inv_ref[...]).astype(bf16)

    @pl.when(step >= count)
    def _():
        core = s_ref[CORE]
        k = step - count
        first = 2 * PAIR * lax.rem(s_ref[Z] + pick(k, depths), NZ)
        for y in range(NY):
            cols = slice(y * ROWS, (y + 1) * ROWS)
            at = pl.multiple_of((2 * y + core) * ROWS, ROWS)
            gain = gain_ref[:, pl.ds(pl.multiple_of(first + at, ROWS), ROWS)]
            grad = lax.dot_general(
                c_ref[...], held[k, cols], (((1,), (1,)), ((), ())), preferred_element_type=f32
            )
            finish(grad * gain, at)
            at = pl.multiple_of((2 * y + 1 - core) * ROWS, ROWS)
            finish(got[k, :, cols].astype(f32), at)


def hidden_call(depths, scalars, hidden, mine, gain, inverse, gots, w):
    count = len(depths)
    weights = [w[dz, dy] for dz in depths for dy in range(NY)]

    def place(t, s):
        return pair_of(s, jnp.maximum(t - count, 0), depths)

    return pl.pallas_call(
        functools.partial(hidden_kernel, depths),
        grid_spec=pltpu.PrefetchScalarGridSpec(
            num_scalar_prefetch=1,
            grid=(2 * count,),
            in_specs=[
                pl.BlockSpec(
                    (ROWS, PAIR), lambda t, s: (0, pair_of(s, jnp.minimum(t, count - 1), depths))
                ),
                pl.BlockSpec((ROWS, KV), lambda t, s: (0, HALF // KV)),
                pl.BlockSpec((1, D), lambda t, s: (0, 0)),
                pl.BlockSpec((ROWS, 128), lambda t, s: (0, 0)),
                pl.BlockSpec((ROWS, 2 * PAIR), lambda t, s: (0, place(t, s))),
            ]
            + [pl.BlockSpec(memory_space=pl.ANY)] * len(gots)
            + [pl.BlockSpec(memory_space=pl.ANY)] * len(weights),
            out_specs=[
                pl.BlockSpec((ROWS, KV), lambda t, s: (0, 0)),
                pl.BlockSpec((ROWS, 2 * PAIR), lambda t, s: (0, place(t, s))),
            ],
            scratch_shapes=[
                pltpu.VMEM((count, PAIR, KV), bf16),
                pltpu.SemaphoreType.DMA((NY * count,)),
                pltpu.VMEM((ROWS, KV), f32),
                pltpu.VMEM((ROWS, 128), f32),
                pltpu.VMEM((count + 2, ROWS, PAIR), bf16),
                pltpu.SemaphoreType.DMA((count + 2,)),
            ],
        ),
        out_shape=[
            jax.ShapeDtypeStruct((ROWS, KV), bf16),
            jax.ShapeDtypeStruct((ROWS, D), bf16),
        ],
        compiler_params=params(1),
        cost_estimate=cost(100),
        name="hidden_grad",
    )(scalars, mine, mine, gain, inverse, hidden, *gots, *weights)


def update_kernel(rate, s_ref, w_ref, a_ref, b_ref, c_ref, d_ref, anchor_ref, out_ref):
    grad = a_ref[...].astype(f32) + b_ref[...].astype(f32)
    grad = grad + (c_ref[...].astype(f32) + d_ref[...].astype(f32))
    out_ref[...] = (w_ref[...].astype(f32) - rate * grad).astype(bf16)
    cols = anchor_ref.shape[1]
    at = pl.ds(pl.multiple_of(s_ref[FRAG] * cols, cols), cols)
    grad = a_ref[:, at].astype(f32) + b_ref[:, at].astype(f32)
    grad = grad + (c_ref[:, at].astype(f32) + d_ref[:, at].astype(f32))
    now = w_ref[:, at].astype(f32) - rate * grad
    out_ref[:, at] = (mix_weight * anchor_ref[...] + (1.0 - mix_weight) * now).astype(bf16)


def update_call(rate, scalars, weight, parts, anchor):
    tile = 256
    row = pl.BlockSpec((tile, KV), lambda t, s: (t, 0))
    return pl.pallas_call(
        functools.partial(update_kernel, rate),
        grid_spec=pltpu.PrefetchScalarGridSpec(
            num_scalar_prefetch=1,
            grid=(ROWS // tile,),
            in_specs=[row] * 5 + [pl.BlockSpec((tile, anchor.shape[1]), lambda t, s: (t, 0))],
            out_specs=row,
        ),
        out_shape=jax.ShapeDtypeStruct((ROWS, KV), bf16),
        compiler_params=params(1),
        cost_estimate=cost(3),
        name="update",
    )(scalars, weight, *parts, anchor)


by_delta = outer_rate * (1.0 + outer_momentum)
by_momentum = outer_rate * outer_momentum * outer_momentum


def term_kernel(replicas, s_ref, w_ref, a_ref, m_ref, out_ref):
    rows = a_ref.shape[2]
    out_ref[...] = w_ref[...].astype(f32) * (by_delta / replicas)
    at = pl.ds(pl.multiple_of(s_ref[REPLICA] * rows, rows), rows)
    out_ref[at, :] += (1.0 - by_delta) * a_ref[0, 0] - by_momentum * m_ref[0, 0]


def term_call(replicas, scalars, weight, anchor, momentum):
    _, _, rows, cols = anchor.shape
    state = pl.BlockSpec((1, 1, rows, cols), lambda t, s: (s[FRAG], 0, 0, 0))
    return pl.pallas_call(
        functools.partial(term_kernel, replicas),
        grid_spec=pltpu.PrefetchScalarGridSpec(
            num_scalar_prefetch=1,
            grid=(1,),
            in_specs=[pl.BlockSpec((ROWS, cols), lambda t, s: (0, s[FRAG])), state, state],
            out_specs=pl.BlockSpec((ROWS, cols), lambda t, s: (0, 0)),
        ),
        out_shape=jax.ShapeDtypeStruct((ROWS, cols), f32),
        compiler_params=params(1),
        cost_estimate=cost(1),
        name="outer_term",
    )(scalars, weight, anchor, momentum)


def outer_kernel(s_ref, total_ref, a_ref, m_ref, a_out, m_out):
    a_out[...] = a_ref[...]
    m_out[...] = m_ref[...]
    rows = a_ref.shape[2]
    frag = s_ref[FRAG]
    a, m = a_ref[frag, 0], m_ref[frag, 0]
    at = pl.ds(pl.multiple_of(s_ref[REPLICA] * rows, rows), rows)
    kept = (1.0 - by_delta) * a - by_momentum * m
    delta = a - (total_ref[at, :] - kept) / by_delta
    m_new = outer_momentum * m + delta
    m_out[frag, 0] = m_new
    a_out[frag, 0] = a - outer_rate * (delta + outer_momentum * m_new)


def outer_call(scalars, total, anchor, momentum):
    whole = pl.BlockSpec(anchor.shape, lambda t, s: (0, 0, 0, 0))
    return pl.pallas_call(
        outer_kernel,
        grid_spec=pltpu.PrefetchScalarGridSpec(
            num_scalar_prefetch=1,
            grid=(1,),
            in_specs=[pl.BlockSpec(total.shape, lambda t, s: (0, 0)), whole, whole],
            out_specs=[whole, whole],
        ),
        out_shape=[jax.ShapeDtypeStruct(anchor.shape, f32)] * 2,
        compiler_params=params(1),
        cost_estimate=cost(100),
        name="outer_step",
    )(scalars, total, anchor, momentum)


def gain_kernel(places, s_ref, *rest):
    grads, weights, out_ref = rest[:8], rest[8:16], rest[16]
    rows = grads[0].shape[0]
    ones = jnp.ones((8, KV), bf16)
    for k, (dz, dy) in enumerate(places):
        product = (grads[k][...].astype(f32) * weights[k][...].astype(f32)).astype(bf16)
        sums = lax.dot_general(ones, product, (((1,), (1,)), ((), ())), preferred_element_type=f32)
        block = lax.rem(s_ref[Z] + dz, NZ) * NY + lax.rem(s_ref[Y] + dy, NY)
        at = pl.multiple_of(block * ROWS + pl.program_id(0) * rows, rows)
        out_ref[:, pl.ds(at, rows)] = sums[:1]


def gain_call(places, scalars, g, w):
    tile = 256
    row = pl.BlockSpec((tile, KV), lambda t, s: (t, 0))
    return pl.pallas_call(
        functools.partial(gain_kernel, places),
        grid_spec=pltpu.PrefetchScalarGridSpec(
            num_scalar_prefetch=1,
            grid=(ROWS // tile,),
            in_specs=[row] * 16,
            out_specs=pl.BlockSpec((1, HALF), lambda t, s: (0, 0)),
        ),
        out_shape=jax.ShapeDtypeStruct((1, HALF), f32),
        compiler_params=params(1),
        cost_estimate=cost(0),
        name="gain_grad",
    )(scalars, *[g[p] for p in places], *[w[p] for p in places])


def after(x, *others):
    return lax.optimization_barrier((x, *others))[0]


def add(*terms):
    total = terms[0].astype(f32)
    for term in terms[1:]:
        total = total + term.astype(f32)
    return total.astype(bf16)


def body(hidden_in, value_cot, proj_weight, norm_gain, anchor, momentum, excluded, fragment):
    inner_rate = 0.01 / ROWS**0.5
    gain_rate = 0.1 / ROWS**0.5
    hidden, weight = hidden_in[0], proj_weight[0]
    here = lax.axis_index("fsdp")
    replica = lax.axis_index("replica")
    z, y, core = here // (NY * NC), (here // NC) % NY, here % NC
    scalars = jnp.stack([z, y, core, here * ROWS, fragment[0], replica]).astype(jnp.int32)

    w = {(0, 0): weight}
    w[1, 0] = shift(weight, -1, 0, 0, "ag_zm")
    w[0, 1] = shift(weight, 0, 1, 0, "ag_y")
    w[3, 0] = shift(weight, 1, 0, 0, "ag_zp")
    near = (w[0, 1], w[1, 0], w[3, 0])
    w[1, 1] = shift(after(w[0, 1], *near), -1, 0, 0, "ag_B")
    w[2, 0] = shift(after(w[3, 0], *near), 1, 0, 0, "ag_A")

    total = term_call(lax.axis_size("replica"), scalars, weight, anchor, momentum)
    first_term = total
    total = total + flip_replica(total, 2)
    first_sum = total
    total = total + flip_replica(total, 6)
    second_sum = total
    total = total + flip_replica(total, 1)

    mine, send, inverse = norm_call(
        after(scalars, first_term), hidden, value_cot[0], norm_gain, excluded
    )
    recv = shift(after(send, first_sum, *near), 0, 0, 1, "swap_x")

    g = {}

    def make(places, waits, estimate):
        g.update(zip(places, grad_call(places, after(scalars, *waits), mine, recv, estimate)))

    make([(2, 1)], [recv], 3)
    make([(3, 1), (1, 1), (2, 0)], [g[2, 1], second_sum], 8)
    make([(3, 0), (0, 1), (1, 0), (0, 0)], [g[2, 0], w[1, 1], w[2, 0]], 10)
    w[2, 1] = shift(after(w[1, 1], g[2, 1]), -1, 0, 0, "ag_D")
    w[3, 1] = shift(after(w[0, 1], w[2, 0], g[2, 1]), 1, 0, 0, "ag_C")
    far = shift(g[2, 1], 0, 1, 0, "rs_D")
    left = shift(g[3, 1], -1, 0, 0, "rs_C")
    side = shift(g[1, 1], 0, 1, 0, "rs_B")

    near_half, far_half = (0, 1), (3, 2)
    sent0 = half_call(near_half, after(scalars, g[0, 0]), recv, norm_gain, w, "half_near", 10)
    got0 = [shift(v, 0, 0, 1, "swap_w0") for v in sent0]
    over = shift(add(g[2, 0], after(far, sent0[0])), 1, 0, 0, "rs_A")
    sent1 = half_call(far_half, after(scalars, sent0[0], far), recv, norm_gain, w, "half_far", 0)
    got1 = [shift(v, 0, 0, 1, "swap_w1") for v in sent1]

    order = [(dz, dy) for dz in range(NZ) for dy in range(NY)]
    partial = gain_call(order, after(scalars, sent1[0], side), g, w)
    left, side, over = (after(v, partial) for v in (left, side, over))
    from_next = shift(after(g[3, 0], left), -1, 0, 0, "rs_zm")
    from_side = shift(add(g[0, 1], left), 0, 1, 0, "rs_y")
    from_last = shift(add(g[1, 0], side, over), 1, 0, 0, "rs_zp")

    anchor_out, momentum_out = outer_call(
        after(scalars, left, side, over), total, anchor, momentum
    )
    values_out, hidden_grad = hidden_call(
        (*near_half, *far_half),
        after(scalars, anchor_out), hidden, mine, norm_gain, inverse,
        [*got0[:-1], *got1[:-1], got0[-1], got1[-1]], w,
    )

    partial = partial + shift(partial, 0, 1, 0, "gain_y")
    partial = partial + flip_z(partial, 1)
    partial = partial + flip_z(partial, 3)
    other = shift(partial, 0, 0, 1, "gain_c")
    even = jnp.where(core == 0, partial, other).reshape(HALF // ROWS, ROWS)
    odd = jnp.where(core == 0, other, partial).reshape(HALF // ROWS, ROWS)
    gain_grad = jnp.stack([even, odd], axis=1).reshape(1, D) / norm_gain
    new_gain = norm_gain - gain_rate * gain_grad

    new_weight = update_call(
        inner_rate,
        scalars,
        weight,
        (after(g[0, 0], hidden_grad), from_next, from_side, from_last),
        total,
    )
    return (
        values_out[None],
        hidden_grad[None],
        new_weight[None],
        new_gain,
        anchor_out,
        momentum_out,
    )


def solution(mesh):
    placed = (
        P("replica", "fsdp", None),
        P("replica", "fsdp", None),
        P("replica", "fsdp", None),
        P("replica", None),
        P(None, "fsdp", "replica", None),
        P(None, "fsdp", "replica", None),
        P("replica", None),
        P(),
    )
    return jax.shard_map(
        body,
        mesh=mesh,
        in_specs=placed,
        out_specs=(
            P("replica", "fsdp", None),
            P("replica", "fsdp", None),
            P("replica", "fsdp", None),
            P("replica", None),
            P(None, "fsdp", "replica", None),
            P(None, "fsdp", "replica", None),
        ),
        check_vma=False,
    )
```

```python
import functools

import jax
import jax.numpy as jnp
from jax import lax
from jax.experimental import pallas as pl
from jax.experimental.pallas import tpu as pltpu
from jax.sharding import PartitionSpec as P

outer_momentum = 0.9
outer_rate = 0.7
mix_weight = 0.5

ROWS = 512
D = 8192
KV = 1024
HALF = D // 2
WIDE = HALF + KV
VMEM = 62 * 1024 * 1024
NZ, NY, NC = 4, 2, 2
bf16, f32 = jnp.bfloat16, jnp.float32


def params(n):
    return pltpu.CompilerParams(dimension_semantics=("arbitrary",) * n, vmem_limit_bytes=VMEM)


def cost(microseconds):
    return pl.CostEstimate(flops=0, bytes_accessed=int(microseconds * 3.3e6), transcendentals=0)


def shift(x, dz, dy, dc, name="x"):
    pairs = []
    for z in range(NZ):
        for y in range(NY):
            for c in range(NC):
                to = ((z + dz) % NZ, (y + dy) % NY, (c + dc) % NC)
                pairs.append(((z * NY + y) * NC + c, (to[0] * NY + to[1]) * NC + to[2]))
    with jax.named_scope(name):
        return lax.ppermute(x, "fsdp", pairs)


def flip_z(x, mask):
    pairs = [(i, i ^ (mask * NY * NC)) for i in range(NZ * NY * NC)]
    return lax.ppermute(x, "fsdp", pairs)


def flip_replica(x, mask):
    return lax.ppermute(x, "replica", [(i, i ^ mask) for i in range(8)])


Z, Y, CORE, FIRST, FRAG, REPLICA = range(6)
PAIR = 2 * ROWS


def pick(step, values):
    found = values[-1]
    for k, value in enumerate(values[:-1]):
        found = jnp.where(step == k, value, found)
    return found


def block_of(s, step, places):
    dz, dy = pick(step, [p[0] for p in places]), pick(step, [p[1] for p in places])
    return lax.rem(s[Z] + dz, NZ) * NY + lax.rem(s[Y] + dy, NY)


def pair_of(s, step, depths):
    return lax.rem(s[Z] + pick(step, depths), NZ)


def lanes(v, k):
    return v[:, k * 128 : (k + 1) * 128]


def norm_kernel(s_ref, x_ref, cot_ref, gain_ref, excl_ref, mine_ref, *rest):
    sends, (masked_ref, inv_ref) = rest[:NZ], rest[NZ:]
    core = s_ref[CORE]
    rows = x_ref.shape[0]
    position = s_ref[FIRST] + pl.program_id(0) * rows
    position = position + lax.broadcasted_iota(jnp.int32, (rows, 1), 0)
    hits = jnp.where(position == excl_ref[...], 1.0, 0.0)
    kept = 1.0 - jnp.max(hits, axis=1, keepdims=True)
    masked = (cot_ref[...].astype(f32) * kept).astype(bf16)
    mine_ref[:, HALF:] = masked
    masked_ref[...] = masked
    total = jnp.zeros((rows, 128), f32)
    for b in range(D // 128):
        v = x_ref[:, b * 128 : (b + 1) * 128].astype(f32)
        total = total + v * v
    total = jnp.sum(total, axis=1, keepdims=True)
    inverse = jnp.broadcast_to(lax.rsqrt(total / D + 1e-05), inv_ref.shape)
    inv_ref[...] = inverse

    def scaled(at, out, to):
        x = x_ref[:, pl.ds(at, ROWS)].astype(f32)
        gain = gain_ref[:, pl.ds(at, ROWS)]
        for k in range(ROWS // 128):
            v = lanes(x, k) * inverse * lanes(gain, k)
            out[:, to + k * 128 : to + (k + 1) * 128] = v.astype(bf16)

    for j in range(HALF // ROWS):
        scaled(pl.multiple_of((2 * j + core) * ROWS, ROWS), mine_ref, j * ROWS)
    for dz, send_ref in enumerate(sends):
        first = lax.rem(s_ref[Z] + dz, NZ) * NY
        for y in range(NY):
            at = pl.multiple_of((2 * (first + y) + 1 - core) * ROWS, ROWS)
            scaled(at, send_ref, y * ROWS)


def norm_call(scalars, hidden, cot, gain, excl):
    tile = 128
    return pl.pallas_call(
        norm_kernel,
        grid_spec=pltpu.PrefetchScalarGridSpec(
            num_scalar_prefetch=1,
            grid=(ROWS // tile,),
            in_specs=[
                pl.BlockSpec((tile, D), lambda t, s: (t, 0)),
                pl.BlockSpec((tile, KV), lambda t, s: (t, 0)),
                pl.BlockSpec((1, D), lambda t, s: (0, 0)),
                pl.BlockSpec((1, 1024), lambda t, s: (0, 0)),
            ],
            out_specs=[
                pl.BlockSpec((tile, WIDE), lambda t, s: (t, 0)),
                *[pl.BlockSpec((tile, PAIR), lambda t, s: (t, 0))] * NZ,
                pl.BlockSpec((tile, KV), lambda t, s: (t, 0)),
                pl.BlockSpec((tile, 128), lambda t, s: (t, 0)),
            ],
        ),
        out_shape=[
            jax.ShapeDtypeStruct((ROWS, WIDE), bf16),
            *[jax.ShapeDtypeStruct((ROWS, PAIR), bf16)] * NZ,
            jax.ShapeDtypeStruct((ROWS, KV), bf16),
            jax.ShapeDtypeStruct((ROWS, 128), f32),
        ],
        compiler_params=params(1),
        cost_estimate=cost(8),
        name="norm",
    )(scalars, hidden, cot, gain, excl)


def grad_kernel(places, s_ref, x0_ref, c0_ref, c1_ref, *rest):
    count = len(places)
    x1_refs, outs, (x1, x1_sems, held, sems) = rest[:count], rest[count : 2 * count], rest[2 * count :]
    step = pl.program_id(0)
    dims = (((0,), (0,)), ((), ()))
    loads = []
    for k, (_, dy) in enumerate(places):
        at = pl.multiple_of(lax.rem(s_ref[Y] + dy, NY) * ROWS, ROWS)
        loads.append(
            pltpu.make_async_copy(x1_refs[k].at[:, pl.ds(at, ROWS)], x1.at[k], x1_sems.at[k])
        )
    copies = [pltpu.make_async_copy(held.at[k % 2], outs[k], sems.at[k % 2]) for k in range(count)]

    @pl.when(step == 0)
    def _():
        for load in loads:
            load.start()

    total = lax.dot_general(x0_ref[...], c0_ref[...], dims, preferred_element_type=f32)
    for k in range(count):

        @pl.when(step == k)
        def _(k=k):
            loads[k].wait()

    total = total + lax.dot_general(x1[step], c1_ref[...], dims, preferred_element_type=f32)
    total = total.astype(bf16)
    for k in range(count):

        @pl.when(step == k)
        def _(k=k):
            if k >= 2:
                copies[k - 2].wait()
            held[k % 2] = total
            copies[k].start()
            if k == count - 1:
                for copy in copies[max(k - 1, 0) :]:
                    copy.wait()


def grad_call(places, scalars, mine, recv, recv_cot, estimate):
    count = len(places)
    c = pl.BlockSpec((ROWS, KV), lambda t, s: (0, 0))
    return pl.pallas_call(
        functools.partial(grad_kernel, places),
        grid_spec=pltpu.PrefetchScalarGridSpec(
            num_scalar_prefetch=1,
            grid=(count,),
            in_specs=[
                pl.BlockSpec((ROWS, ROWS), lambda t, s: (0, block_of(s, t, places))),
                pl.BlockSpec((ROWS, KV), lambda t, s: (0, HALF // KV)),
                c,
            ]
            + [pl.BlockSpec(memory_space=pltpu.HBM)] * count,
            out_specs=[pl.BlockSpec(memory_space=pltpu.HBM)] * count,
            scratch_shapes=[
                pltpu.VMEM((count, ROWS, ROWS), bf16),
                pltpu.SemaphoreType.DMA((count,)),
                pltpu.VMEM((2, ROWS, KV), bf16),
                pltpu.SemaphoreType.DMA((2,)),
            ],
        ),
        out_shape=[jax.ShapeDtypeStruct((ROWS, KV), bf16)] * count,
        compiler_params=params(1),
        cost_estimate=cost(estimate),
        name="weight_grad_blocks",
    )(scalars, mine, mine, recv_cot, *[recv[dz] for dz, _ in places])


def weight_copies(depths, s_ref, weights, held, sems):
    copies = []
    for k in range(len(depths)):
        for dy in range(NY):
            at = pl.multiple_of(lax.rem(s_ref[Y] + dy, NY) * ROWS, ROWS)
            n = NY * k + dy
            copies.append(
                pltpu.make_async_copy(weights[n], held.at[k, pl.ds(at, ROWS)], sems.at[n])
            )
    return copies


def half_kernel(depths, s_ref, c_ref, gain_ref, *rest):
    count = len(depths)
    xs, weights, rest = rest[:count], rest[count : 3 * count], rest[3 * count :]
    outs, (x, x_sems, held, sems, values, made, out_sems) = rest[: count + 1], rest[count + 1 :]
    step = pl.program_id(0)
    loads = [pltpu.make_async_copy(ref, x.at[k], x_sems.at[k]) for k, ref in enumerate(xs)]
    copies = weight_copies(depths, s_ref, weights, held, sems)
    back = [
        pltpu.make_async_copy(made.at[k % 2], outs[k], out_sems.at[k % 2]) for k in range(count + 1)
    ]

    @pl.when(step == 0)
    def _():
        for k in range(count):
            loads[k].start()
            copies[NY * k].start()
            copies[NY * k + 1].start()

    for k in range(count):

        @pl.when(step == k)
        def _(k=k):
            loads[k].wait()
            copies[NY * k].wait()
            copies[NY * k + 1].wait()
            if k >= 2:
                back[k - 2].wait()

    w = held[step]
    part = jnp.dot(x[step], w, preferred_element_type=f32)

    @pl.when(step == 0)
    def _():
        values[...] = part

    @pl.when(step > 0)
    def _():
        values[...] += part

    grad = lax.dot_general(c_ref[...], w, (((1,), (1,)), ((), ())), preferred_element_type=f32)
    first = lax.rem(s_ref[Z] + pick(step, depths), NZ) * NY
    slot = lax.rem(step, 2)
    for k in range(NY):
        at = pl.multiple_of((2 * (first + k) + s_ref[CORE]) * ROWS, ROWS)
        cols = slice(k * ROWS, (k + 1) * ROWS)
        made[slot, :, cols] = (grad[:, cols] * gain_ref[:, pl.ds(at, ROWS)]).astype(bf16)

    for k in range(count):

        @pl.when(step == k)
        def _(k=k):
            back[k].start()
            if k == count - 1:
                if count >= 2:
                    back[count - 2].wait()
                made[count % 2] = values[...].astype(bf16)
                back[count].start()
                back[count - 1].wait()
                back[count].wait()


def half_call(depths, scalars, x, cot, gain, w, name, estimate):
    count = len(depths)
    weights = [w[dz, dy] for dz in depths for dy in range(NY)]
    return pl.pallas_call(
        functools.partial(half_kernel, depths),
        grid_spec=pltpu.PrefetchScalarGridSpec(
            num_scalar_prefetch=1,
            grid=(count,),
            in_specs=[
                pl.BlockSpec((ROWS, KV), lambda t, s: (0, 0)),
                pl.BlockSpec((1, D), lambda t, s: (0, 0)),
            ]
            + [pl.BlockSpec(memory_space=pltpu.HBM)] * (count + len(weights)),
            out_specs=[pl.BlockSpec(memory_space=pltpu.HBM)] * (count + 1),
            scratch_shapes=[
                pltpu.VMEM((count, ROWS, PAIR), bf16),
                pltpu.SemaphoreType.DMA((count,)),
                pltpu.VMEM((count, PAIR, KV), bf16),
                pltpu.SemaphoreType.DMA((NY * count,)),
                pltpu.VMEM((ROWS, KV), f32),
                pltpu.VMEM((2, ROWS, PAIR), bf16),
                pltpu.SemaphoreType.DMA((2,)),
            ],
        ),
        out_shape=[jax.ShapeDtypeStruct((ROWS, PAIR), bf16)] * (count + 1),
        compiler_params=params(1),
        cost_estimate=cost(estimate),
        name=name,
    )(scalars, cot, gain, *[x[dz] for dz in depths], *weights)


def hidden_kernel(depths, s_ref, x_ref, c_ref, gain_ref, inv_ref, h_ref, *rest):
    step, count = pl.program_id(0), len(depths)
    gots, weights, rest = rest[: count + 2], rest[count + 2 : 3 * count + 2], rest[3 * count + 2 :]
    values_ref, out_ref, held, sems, values, mean, got, got_sems = rest
    received = [
        pltpu.make_async_copy(ref, got.at[k], got_sems.at[k]) for k, ref in enumerate(gots)
    ]
    copies = weight_copies(depths, s_ref, weights, held, sems)

    @pl.when(step == 0)
    def _():
        for copy in copies:
            copy.start()
        for copy in (*received[count:], *received[:count]):
            copy.start()

    for k in range(count):

        @pl.when(step == k)
        def _(k=k):
            copies[NY * k].wait()
            copies[NY * k + 1].wait()

        @pl.when(step == count + k)
        def _(k=k):
            received[k].wait()

    @pl.when(step < count)
    def _():
        part = jnp.dot(x_ref[...], held[step], preferred_element_type=f32)

        @pl.when(step == 0)
        def _():
            values[...] = part

        @pl.when(step > 0)
        def _():
            values[...] += part

    @pl.when(step == count)
    def _():
        for k in (count, count + 1):
            received[k].wait()
            values[...] += got[k].astype(f32)
        values_ref[...] = values[...].astype(bf16)
        dots = jnp.sum(values[...] * c_ref[...].astype(f32), axis=1, keepdims=True) / D
        mean[...] = jnp.broadcast_to(dots, mean.shape) * inv_ref[...]

    def finish(weighted, at):
        for n in range(ROWS // 128):
            cols = pl.ds(at + n * 128, 128)
            v = lanes(weighted, n) - h_ref[:, cols].astype(f32) * mean[...]
            out_ref[:, cols] = (v * inv_ref[...]).astype(bf16)

    @pl.when(step >= count)
    def _():
        core = s_ref[CORE]
        k = step - count
        first = 2 * PAIR * lax.rem(s_ref[Z] + pick(k, depths), NZ)
        for y in range(NY):
            cols = slice(y * ROWS, (y + 1) * ROWS)
            at = pl.multiple_of((2 * y + core) * ROWS, ROWS)
            gain = gain_ref[:, pl.ds(pl.multiple_of(first + at, ROWS), ROWS)]
            grad = lax.dot_general(
                c_ref[...], held[k, cols], (((1,), (1,)), ((), ())), preferred_element_type=f32
            )
            finish(grad * gain, at)
            at = pl.multiple_of((2 * y + 1 - core) * ROWS, ROWS)
            finish(got[k, :, cols].astype(f32), at)


def hidden_call(depths, scalars, hidden, mine, gain, inverse, gots, w):
    count = len(depths)
    weights = [w[dz, dy] for dz in depths for dy in range(NY)]

    def place(t, s):
        return pair_of(s, jnp.maximum(t - count, 0), depths)

    return pl.pallas_call(
        functools.partial(hidden_kernel, depths),
        grid_spec=pltpu.PrefetchScalarGridSpec(
            num_scalar_prefetch=1,
            grid=(2 * count,),
            in_specs=[
                pl.BlockSpec(
                    (ROWS, PAIR), lambda t, s: (0, pair_of(s, jnp.minimum(t, count - 1), depths))
                ),
                pl.BlockSpec((ROWS, KV), lambda t, s: (0, HALF // KV)),
                pl.BlockSpec((1, D), lambda t, s: (0, 0)),
                pl.BlockSpec((ROWS, 128), lambda t, s: (0, 0)),
                pl.BlockSpec((ROWS, 2 * PAIR), lambda t, s: (0, place(t, s))),
            ]
            + [pl.BlockSpec(memory_space=pltpu.HBM)] * len(gots)
            + [pl.BlockSpec(memory_space=pltpu.HBM)] * len(weights),
            out_specs=[
                pl.BlockSpec((ROWS, KV), lambda t, s: (0, 0)),
                pl.BlockSpec((ROWS, 2 * PAIR), lambda t, s: (0, place(t, s))),
            ],
            scratch_shapes=[
                pltpu.VMEM((count, PAIR, KV), bf16),
                pltpu.SemaphoreType.DMA((NY * count,)),
                pltpu.VMEM((ROWS, KV), f32),
                pltpu.VMEM((ROWS, 128), f32),
                pltpu.VMEM((count + 2, ROWS, PAIR), bf16),
                pltpu.SemaphoreType.DMA((count + 2,)),
            ],
        ),
        out_shape=[
            jax.ShapeDtypeStruct((ROWS, KV), bf16),
            jax.ShapeDtypeStruct((ROWS, D), bf16),
        ],
        compiler_params=params(1),
        cost_estimate=cost(100),
        name="hidden_grad",
    )(scalars, mine, mine, gain, inverse, hidden, *gots, *weights)


def update_kernel(rate, s_ref, w_ref, a_ref, b_ref, c_ref, d_ref, total_ref, *rest):
    anchor_ref, momentum_ref, all_ref, out_ref, anchor_out, momentum_out = rest
    grad = a_ref[...].astype(f32) + b_ref[...].astype(f32)
    grad = grad + (c_ref[...].astype(f32) + d_ref[...].astype(f32))
    out_ref[...] = (w_ref[...].astype(f32) - rate * grad).astype(bf16)
    cols = total_ref.shape[1]
    at = pl.ds(pl.multiple_of(s_ref[FRAG] * cols, cols), cols)
    grad = a_ref[:, at].astype(f32) + b_ref[:, at].astype(f32)
    grad = grad + (c_ref[:, at].astype(f32) + d_ref[:, at].astype(f32))
    now = w_ref[:, at].astype(f32) - rate * grad
    out_ref[:, at] = (mix_weight * total_ref[...] + (1.0 - mix_weight) * now).astype(bf16)

    @pl.when(pl.program_id(0) == 0)
    def _():
        anchor_out[...] = anchor_ref[...]
        momentum_out[...] = momentum_ref[...]
        rows = anchor_ref.shape[2]
        frag = s_ref[FRAG]
        a, m = anchor_ref[frag, 0], momentum_ref[frag, 0]
        at = pl.ds(pl.multiple_of(s_ref[REPLICA] * rows, rows), rows)
        kept = (1.0 - by_delta) * a - by_momentum * m
        delta = a - (all_ref[at, :] - kept) / by_delta
        m_new = outer_momentum * m + delta
        momentum_out[frag, 0] = m_new
        anchor_out[frag, 0] = a - outer_rate * (delta + outer_momentum * m_new)


def update_call(rate, scalars, weight, parts, total, anchor, momentum):
    tile = 256
    row = pl.BlockSpec((tile, KV), lambda t, s: (t, 0))
    whole = pl.BlockSpec(anchor.shape, lambda t, s: (0, 0, 0, 0))
    return pl.pallas_call(
        functools.partial(update_kernel, rate),
        grid_spec=pltpu.PrefetchScalarGridSpec(
            num_scalar_prefetch=1,
            grid=(ROWS // tile,),
            in_specs=[
                *[row] * 5,
                pl.BlockSpec((tile, total.shape[1]), lambda t, s: (t, 0)),
                whole,
                whole,
                pl.BlockSpec(total.shape, lambda t, s: (0, 0)),
            ],
            out_specs=[row, whole, whole],
        ),
        out_shape=[
            jax.ShapeDtypeStruct((ROWS, KV), bf16),
            jax.ShapeDtypeStruct(anchor.shape, f32),
            jax.ShapeDtypeStruct(anchor.shape, f32),
        ],
        compiler_params=params(1),
        cost_estimate=cost(3),
        name="update",
    )(scalars, weight, *parts, total, anchor, momentum, total)


by_delta = outer_rate * (1.0 + outer_momentum)
by_momentum = outer_rate * outer_momentum * outer_momentum


def term_kernel(replicas, s_ref, w_ref, a_ref, m_ref, out_ref):
    rows = a_ref.shape[2]
    out_ref[...] = w_ref[...].astype(f32) * (by_delta / replicas)
    at = pl.ds(pl.multiple_of(s_ref[REPLICA] * rows, rows), rows)
    out_ref[at, :] += (1.0 - by_delta) * a_ref[0, 0] - by_momentum * m_ref[0, 0]


def term_call(replicas, scalars, weight, anchor, momentum):
    _, _, rows, cols = anchor.shape
    state = pl.BlockSpec((1, 1, rows, cols), lambda t, s: (s[FRAG], 0, 0, 0))
    return pl.pallas_call(
        functools.partial(term_kernel, replicas),
        grid_spec=pltpu.PrefetchScalarGridSpec(
            num_scalar_prefetch=1,
            grid=(1,),
            in_specs=[pl.BlockSpec((ROWS, cols), lambda t, s: (0, s[FRAG])), state, state],
            out_specs=pl.BlockSpec((ROWS, cols), lambda t, s: (0, 0)),
        ),
        out_shape=jax.ShapeDtypeStruct((ROWS, cols), f32),
        compiler_params=params(1),
        cost_estimate=cost(1),
        name="outer_term",
    )(scalars, weight, anchor, momentum)


def gain_kernel(places, add, s_ref, *rest):
    count = len(places)
    grads, weights, rest = rest[:count], rest[count : 2 * count], rest[2 * count :]
    out_ref = rest[-1]
    rows = grads[0].shape[0]
    ones = jnp.ones((8, KV), bf16)

    @pl.when(pl.program_id(0) == 0)
    def _():
        out_ref[...] = rest[0][...] if add else jnp.zeros(out_ref.shape, f32)

    for k, (dz, dy) in enumerate(places):
        product = (grads[k][...].astype(f32) * weights[k][...].astype(f32)).astype(bf16)
        sums = lax.dot_general(ones, product, (((1,), (1,)), ((), ())), preferred_element_type=f32)
        block = lax.rem(s_ref[Z] + dz, NZ) * NY + lax.rem(s_ref[Y] + dy, NY)
        at = pl.multiple_of(block * ROWS + pl.program_id(0) * rows, rows)
        out_ref[:, pl.ds(at, rows)] = sums[:1]


def gain_call(places, scalars, g, w, before=None):
    tile = 256
    row = pl.BlockSpec((tile, KV), lambda t, s: (t, 0))
    whole = pl.BlockSpec((1, HALF), lambda t, s: (0, 0))
    extra = [] if before is None else [before]
    return pl.pallas_call(
        functools.partial(gain_kernel, places, before is not None),
        grid_spec=pltpu.PrefetchScalarGridSpec(
            num_scalar_prefetch=1,
            grid=(ROWS // tile,),
            in_specs=[row] * (2 * len(places)) + [whole] * len(extra),
            out_specs=whole,
        ),
        out_shape=jax.ShapeDtypeStruct((1, HALF), f32),
        compiler_params=params(1),
        cost_estimate=cost(0),
        name="gain_grad",
    )(scalars, *[g[p] for p in places], *[w[p] for p in places], *extra)


def relay_kernel(a_ref, b_ref, c_ref, d_ref, e_ref, two_ref, three_ref):
    two_ref[...] = (a_ref[...].astype(f32) + b_ref[...].astype(f32)).astype(bf16)
    three = c_ref[...].astype(f32) + d_ref[...].astype(f32) + e_ref[...].astype(f32)
    three_ref[...] = three.astype(bf16)


def relay_call(*terms):
    row = pl.BlockSpec((ROWS // 4, KV), lambda t: (t, 0))
    return pl.pallas_call(
        relay_kernel,
        grid=(4,),
        in_specs=[row] * 5,
        out_specs=[row] * 2,
        out_shape=[jax.ShapeDtypeStruct((ROWS, KV), bf16)] * 2,
        compiler_params=params(1),
        cost_estimate=cost(3),
        name="relay_sums",
    )(*terms)


def after(x, *others):
    return lax.optimization_barrier((x, *others))[0]


def add(*terms):
    total = terms[0].astype(f32)
    for term in terms[1:]:
        total = total + term.astype(f32)
    return total.astype(bf16)


def body(hidden_in, value_cot, proj_weight, norm_gain, anchor, momentum, excluded, fragment):
    inner_rate = 0.01 / ROWS**0.5
    gain_rate = 0.1 / ROWS**0.5
    hidden, weight = hidden_in[0], proj_weight[0]
    here = lax.axis_index("fsdp")
    replica = lax.axis_index("replica")
    z, y, core = here // (NY * NC), (here // NC) % NY, here % NC
    scalars = jnp.stack([z, y, core, here * ROWS, fragment[0], replica]).astype(jnp.int32)

    w = {(0, 0): weight}
    w[1, 0] = shift(weight, -1, 0, 0, "ag_zm")
    w[0, 1] = shift(weight, 0, 1, 0, "ag_y")
    w[3, 0] = shift(weight, 1, 0, 0, "ag_zp")
    near = (w[0, 1], w[1, 0], w[3, 0])
    w[1, 1] = shift(after(w[0, 1], *near), -1, 0, 0, "ag_B")
    w[2, 0] = shift(after(w[3, 0], *near), 1, 0, 0, "ag_A")

    total = term_call(lax.axis_size("replica"), scalars, weight, anchor, momentum)
    first_term = total
    total = total + flip_replica(after(total, w[0, 1]), 1)
    first_sum = total
    total = total + flip_replica(total, 2)
    second_sum = total
    total = total + flip_replica(total, 6)

    mine, *send, inverse = norm_call(
        after(scalars, first_term), hidden, value_cot[0], norm_gain, excluded
    )
    recv = [shift(v, 0, 0, 1, "swap_x") for v in send]
    recv_cot = recv.pop()

    g = {}

    def make(places, waits, estimate):
        g.update(zip(places, grad_call(places, after(scalars, *waits), mine, recv, recv_cot, estimate)))

    make([(2, 1), (1, 1), (3, 1), (2, 0), (3, 0), (0, 1), (1, 0), (0, 0)], near, 16)
    far = shift(after(g[2, 1], first_sum), 0, 1, 0, "rs_D")
    side = shift(g[1, 1], 0, 1, 0, "rs_B")
    w[2, 1] = shift(after(w[1, 1], g[2, 0]), -1, 0, 0, "ag_D")
    w[3, 1] = shift(after(w[0, 1], w[2, 0], g[2, 0]), 1, 0, 0, "ag_C")

    near_half, far_half = (0, 1), (3, 2)
    sent0 = half_call(
        near_half, after(scalars, g[0, 0]), recv, recv_cot, norm_gain, w, "half_near", 10
    )
    got0 = [shift(v, 0, 0, 1, "swap_w0") for v in sent0]
    near_order = [(dz, dy) for dz in near_half for dy in range(NY)]
    far_order = [(dz, dy) for dz in far_half for dy in range(NY)]
    near_sums = gain_call(near_order, after(scalars, sent0[0]), g, w)
    left = shift(after(g[3, 1], near_sums), -1, 0, 0, "rs_C")
    over = shift(add(g[2, 0], after(far, near_sums)), 1, 0, 0, "rs_A")
    sent1 = half_call(
        far_half, after(scalars, sent0[0], far), recv, recv_cot, norm_gain, w,
        "half_far", 0,
    )
    got1 = [shift(v, 0, 0, 1, "swap_w1") for v in sent1]

    partial = gain_call(far_order, after(scalars, sent1[0], second_sum), g, w, near_sums)
    left, side, over = (after(v, partial) for v in (left, side, over))
    from_next = shift(after(g[3, 0], left), -1, 0, 0, "rs_zm")
    to_side, to_last = relay_call(g[0, 1], left, g[1, 0], side, over)
    from_side = shift(to_side, 0, 1, 0, "rs_y")
    from_last = shift(to_last, 1, 0, 0, "rs_zp")

    values_out, hidden_grad = hidden_call(
        (*near_half, *far_half),
        after(scalars, left, side, over), hidden, mine, norm_gain, inverse,
        [*got0[:-1], *got1[:-1], got0[-1], got1[-1]], w,
    )

    partial = partial + shift(partial, 0, 1, 0, "gain_y")
    partial = partial + flip_z(partial, 1)
    partial = partial + flip_z(partial, 3)
    other = shift(after(partial, hidden_grad), 0, 0, 1, "gain_c")
    new_weight, anchor_out, momentum_out = update_call(
        inner_rate,
        scalars,
        weight,
        (after(g[0, 0], hidden_grad), from_next, from_side, from_last),
        total,
        anchor,
        momentum,
    )
    other = after(other, new_weight)
    even = jnp.where(core == 0, partial, other).reshape(HALF // ROWS, ROWS)
    odd = jnp.where(core == 0, other, partial).reshape(HALF // ROWS, ROWS)
    gain_grad = jnp.stack([even, odd], axis=1).reshape(1, D) / norm_gain
    new_gain = norm_gain - gain_rate * gain_grad

    return (
        values_out[None],
        hidden_grad[None],
        new_weight[None],
        new_gain,
        anchor_out,
        momentum_out,
    )


def solution(mesh):
    placed = (
        P("replica", "fsdp", None),
        P("replica", "fsdp", None),
        P("replica", "fsdp", None),
        P("replica", None),
        P(None, "fsdp", "replica", None),
        P(None, "fsdp", "replica", None),
        P("replica", None),
        P(),
    )
    return jax.shard_map(
        body,
        mesh=mesh,
        in_specs=placed,
        out_specs=(
            P("replica", "fsdp", None),
            P("replica", "fsdp", None),
            P("replica", "fsdp", None),
            P("replica", None),
            P(None, "fsdp", "replica", None),
            P(None, "fsdp", "replica", None),
        ),
        check_vma=False,
    )
```

```python
import functools

import jax
import jax.numpy as jnp
from jax import lax
from jax.experimental import pallas as pl
from jax.experimental.pallas import tpu as pltpu
from jax.sharding import PartitionSpec as P

outer_momentum = 0.9
outer_rate = 0.7
mix_weight = 0.5

ROWS = 512
D = 8192
KV = 1024
HALF = D // 2
WIDE = HALF + KV
VMEM = 62 * 1024 * 1024
NZ, NY, NC = 4, 2, 2
bf16, f32 = jnp.bfloat16, jnp.float32


def params(n):
    return pltpu.CompilerParams(dimension_semantics=("arbitrary",) * n, vmem_limit_bytes=VMEM)


def cost(microseconds):
    return pl.CostEstimate(flops=0, bytes_accessed=int(microseconds * 3.3e6), transcendentals=0)


def shift(x, dz, dy, dc, name="x"):
    pairs = []
    for z in range(NZ):
        for y in range(NY):
            for c in range(NC):
                to = ((z + dz) % NZ, (y + dy) % NY, (c + dc) % NC)
                pairs.append(((z * NY + y) * NC + c, (to[0] * NY + to[1]) * NC + to[2]))
    with jax.named_scope(name):
        return lax.ppermute(x, "fsdp", pairs)


def flip_z(x, mask):
    pairs = [(i, i ^ (mask * NY * NC)) for i in range(NZ * NY * NC)]
    return lax.ppermute(x, "fsdp", pairs)


def flip_replica(x, mask):
    return lax.ppermute(x, "replica", [(i, i ^ mask) for i in range(8)])


Z, Y, CORE, FIRST, FRAG, REPLICA = range(6)
PAIR = 2 * ROWS


def pick(step, values):
    found = values[-1]
    for k, value in enumerate(values[:-1]):
        found = jnp.where(step == k, value, found)
    return found


def block_of(s, step, places):
    dz, dy = pick(step, [p[0] for p in places]), pick(step, [p[1] for p in places])
    return lax.rem(s[Z] + dz, NZ) * NY + lax.rem(s[Y] + dy, NY)


def pair_of(s, step, depths):
    return lax.rem(s[Z] + pick(step, depths), NZ)


def lanes(v, k):
    return v[:, k * 128 : (k + 1) * 128]


def norm_kernel(s_ref, x_ref, cot_ref, gain_ref, excl_ref, mine_ref, *rest):
    sends, (masked_ref, inv_ref) = rest[:NZ], rest[NZ:]
    core = s_ref[CORE]
    rows = x_ref.shape[0]
    position = s_ref[FIRST] + pl.program_id(0) * rows
    position = position + lax.broadcasted_iota(jnp.int32, (rows, 1), 0)
    hits = jnp.where(position == excl_ref[...], 1.0, 0.0)
    kept = 1.0 - jnp.max(hits, axis=1, keepdims=True)
    masked = (cot_ref[...].astype(f32) * kept).astype(bf16)
    mine_ref[:, HALF:] = masked
    masked_ref[...] = masked
    total = jnp.zeros((rows, 128), f32)
    for b in range(D // 128):
        v = x_ref[:, b * 128 : (b + 1) * 128].astype(f32)
        total = total + v * v
    total = jnp.sum(total, axis=1, keepdims=True)
    inverse = jnp.broadcast_to(lax.rsqrt(total / D + 1e-05), inv_ref.shape)
    inv_ref[...] = inverse

    def scaled(at, out, to):
        x = x_ref[:, pl.ds(at, ROWS)].astype(f32)
        gain = gain_ref[:, pl.ds(at, ROWS)]
        for k in range(ROWS // 128):
            v = lanes(x, k) * inverse * lanes(gain, k)
            out[:, to + k * 128 : to + (k + 1) * 128] = v.astype(bf16)

    for j in range(HALF // ROWS):
        scaled(pl.multiple_of((2 * j + core) * ROWS, ROWS), mine_ref, j * ROWS)
    for dz, send_ref in enumerate(sends):
        first = lax.rem(s_ref[Z] + dz, NZ) * NY
        for y in range(NY):
            at = pl.multiple_of((2 * (first + y) + 1 - core) * ROWS, ROWS)
            scaled(at, send_ref, y * ROWS)


def norm_call(scalars, hidden, cot, gain, excl):
    tile = 128
    return pl.pallas_call(
        norm_kernel,
        grid_spec=pltpu.PrefetchScalarGridSpec(
            num_scalar_prefetch=1,
            grid=(ROWS // tile,),
            in_specs=[
                pl.BlockSpec((tile, D), lambda t, s: (t, 0)),
                pl.BlockSpec((tile, KV), lambda t, s: (t, 0)),
                pl.BlockSpec((1, D), lambda t, s: (0, 0)),
                pl.BlockSpec((1, 1024), lambda t, s: (0, 0)),
            ],
            out_specs=[
                pl.BlockSpec((tile, WIDE), lambda t, s: (t, 0)),
                *[pl.BlockSpec((tile, PAIR), lambda t, s: (t, 0))] * NZ,
                pl.BlockSpec((tile, KV), lambda t, s: (t, 0)),
                pl.BlockSpec((tile, 128), lambda t, s: (t, 0)),
            ],
        ),
        out_shape=[
            jax.ShapeDtypeStruct((ROWS, WIDE), bf16),
            *[jax.ShapeDtypeStruct((ROWS, PAIR), bf16)] * NZ,
            jax.ShapeDtypeStruct((ROWS, KV), bf16),
            jax.ShapeDtypeStruct((ROWS, 128), f32),
        ],
        compiler_params=params(1),
        cost_estimate=cost(8),
        name="norm",
    )(scalars, hidden, cot, gain, excl)


def grad_kernel(places, s_ref, x0_ref, c0_ref, c1_ref, *rest):
    count = len(places)
    x1_refs, outs, (x1, x1_sems, held, sems) = rest[:count], rest[count : 2 * count], rest[2 * count :]
    step = pl.program_id(0)
    dims = (((0,), (0,)), ((), ()))
    loads = []
    for k, (_, dy) in enumerate(places):
        at = pl.multiple_of(lax.rem(s_ref[Y] + dy, NY) * ROWS, ROWS)
        loads.append(
            pltpu.make_async_copy(x1_refs[k].at[:, pl.ds(at, ROWS)], x1.at[k], x1_sems.at[k])
        )
    copies = [pltpu.make_async_copy(held.at[k % 2], outs[k], sems.at[k % 2]) for k in range(count)]

    @pl.when(step == 0)
    def _():
        for load in loads:
            load.start()

    total = lax.dot_general(x0_ref[...], c0_ref[...], dims, preferred_element_type=f32)
    for k in range(count):

        @pl.when(step == k)
        def _(k=k):
            loads[k].wait()

    total = total + lax.dot_general(x1[step], c1_ref[...], dims, preferred_element_type=f32)
    total = total.astype(bf16)
    for k in range(count):

        @pl.when(step == k)
        def _(k=k):
            if k >= 2:
                copies[k - 2].wait()
            held[k % 2] = total
            copies[k].start()
            if k == count - 1:
                for copy in copies[max(k - 1, 0) :]:
                    copy.wait()


def grad_call(places, scalars, mine, recv, recv_cot, estimate):
    count = len(places)
    c = pl.BlockSpec((ROWS, KV), lambda t, s: (0, 0))
    return pl.pallas_call(
        functools.partial(grad_kernel, places),
        grid_spec=pltpu.PrefetchScalarGridSpec(
            num_scalar_prefetch=1,
            grid=(count,),
            in_specs=[
                pl.BlockSpec((ROWS, ROWS), lambda t, s: (0, block_of(s, t, places))),
                pl.BlockSpec((ROWS, KV), lambda t, s: (0, HALF // KV)),
                c,
            ]
            + [pl.BlockSpec(memory_space=pltpu.HBM)] * count,
            out_specs=[pl.BlockSpec(memory_space=pltpu.HBM)] * count,
            scratch_shapes=[
                pltpu.VMEM((count, ROWS, ROWS), bf16),
                pltpu.SemaphoreType.DMA((count,)),
                pltpu.VMEM((2, ROWS, KV), bf16),
                pltpu.SemaphoreType.DMA((2,)),
            ],
        ),
        out_shape=[jax.ShapeDtypeStruct((ROWS, KV), bf16)] * count,
        compiler_params=params(1),
        cost_estimate=cost(estimate),
        name="weight_grad_blocks",
    )(scalars, mine, mine, recv_cot, *[recv[dz] for dz, _ in places])


def weight_copies(depths, s_ref, weights, held, sems):
    copies = []
    for k in range(len(depths)):
        for dy in range(NY):
            at = pl.multiple_of(lax.rem(s_ref[Y] + dy, NY) * ROWS, ROWS)
            n = NY * k + dy
            copies.append(
                pltpu.make_async_copy(weights[n], held.at[k, pl.ds(at, ROWS)], sems.at[n])
            )
    return copies


def half_kernel(depths, s_ref, gain_ref, *rest):
    count = len(depths)
    cots, xs, mine_ref, rest = rest[:2], rest[2 : 2 + count], rest[2 + count], rest[3 + count :]
    weights, outs = rest[: NY * count], rest[NY * count : NY * count + 2 * (count + 1)]
    x, cot, held, values, made, in_sems, sems, out_sems = rest[NY * count + 2 * (count + 1) :]
    step = pl.program_id(0)
    copies = weight_copies(depths, s_ref, weights, held, sems)
    loads = []
    for k, ref in enumerate(xs):
        at = pl.multiple_of(lax.rem(s_ref[Z] + depths[k], NZ) * PAIR, PAIR)
        own = mine_ref.at[:, pl.ds(at, PAIR)]
        for n, source in enumerate((ref, own)):
            to = x.at[k, n * ROWS : (n + 1) * ROWS]
            loads.append(pltpu.make_async_copy(source, to, in_sems.at[2 * k + n]))
    for n, ref in enumerate(cots):
        to = cot.at[n * ROWS : (n + 1) * ROWS]
        loads.append(pltpu.make_async_copy(ref, to, in_sems.at[2 * count + n]))
    back = []
    for k in range(count + 1):
        for n in range(2):
            source = made.at[k % 2, n * ROWS : (n + 1) * ROWS]
            back.append(
                pltpu.make_async_copy(source, outs[n * (count + 1) + k], out_sems.at[k % 2, n])
            )

    @pl.when(step == 0)
    def _():
        for k in range(count):
            for copy in (*loads[2 * k : 2 * k + 2], *copies[NY * k : NY * k + NY]):
                copy.start()
            if k == 0:
                for copy in loads[2 * count :]:
                    copy.start()
        for copy in loads[2 * count :]:
            copy.wait()

    for k in range(count):

        @pl.when(step == k)
        def _(k=k):
            for copy in (*loads[2 * k : 2 * k + 2], *copies[NY * k : NY * k + NY]):
                copy.wait()
            if k >= 2:
                back[2 * k - 4].wait()
                back[2 * k - 3].wait()

    w = held[step]
    grad = lax.dot_general(cot[...], w, (((1,), (1,)), ((), ())), preferred_element_type=f32)
    first = lax.rem(s_ref[Z] + pick(step, depths), NZ) * NY
    slot = lax.rem(step, 2)
    for k in range(NY):
        at = pl.multiple_of((2 * (first + k) + s_ref[CORE]) * ROWS, ROWS)
        cols = slice(k * ROWS, (k + 1) * ROWS)
        made[slot, :, cols] = (grad[:, cols] * gain_ref[:, pl.ds(at, ROWS)]).astype(bf16)

    for k in range(count):

        @pl.when(step == k)
        def _(k=k):
            back[2 * k].start()
            back[2 * k + 1].start()

    part = jnp.dot(x[step], w, preferred_element_type=f32)

    @pl.when(step == 0)
    def _():
        values[...] = part

    @pl.when((step > 0) & (step < count - 1))
    def _():
        values[...] += part

    @pl.when(step == count - 1)
    def _():
        if count >= 2:
            back[2 * count - 4].wait()
            back[2 * count - 3].wait()
        made[count % 2] = (values[...] + part).astype(bf16)
        for copy in back[2 * count :]:
            copy.start()
        for copy in back[2 * count - 2 :]:
            copy.wait()


def half_call(depths, scalars, x, mine, cots, gain, w, name):
    count = len(depths)
    weights = [w[dz, dy] for dz in depths for dy in range(NY)]
    made = pl.pallas_call(
        functools.partial(half_kernel, depths),
        grid_spec=pltpu.PrefetchScalarGridSpec(
            num_scalar_prefetch=1,
            grid=(count,),
            in_specs=[pl.BlockSpec((1, D), lambda t, s: (0, 0))]
            + [pl.BlockSpec(memory_space=pltpu.HBM)] * (3 + count + len(weights)),
            out_specs=[pl.BlockSpec(memory_space=pltpu.HBM)] * (2 * (count + 1)),
            scratch_shapes=[
                pltpu.VMEM((count, 2 * ROWS, PAIR), bf16),
                pltpu.VMEM((2 * ROWS, KV), bf16),
                pltpu.VMEM((count, PAIR, KV), bf16),
                pltpu.VMEM((2 * ROWS, KV), f32),
                pltpu.VMEM((2, 2 * ROWS, PAIR), bf16),
                pltpu.SemaphoreType.DMA((2 * count + 2,)),
                pltpu.SemaphoreType.DMA((NY * count,)),
                pltpu.SemaphoreType.DMA((2, 2)),
            ],
        ),
        out_shape=[jax.ShapeDtypeStruct((ROWS, PAIR), bf16)] * (2 * (count + 1)),
        compiler_params=params(1),
        cost_estimate=cost(10),
        name=name,
    )(scalars, gain, *cots, *[x[dz] for dz in depths], mine, *weights)
    return made[: count + 1], made[count + 1 :]


def hidden_kernel(depths, s_ref, x_ref, c_ref, inv_ref, *rest):
    count = len(depths)
    owns, gots, tails = rest[:count], rest[count : 2 * count], rest[2 * count : -2]
    values_ref, out_ref = rest[-2:]
    core = s_ref[CORE]
    values = tails[0][...].astype(f32)
    for tail in tails[1:]:
        values = values + tail[...].astype(f32)
    values_ref[...] = values.astype(bf16)
    mean = jnp.sum(values * c_ref[...].astype(f32), axis=1, keepdims=True) / D
    inverse = inv_ref[...]
    mean = jnp.broadcast_to(mean, inverse.shape) * inverse
    for dz, own_ref, got_ref in zip(depths, owns, gots):
        first = lax.rem(s_ref[Z] + dz, NZ) * NY
        for y in range(NY):
            for parity, w_ref in ((core, own_ref), (1 - core, got_ref)):
                at = pl.multiple_of((2 * (first + y) + parity) * ROWS, ROWS)
                x = x_ref[:, pl.ds(at, ROWS)].astype(f32)
                w = w_ref[:, y * ROWS : (y + 1) * ROWS].astype(f32)
                for n in range(ROWS // 128):
                    v = (lanes(w, n) - lanes(x, n) * mean) * inverse
                    out_ref[:, pl.ds(at + n * 128, 128)] = v.astype(bf16)


def hidden_call(depths, scalars, hidden, cot, inverse, owns, gots, tails):
    tile = 128
    wide = pl.BlockSpec((tile, D), lambda t, s: (t, 0))
    row = pl.BlockSpec((tile, KV), lambda t, s: (t, 0))
    return pl.pallas_call(
        functools.partial(hidden_kernel, depths),
        grid_spec=pltpu.PrefetchScalarGridSpec(
            num_scalar_prefetch=1,
            grid=(ROWS // tile,),
            in_specs=[
                wide,
                row,
                pl.BlockSpec((tile, 128), lambda t, s: (t, 0)),
                *[row] * (2 * len(depths) + len(tails)),
            ],
            out_specs=[row, wide],
        ),
        out_shape=[
            jax.ShapeDtypeStruct((ROWS, KV), bf16),
            jax.ShapeDtypeStruct((ROWS, D), bf16),
        ],
        compiler_params=params(1),
        cost_estimate=cost(100),
        name="hidden_grad",
    )(scalars, hidden, cot, inverse, *owns, *gots, *tails)


def update_kernel(rate, s_ref, w_ref, a_ref, b_ref, c_ref, d_ref, total_ref, *rest):
    anchor_ref, momentum_ref, all_ref, out_ref, anchor_out, momentum_out = rest
    grad = a_ref[...].astype(f32) + b_ref[...].astype(f32)
    grad = grad + (c_ref[...].astype(f32) + d_ref[...].astype(f32))
    out_ref[...] = (w_ref[...].astype(f32) - rate * grad).astype(bf16)
    cols = total_ref.shape[1]
    at = pl.ds(pl.multiple_of(s_ref[FRAG] * cols, cols), cols)
    grad = a_ref[:, at].astype(f32) + b_ref[:, at].astype(f32)
    grad = grad + (c_ref[:, at].astype(f32) + d_ref[:, at].astype(f32))
    now = w_ref[:, at].astype(f32) - rate * grad
    out_ref[:, at] = (mix_weight * total_ref[...] + (1.0 - mix_weight) * now).astype(bf16)

    @pl.when(pl.program_id(0) == 0)
    def _():
        anchor_out[...] = anchor_ref[...]
        momentum_out[...] = momentum_ref[...]
        rows = anchor_ref.shape[2]
        frag = s_ref[FRAG]
        a, m = anchor_ref[frag, 0], momentum_ref[frag, 0]
        at = pl.ds(pl.multiple_of(s_ref[REPLICA] * rows, rows), rows)
        kept = (1.0 - by_delta) * a - by_momentum * m
        delta = a - (all_ref[at, :] - kept) / by_delta
        m_new = outer_momentum * m + delta
        momentum_out[frag, 0] = m_new
        anchor_out[frag, 0] = a - outer_rate * (delta + outer_momentum * m_new)


def update_call(rate, scalars, weight, parts, total, anchor, momentum):
    tile = 256
    row = pl.BlockSpec((tile, KV), lambda t, s: (t, 0))
    whole = pl.BlockSpec(anchor.shape, lambda t, s: (0, 0, 0, 0))
    return pl.pallas_call(
        functools.partial(update_kernel, rate),
        grid_spec=pltpu.PrefetchScalarGridSpec(
            num_scalar_prefetch=1,
            grid=(ROWS // tile,),
            in_specs=[
                *[row] * 5,
                pl.BlockSpec((tile, total.shape[1]), lambda t, s: (t, 0)),
                whole,
                whole,
                pl.BlockSpec(total.shape, lambda t, s: (0, 0)),
            ],
            out_specs=[row, whole, whole],
        ),
        out_shape=[
            jax.ShapeDtypeStruct((ROWS, KV), bf16),
            jax.ShapeDtypeStruct(anchor.shape, f32),
            jax.ShapeDtypeStruct(anchor.shape, f32),
        ],
        compiler_params=params(1),
        cost_estimate=cost(3),
        name="update",
    )(scalars, weight, *parts, total, anchor, momentum, total)


by_delta = outer_rate * (1.0 + outer_momentum)
by_momentum = outer_rate * outer_momentum * outer_momentum


def term_kernel(replicas, s_ref, w_ref, a_ref, m_ref, out_ref):
    rows = a_ref.shape[2]
    out_ref[...] = w_ref[...].astype(f32) * (by_delta / replicas)
    at = pl.ds(pl.multiple_of(s_ref[REPLICA] * rows, rows), rows)
    out_ref[at, :] += (1.0 - by_delta) * a_ref[0, 0] - by_momentum * m_ref[0, 0]


def term_call(replicas, scalars, weight, anchor, momentum):
    _, _, rows, cols = anchor.shape
    state = pl.BlockSpec((1, 1, rows, cols), lambda t, s: (s[FRAG], 0, 0, 0))
    return pl.pallas_call(
        functools.partial(term_kernel, replicas),
        grid_spec=pltpu.PrefetchScalarGridSpec(
            num_scalar_prefetch=1,
            grid=(1,),
            in_specs=[pl.BlockSpec((ROWS, cols), lambda t, s: (0, s[FRAG])), state, state],
            out_specs=pl.BlockSpec((ROWS, cols), lambda t, s: (0, 0)),
        ),
        out_shape=jax.ShapeDtypeStruct((ROWS, cols), f32),
        compiler_params=params(1),
        cost_estimate=cost(1),
        name="outer_term",
    )(scalars, weight, anchor, momentum)


def gain_kernel(places, add, s_ref, *rest):
    count = len(places)
    grads, weights, rest = rest[:count], rest[count : 2 * count], rest[2 * count :]
    out_ref = rest[-1]
    rows = grads[0].shape[0]
    ones = jnp.ones((8, KV), bf16)

    @pl.when(pl.program_id(0) == 0)
    def _():
        out_ref[...] = rest[0][...] if add else jnp.zeros(out_ref.shape, f32)

    for k, (dz, dy) in enumerate(places):
        product = (grads[k][...].astype(f32) * weights[k][...].astype(f32)).astype(bf16)
        sums = lax.dot_general(ones, product, (((1,), (1,)), ((), ())), preferred_element_type=f32)
        block = lax.rem(s_ref[Z] + dz, NZ) * NY + lax.rem(s_ref[Y] + dy, NY)
        at = pl.multiple_of(block * ROWS + pl.program_id(0) * rows, rows)
        out_ref[:, pl.ds(at, rows)] = sums[:1]


def gain_call(places, scalars, g, w, before=None):
    tile = 256
    row = pl.BlockSpec((tile, KV), lambda t, s: (t, 0))
    whole = pl.BlockSpec((1, HALF), lambda t, s: (0, 0))
    extra = [] if before is None else [before]
    return pl.pallas_call(
        functools.partial(gain_kernel, places, before is not None),
        grid_spec=pltpu.PrefetchScalarGridSpec(
            num_scalar_prefetch=1,
            grid=(ROWS // tile,),
            in_specs=[row] * (2 * len(places)) + [whole] * len(extra),
            out_specs=whole,
        ),
        out_shape=jax.ShapeDtypeStruct((1, HALF), f32),
        compiler_params=params(1),
        cost_estimate=cost(0),
        name="gain_grad",
    )(scalars, *[g[p] for p in places], *[w[p] for p in places], *extra)


def relay_kernel(a_ref, b_ref, c_ref, d_ref, e_ref, two_ref, three_ref):
    two_ref[...] = (a_ref[...].astype(f32) + b_ref[...].astype(f32)).astype(bf16)
    three = c_ref[...].astype(f32) + d_ref[...].astype(f32) + e_ref[...].astype(f32)
    three_ref[...] = three.astype(bf16)


def relay_call(*terms):
    row = pl.BlockSpec((ROWS // 4, KV), lambda t: (t, 0))
    return pl.pallas_call(
        relay_kernel,
        grid=(4,),
        in_specs=[row] * 5,
        out_specs=[row] * 2,
        out_shape=[jax.ShapeDtypeStruct((ROWS, KV), bf16)] * 2,
        compiler_params=params(1),
        cost_estimate=cost(3),
        name="relay_sums",
    )(*terms)


def after(x, *others):
    return lax.optimization_barrier((x, *others))[0]


def add(*terms):
    total = terms[0].astype(f32)
    for term in terms[1:]:
        total = total + term.astype(f32)
    return total.astype(bf16)


def body(hidden_in, value_cot, proj_weight, norm_gain, anchor, momentum, excluded, fragment):
    inner_rate = 0.01 / ROWS**0.5
    gain_rate = 0.1 / ROWS**0.5
    hidden, weight = hidden_in[0], proj_weight[0]
    here = lax.axis_index("fsdp")
    replica = lax.axis_index("replica")
    z, y, core = here // (NY * NC), (here // NC) % NY, here % NC
    scalars = jnp.stack([z, y, core, here * ROWS, fragment[0], replica]).astype(jnp.int32)

    w = {(0, 0): weight}
    w[1, 0] = shift(weight, -1, 0, 0, "ag_zm")
    w[0, 1] = shift(weight, 0, 1, 0, "ag_y")
    w[3, 0] = shift(weight, 1, 0, 0, "ag_zp")
    near = (w[0, 1], w[1, 0], w[3, 0])
    w[1, 1] = shift(after(w[0, 1], *near), -1, 0, 0, "ag_B")
    w[2, 0] = shift(after(w[3, 0], *near), 1, 0, 0, "ag_A")

    total = term_call(lax.axis_size("replica"), scalars, weight, anchor, momentum)
    first_term = total
    total = total + flip_replica(after(total, w[0, 1]), 1)
    first_sum = total
    total = total + flip_replica(total, 2)
    second_sum = total
    total = total + flip_replica(total, 6)

    mine, *send, inverse = norm_call(
        after(scalars, first_term), hidden, value_cot[0], norm_gain, excluded
    )
    masked = send[-1]
    recv = [shift(v, 0, 0, 1, "swap_x") for v in send]
    recv_cot = recv.pop()

    g = {}

    def make(places, waits, estimate):
        g.update(zip(places, grad_call(places, after(scalars, *waits), mine, recv, recv_cot, estimate)))

    make([(2, 1), (1, 1), (3, 1), (2, 0), (3, 0), (0, 1), (1, 0), (0, 0)], near, 16)
    far = shift(after(g[2, 1], first_sum), 0, 1, 0, "rs_D")
    w[2, 1] = shift(after(w[1, 1], g[2, 0]), -1, 0, 0, "ag_D")
    w[3, 1] = shift(after(w[0, 1], w[2, 0], g[2, 0]), 1, 0, 0, "ag_C")

    near_half, far_half = (0, 1), (3, 2)
    cots = (recv_cot, masked)
    sent0, own0 = half_call(
        near_half, after(scalars, g[0, 0]), recv, mine, cots, norm_gain, w, "half_near"
    )
    got0 = [shift(v, 0, 0, 1, "swap_w0") for v in sent0]
    near_order = [(dz, dy) for dz in near_half for dy in range(NY)]
    far_order = [(dz, dy) for dz in far_half for dy in range(NY)]
    near_sums = gain_call(near_order, after(scalars, sent0[0]), g, w)
    side = shift(after(g[1, 1], sent0[0]), 0, 1, 0, "rs_B")
    left = shift(after(g[3, 1], near_sums, w[2, 1]), -1, 0, 0, "rs_C")
    over = shift(add(g[2, 0], after(far, near_sums)), 1, 0, 0, "rs_A")
    sent1, own1 = half_call(
        far_half, after(scalars, sent0[0], far), recv, mine, cots, norm_gain, w, "half_far"
    )
    got1 = [shift(v, 0, 0, 1, "swap_w1") for v in sent1]

    partial = gain_call(far_order, after(scalars, sent1[0], second_sum), g, w, near_sums)
    left, side, over = (after(v, partial) for v in (left, side, over))
    from_next = shift(after(g[3, 0], left), -1, 0, 0, "rs_zm")
    to_side, to_last = relay_call(g[0, 1], left, g[1, 0], side, over)
    from_side = shift(to_side, 0, 1, 0, "rs_y")
    from_last = shift(to_last, 1, 0, 0, "rs_zp")

    values_out, hidden_grad = hidden_call(
        (*near_half, *far_half), after(scalars, left, side, over), hidden, masked, inverse,
        (*own0[:-1], *own1[:-1]), (*got0[:-1], *got1[:-1]),
        (own0[-1], own1[-1], got0[-1], got1[-1]),
    )

    partial = partial + shift(partial, 0, 1, 0, "gain_y")
    partial = partial + flip_z(partial, 1)
    partial = partial + flip_z(partial, 3)
    other = shift(after(partial, hidden_grad), 0, 0, 1, "gain_c")
    new_weight, anchor_out, momentum_out = update_call(
        inner_rate,
        scalars,
        weight,
        (after(g[0, 0], hidden_grad), from_next, from_side, from_last),
        total,
        anchor,
        momentum,
    )
    other = after(other, new_weight)
    even = jnp.where(core == 0, partial, other).reshape(HALF // ROWS, ROWS)
    odd = jnp.where(core == 0, other, partial).reshape(HALF // ROWS, ROWS)
    gain_grad = jnp.stack([even, odd], axis=1).reshape(1, D) / norm_gain
    new_gain = norm_gain - gain_rate * gain_grad

    return (
        values_out[None],
        hidden_grad[None],
        new_weight[None],
        new_gain,
        anchor_out,
        momentum_out,
    )


def solution(mesh):
    placed = (
        P("replica", "fsdp", None),
        P("replica", "fsdp", None),
        P("replica", "fsdp", None),
        P("replica", None),
        P(None, "fsdp", "replica", None),
        P(None, "fsdp", "replica", None),
        P("replica", None),
        P(),
    )
    return jax.shard_map(
        body,
        mesh=mesh,
        in_specs=placed,
        out_specs=(
            P("replica", "fsdp", None),
            P("replica", "fsdp", None),
            P("replica", "fsdp", None),
            P("replica", None),
            P(None, "fsdp", "replica", None),
            P(None, "fsdp", "replica", None),
        ),
        check_vma=False,
    )
```

```python
import functools

import jax
import jax.numpy as jnp
from jax import lax
from jax.experimental import pallas as pl
from jax.experimental.pallas import tpu as pltpu
from jax.sharding import PartitionSpec as P

outer_momentum = 0.9
outer_rate = 0.7
mix_weight = 0.5

ROWS = 512
D = 8192
KV = 1024
HALF = D // 2
WIDE = HALF + KV
VMEM = 62 * 1024 * 1024
NZ, NY, NC = 4, 2, 2
bf16, f32 = jnp.bfloat16, jnp.float32


def params(n):
    return pltpu.CompilerParams(dimension_semantics=("arbitrary",) * n, vmem_limit_bytes=VMEM)


def cost(microseconds):
    return pl.CostEstimate(flops=0, bytes_accessed=int(microseconds * 3.3e6), transcendentals=0)


def shift(x, dz, dy, dc, name="x"):
    pairs = []
    for z in range(NZ):
        for y in range(NY):
            for c in range(NC):
                to = ((z + dz) % NZ, (y + dy) % NY, (c + dc) % NC)
                pairs.append(((z * NY + y) * NC + c, (to[0] * NY + to[1]) * NC + to[2]))
    with jax.named_scope(name):
        return lax.ppermute(x, "fsdp", pairs)


def flip_z(x, mask):
    pairs = [(i, i ^ (mask * NY * NC)) for i in range(NZ * NY * NC)]
    return lax.ppermute(x, "fsdp", pairs)


def flip_replica(x, mask):
    return lax.ppermute(x, "replica", [(i, i ^ mask) for i in range(8)])


Z, Y, CORE, FIRST, FRAG, REPLICA = range(6)
PAIR = 2 * ROWS


def pick(step, values):
    found = values[-1]
    for k, value in enumerate(values[:-1]):
        found = jnp.where(step == k, value, found)
    return found


def block_of(s, step, places):
    dz, dy = pick(step, [p[0] for p in places]), pick(step, [p[1] for p in places])
    return lax.rem(s[Z] + dz, NZ) * NY + lax.rem(s[Y] + dy, NY)


def pair_of(s, step, depths):
    return lax.rem(s[Z] + pick(step, depths), NZ)


def lanes(v, k):
    return v[:, k * 128 : (k + 1) * 128]


def norm_kernel(s_ref, x_ref, cot_ref, gain_ref, excl_ref, mine_ref, *rest):
    sends, (masked_ref, inv_ref) = rest[:NZ], rest[NZ:]
    core = s_ref[CORE]
    rows = x_ref.shape[0]
    position = s_ref[FIRST] + pl.program_id(0) * rows
    position = position + lax.broadcasted_iota(jnp.int32, (rows, 1), 0)
    hits = jnp.where(position == excl_ref[...], 1.0, 0.0)
    kept = 1.0 - jnp.max(hits, axis=1, keepdims=True)
    masked = (cot_ref[...].astype(f32) * kept).astype(bf16)
    mine_ref[:, HALF:] = masked
    masked_ref[...] = masked
    total = jnp.zeros((rows, 128), f32)
    for b in range(D // 128):
        v = x_ref[:, b * 128 : (b + 1) * 128].astype(f32)
        total = total + v * v
    total = jnp.sum(total, axis=1, keepdims=True)
    inverse = jnp.broadcast_to(lax.rsqrt(total / D + 1e-05), inv_ref.shape)
    inv_ref[...] = inverse

    def scaled(at, out, to):
        x = x_ref[:, pl.ds(at, ROWS)].astype(f32)
        gain = gain_ref[:, pl.ds(at, ROWS)]
        for k in range(ROWS // 128):
            v = lanes(x, k) * inverse * lanes(gain, k)
            out[:, to + k * 128 : to + (k + 1) * 128] = v.astype(bf16)

    for j in range(HALF // ROWS):
        scaled(pl.multiple_of((2 * j + core) * ROWS, ROWS), mine_ref, j * ROWS)
    for dz, send_ref in enumerate(sends):
        first = lax.rem(s_ref[Z] + dz, NZ) * NY
        for y in range(NY):
            at = pl.multiple_of((2 * (first + y) + 1 - core) * ROWS, ROWS)
            scaled(at, send_ref, y * ROWS)


def norm_call(scalars, hidden, cot, gain, excl):
    tile = 128
    return pl.pallas_call(
        norm_kernel,
        grid_spec=pltpu.PrefetchScalarGridSpec(
            num_scalar_prefetch=1,
            grid=(ROWS // tile,),
            in_specs=[
                pl.BlockSpec((tile, D), lambda t, s: (t, 0)),
                pl.BlockSpec((tile, KV), lambda t, s: (t, 0)),
                pl.BlockSpec((1, D), lambda t, s: (0, 0)),
                pl.BlockSpec((1, 1024), lambda t, s: (0, 0)),
            ],
            out_specs=[
                pl.BlockSpec((tile, WIDE), lambda t, s: (t, 0)),
                *[pl.BlockSpec((tile, PAIR), lambda t, s: (t, 0))] * NZ,
                pl.BlockSpec((tile, KV), lambda t, s: (t, 0)),
                pl.BlockSpec((tile, 128), lambda t, s: (t, 0)),
            ],
        ),
        out_shape=[
            jax.ShapeDtypeStruct((ROWS, WIDE), bf16),
            *[jax.ShapeDtypeStruct((ROWS, PAIR), bf16)] * NZ,
            jax.ShapeDtypeStruct((ROWS, KV), bf16),
            jax.ShapeDtypeStruct((ROWS, 128), f32),
        ],
        compiler_params=params(1),
        cost_estimate=cost(8),
        name="norm",
    )(scalars, hidden, cot, gain, excl)


def grad_kernel(places, s_ref, x0_ref, c0_ref, c1_ref, *rest):
    count = len(places)
    x1_refs, outs, (x1, x1_sems, held, sems) = rest[:count], rest[count : 2 * count], rest[2 * count :]
    step = pl.program_id(0)
    dims = (((0,), (0,)), ((), ()))
    loads = []
    for k, (_, dy) in enumerate(places):
        at = pl.multiple_of(lax.rem(s_ref[Y] + dy, NY) * ROWS, ROWS)
        loads.append(
            pltpu.make_async_copy(x1_refs[k].at[:, pl.ds(at, ROWS)], x1.at[k], x1_sems.at[k])
        )
    copies = [pltpu.make_async_copy(held.at[k % 2], outs[k], sems.at[k % 2]) for k in range(count)]

    @pl.when(step == 0)
    def _():
        for load in loads:
            load.start()

    total = lax.dot_general(x0_ref[...], c0_ref[...], dims, preferred_element_type=f32)
    for k in range(count):

        @pl.when(step == k)
        def _(k=k):
            loads[k].wait()

    total = total + lax.dot_general(x1[step], c1_ref[...], dims, preferred_element_type=f32)
    total = total.astype(bf16)
    for k in range(count):

        @pl.when(step == k)
        def _(k=k):
            if k >= 2:
                copies[k - 2].wait()
            held[k % 2] = total
            copies[k].start()
            if k == count - 1:
                for copy in copies[max(k - 1, 0) :]:
                    copy.wait()


def grad_call(places, scalars, mine, recv, recv_cot, estimate):
    count = len(places)
    c = pl.BlockSpec((ROWS, KV), lambda t, s: (0, 0))
    return pl.pallas_call(
        functools.partial(grad_kernel, places),
        grid_spec=pltpu.PrefetchScalarGridSpec(
            num_scalar_prefetch=1,
            grid=(count,),
            in_specs=[
                pl.BlockSpec((ROWS, ROWS), lambda t, s: (0, block_of(s, t, places))),
                pl.BlockSpec((ROWS, KV), lambda t, s: (0, HALF // KV)),
                c,
            ]
            + [pl.BlockSpec(memory_space=pltpu.HBM)] * count,
            out_specs=[pl.BlockSpec(memory_space=pltpu.HBM)] * count,
            scratch_shapes=[
                pltpu.VMEM((count, ROWS, ROWS), bf16),
                pltpu.SemaphoreType.DMA((count,)),
                pltpu.VMEM((2, ROWS, KV), bf16),
                pltpu.SemaphoreType.DMA((2,)),
            ],
        ),
        out_shape=[jax.ShapeDtypeStruct((ROWS, KV), bf16)] * count,
        compiler_params=params(1),
        cost_estimate=cost(estimate),
        name="weight_grad_blocks",
    )(scalars, mine, mine, recv_cot, *[recv[dz] for dz, _ in places])


def weight_copies(depths, s_ref, weights, held, sems):
    copies = []
    for k in range(len(depths)):
        for dy in range(NY):
            at = pl.multiple_of(lax.rem(s_ref[Y] + dy, NY) * ROWS, ROWS)
            n = NY * k + dy
            copies.append(
                pltpu.make_async_copy(weights[n], held.at[k, pl.ds(at, ROWS)], sems.at[n])
            )
    return copies


def half_kernel(depths, s_ref, gain_ref, *rest):
    count = len(depths)
    cots, xs, mine_ref, rest = rest[:2], rest[2 : 2 + count], rest[2 + count], rest[3 + count :]
    weights, outs = rest[: NY * count], rest[NY * count : NY * count + 2 * (count + 1)]
    x, cot, held, values, made, in_sems, sems, out_sems = rest[NY * count + 2 * (count + 1) :]
    step = pl.program_id(0)
    copies = weight_copies(depths, s_ref, weights, held, sems)
    loads = []
    for k, ref in enumerate(xs):
        at = pl.multiple_of(lax.rem(s_ref[Z] + depths[k], NZ) * PAIR, PAIR)
        own = mine_ref.at[:, pl.ds(at, PAIR)]
        for n, source in enumerate((ref, own)):
            to = x.at[k, n * ROWS : (n + 1) * ROWS]
            loads.append(pltpu.make_async_copy(source, to, in_sems.at[2 * k + n]))
    for n, ref in enumerate(cots):
        to = cot.at[n * ROWS : (n + 1) * ROWS]
        loads.append(pltpu.make_async_copy(ref, to, in_sems.at[2 * count + n]))
    back = []
    for k in range(count + 1):
        for n in range(2):
            source = made.at[k % 2, n * ROWS : (n + 1) * ROWS]
            back.append(
                pltpu.make_async_copy(source, outs[n * (count + 1) + k], out_sems.at[k % 2, n])
            )

    @pl.when(step == 0)
    def _():
        for k in range(count):
            for copy in (*loads[2 * k : 2 * k + 2], *copies[NY * k : NY * k + NY]):
                copy.start()
            if k == 0:
                for copy in loads[2 * count :]:
                    copy.start()
        for copy in loads[2 * count :]:
            copy.wait()

    for k in range(count):

        @pl.when(step == k)
        def _(k=k):
            for copy in (*loads[2 * k : 2 * k + 2], *copies[NY * k : NY * k + NY]):
                copy.wait()
            if k >= 2:
                back[2 * k - 4].wait()
                back[2 * k - 3].wait()

    w = held[step]
    grad = lax.dot_general(cot[...], w, (((1,), (1,)), ((), ())), preferred_element_type=f32)
    first = lax.rem(s_ref[Z] + pick(step, depths), NZ) * NY
    slot = lax.rem(step, 2)
    for k in range(NY):
        at = pl.multiple_of((2 * (first + k) + s_ref[CORE]) * ROWS, ROWS)
        cols = slice(k * ROWS, (k + 1) * ROWS)
        made[slot, :, cols] = (grad[:, cols] * gain_ref[:, pl.ds(at, ROWS)]).astype(bf16)

    for k in range(count):

        @pl.when(step == k)
        def _(k=k):
            back[2 * k].start()
            back[2 * k + 1].start()

    part = jnp.dot(x[step], w, preferred_element_type=f32)

    @pl.when(step == 0)
    def _():
        values[...] = part

    @pl.when((step > 0) & (step < count - 1))
    def _():
        values[...] += part

    @pl.when(step == count - 1)
    def _():
        if count >= 2:
            back[2 * count - 4].wait()
            back[2 * count - 3].wait()
        made[count % 2] = (values[...] + part).astype(bf16)
        for copy in back[2 * count :]:
            copy.start()
        for copy in back[2 * count - 2 :]:
            copy.wait()


def half_call(depths, scalars, x, mine, cots, gain, w, name):
    count = len(depths)
    weights = [w[dz, dy] for dz in depths for dy in range(NY)]
    made = pl.pallas_call(
        functools.partial(half_kernel, depths),
        grid_spec=pltpu.PrefetchScalarGridSpec(
            num_scalar_prefetch=1,
            grid=(count,),
            in_specs=[pl.BlockSpec((1, D), lambda t, s: (0, 0))]
            + [pl.BlockSpec(memory_space=pltpu.HBM)] * (3 + count + len(weights)),
            out_specs=[pl.BlockSpec(memory_space=pltpu.HBM)] * (2 * (count + 1)),
            scratch_shapes=[
                pltpu.VMEM((count, 2 * ROWS, PAIR), bf16),
                pltpu.VMEM((2 * ROWS, KV), bf16),
                pltpu.VMEM((count, PAIR, KV), bf16),
                pltpu.VMEM((2 * ROWS, KV), f32),
                pltpu.VMEM((2, 2 * ROWS, PAIR), bf16),
                pltpu.SemaphoreType.DMA((2 * count + 2,)),
                pltpu.SemaphoreType.DMA((NY * count,)),
                pltpu.SemaphoreType.DMA((2, 2)),
            ],
        ),
        out_shape=[jax.ShapeDtypeStruct((ROWS, PAIR), bf16)] * (2 * (count + 1)),
        compiler_params=params(1),
        cost_estimate=cost(10),
        name=name,
    )(scalars, gain, *cots, *[x[dz] for dz in depths], mine, *weights)
    return made[: count + 1], made[count + 1 :]


def hidden_kernel(depths, s_ref, x_ref, c_ref, inv_ref, *rest):
    count = len(depths)
    owns, gots, tails = rest[:count], rest[count : 2 * count], rest[2 * count : -2]
    values_ref, out_ref = rest[-2:]
    core = s_ref[CORE]
    values = tails[0][...].astype(f32)
    for tail in tails[1:]:
        values = values + tail[...].astype(f32)
    values_ref[...] = values.astype(bf16)
    mean = jnp.sum(values * c_ref[...].astype(f32), axis=1, keepdims=True) / D
    inverse = inv_ref[...]
    mean = jnp.broadcast_to(mean, inverse.shape) * inverse
    for dz, own_ref, got_ref in zip(depths, owns, gots):
        first = lax.rem(s_ref[Z] + dz, NZ) * NY
        for y in range(NY):
            for parity, w_ref in ((core, own_ref), (1 - core, got_ref)):
                at = pl.multiple_of((2 * (first + y) + parity) * ROWS, ROWS)
                x = x_ref[:, pl.ds(at, ROWS)].astype(f32)
                w = w_ref[:, y * ROWS : (y + 1) * ROWS].astype(f32)
                for n in range(ROWS // 128):
                    v = (lanes(w, n) - lanes(x, n) * mean) * inverse
                    out_ref[:, pl.ds(at + n * 128, 128)] = v.astype(bf16)


def hidden_call(depths, scalars, hidden, cot, inverse, owns, gots, tails):
    tile = 128
    wide = pl.BlockSpec((tile, D), lambda t, s: (t, 0))
    row = pl.BlockSpec((tile, KV), lambda t, s: (t, 0))
    return pl.pallas_call(
        functools.partial(hidden_kernel, depths),
        grid_spec=pltpu.PrefetchScalarGridSpec(
            num_scalar_prefetch=1,
            grid=(ROWS // tile,),
            in_specs=[
                wide,
                row,
                pl.BlockSpec((tile, 128), lambda t, s: (t, 0)),
                *[row] * (2 * len(depths) + len(tails)),
            ],
            out_specs=[row, wide],
        ),
        out_shape=[
            jax.ShapeDtypeStruct((ROWS, KV), bf16),
            jax.ShapeDtypeStruct((ROWS, D), bf16),
        ],
        compiler_params=params(1),
        cost_estimate=cost(100),
        name="hidden_grad",
    )(scalars, hidden, cot, inverse, *owns, *gots, *tails)


def update_kernel(rate, s_ref, w_ref, a_ref, b_ref, c_ref, d_ref, total_ref, *rest):
    anchor_ref, momentum_ref, all_ref, out_ref, anchor_out, momentum_out = rest
    grad = a_ref[...].astype(f32) + b_ref[...].astype(f32)
    grad = grad + (c_ref[...].astype(f32) + d_ref[...].astype(f32))
    out_ref[...] = (w_ref[...].astype(f32) - rate * grad).astype(bf16)
    cols = total_ref.shape[1]
    at = pl.ds(pl.multiple_of(s_ref[FRAG] * cols, cols), cols)
    grad = a_ref[:, at].astype(f32) + b_ref[:, at].astype(f32)
    grad = grad + (c_ref[:, at].astype(f32) + d_ref[:, at].astype(f32))
    now = w_ref[:, at].astype(f32) - rate * grad
    out_ref[:, at] = (mix_weight * total_ref[...] + (1.0 - mix_weight) * now).astype(bf16)

    @pl.when(pl.program_id(0) == 0)
    def _():
        anchor_out[...] = anchor_ref[...]
        momentum_out[...] = momentum_ref[...]
        rows = anchor_ref.shape[2]
        frag = s_ref[FRAG]
        a, m = anchor_ref[frag, 0], momentum_ref[frag, 0]
        at = pl.ds(pl.multiple_of(s_ref[REPLICA] * rows, rows), rows)
        kept = (1.0 - by_delta) * a - by_momentum * m
        delta = a - (all_ref[at, :] - kept) / by_delta
        m_new = outer_momentum * m + delta
        momentum_out[frag, 0] = m_new
        anchor_out[frag, 0] = a - outer_rate * (delta + outer_momentum * m_new)


def update_call(rate, scalars, weight, parts, total, anchor, momentum):
    tile = 256
    row = pl.BlockSpec((tile, KV), lambda t, s: (t, 0))
    whole = pl.BlockSpec(anchor.shape, lambda t, s: (0, 0, 0, 0))
    return pl.pallas_call(
        functools.partial(update_kernel, rate),
        grid_spec=pltpu.PrefetchScalarGridSpec(
            num_scalar_prefetch=1,
            grid=(ROWS // tile,),
            in_specs=[
                *[row] * 5,
                pl.BlockSpec((tile, total.shape[1]), lambda t, s: (t, 0)),
                whole,
                whole,
                pl.BlockSpec(total.shape, lambda t, s: (0, 0)),
            ],
            out_specs=[row, whole, whole],
        ),
        out_shape=[
            jax.ShapeDtypeStruct((ROWS, KV), bf16),
            jax.ShapeDtypeStruct(anchor.shape, f32),
            jax.ShapeDtypeStruct(anchor.shape, f32),
        ],
        compiler_params=params(1),
        cost_estimate=cost(3),
        name="update",
    )(scalars, weight, *parts, total, anchor, momentum, total)


by_delta = outer_rate * (1.0 + outer_momentum)
by_momentum = outer_rate * outer_momentum * outer_momentum


def term_kernel(replicas, s_ref, w_ref, a_ref, m_ref, out_ref):
    rows = a_ref.shape[2]
    out_ref[...] = w_ref[...].astype(f32) * (by_delta / replicas)
    at = pl.ds(pl.multiple_of(s_ref[REPLICA] * rows, rows), rows)
    out_ref[at, :] += (1.0 - by_delta) * a_ref[0, 0] - by_momentum * m_ref[0, 0]


def term_call(replicas, scalars, weight, anchor, momentum):
    _, _, rows, cols = anchor.shape
    state = pl.BlockSpec((1, 1, rows, cols), lambda t, s: (s[FRAG], 0, 0, 0))
    return pl.pallas_call(
        functools.partial(term_kernel, replicas),
        grid_spec=pltpu.PrefetchScalarGridSpec(
            num_scalar_prefetch=1,
            grid=(1,),
            in_specs=[pl.BlockSpec((ROWS, cols), lambda t, s: (0, s[FRAG])), state, state],
            out_specs=pl.BlockSpec((ROWS, cols), lambda t, s: (0, 0)),
        ),
        out_shape=jax.ShapeDtypeStruct((ROWS, cols), f32),
        compiler_params=params(1),
        cost_estimate=cost(1),
        name="outer_term",
    )(scalars, weight, anchor, momentum)


def gain_kernel(places, add, s_ref, *rest):
    count = len(places)
    grads, weights, rest = rest[:count], rest[count : 2 * count], rest[2 * count :]
    out_ref = rest[-1]
    rows = grads[0].shape[0]
    ones = jnp.ones((8, KV), bf16)

    @pl.when(pl.program_id(0) == 0)
    def _():
        out_ref[...] = rest[0][...] if add else jnp.zeros(out_ref.shape, f32)

    for k, (dz, dy) in enumerate(places):
        product = (grads[k][...].astype(f32) * weights[k][...].astype(f32)).astype(bf16)
        sums = lax.dot_general(ones, product, (((1,), (1,)), ((), ())), preferred_element_type=f32)
        block = lax.rem(s_ref[Z] + dz, NZ) * NY + lax.rem(s_ref[Y] + dy, NY)
        at = pl.multiple_of(block * ROWS + pl.program_id(0) * rows, rows)
        out_ref[:, pl.ds(at, rows)] = sums[:1]


def gain_call(places, scalars, g, w, before=None):
    tile = 256
    row = pl.BlockSpec((tile, KV), lambda t, s: (t, 0))
    whole = pl.BlockSpec((1, HALF), lambda t, s: (0, 0))
    extra = [] if before is None else [before]
    return pl.pallas_call(
        functools.partial(gain_kernel, places, before is not None),
        grid_spec=pltpu.PrefetchScalarGridSpec(
            num_scalar_prefetch=1,
            grid=(ROWS // tile,),
            in_specs=[row] * (2 * len(places)) + [whole] * len(extra),
            out_specs=whole,
        ),
        out_shape=jax.ShapeDtypeStruct((1, HALF), f32),
        compiler_params=params(1),
        cost_estimate=cost(0),
        name="gain_grad",
    )(scalars, *[g[p] for p in places], *[w[p] for p in places], *extra)


def relay_kernel(a_ref, b_ref, c_ref, d_ref, e_ref, two_ref, three_ref):
    two_ref[...] = (a_ref[...].astype(f32) + b_ref[...].astype(f32)).astype(bf16)
    three = c_ref[...].astype(f32) + d_ref[...].astype(f32) + e_ref[...].astype(f32)
    three_ref[...] = three.astype(bf16)


def relay_call(*terms):
    row = pl.BlockSpec((ROWS // 4, KV), lambda t: (t, 0))
    return pl.pallas_call(
        relay_kernel,
        grid=(4,),
        in_specs=[row] * 5,
        out_specs=[row] * 2,
        out_shape=[jax.ShapeDtypeStruct((ROWS, KV), bf16)] * 2,
        compiler_params=params(1),
        cost_estimate=cost(3),
        name="relay_sums",
    )(*terms)


def after(x, *others):
    return lax.optimization_barrier((x, *others))[0]


def add(*terms):
    total = terms[0].astype(f32)
    for term in terms[1:]:
        total = total + term.astype(f32)
    return total.astype(bf16)


def body(hidden_in, value_cot, proj_weight, norm_gain, anchor, momentum, excluded, fragment):
    inner_rate = 0.01 / ROWS**0.5
    gain_rate = 0.1 / ROWS**0.5
    hidden, weight = hidden_in[0], proj_weight[0]
    here = lax.axis_index("fsdp")
    replica = lax.axis_index("replica")
    z, y, core = here // (NY * NC), (here // NC) % NY, here % NC
    scalars = jnp.stack([z, y, core, here * ROWS, fragment[0], replica]).astype(jnp.int32)

    w = {(0, 0): weight}
    w[1, 0] = shift(weight, -1, 0, 0, "ag_zm")
    w[0, 1] = shift(weight, 0, 1, 0, "ag_y")
    w[3, 0] = shift(weight, 1, 0, 0, "ag_zp")
    near = (w[0, 1], w[1, 0], w[3, 0])
    w[1, 1] = shift(after(w[0, 1], *near), -1, 0, 0, "ag_B")
    w[2, 0] = shift(after(w[3, 0], *near), 1, 0, 0, "ag_A")

    total = term_call(lax.axis_size("replica"), scalars, weight, anchor, momentum)
    first_term = total
    total = total + flip_replica(after(total, w[0, 1]), 1)
    first_sum = total
    total = total + flip_replica(total, 2)
    second_sum = total
    total = total + flip_replica(total, 6)

    mine, *send, inverse = norm_call(
        after(scalars, first_term), hidden, value_cot[0], norm_gain, excluded
    )
    masked = send[-1]
    recv = [shift(v, 0, 0, 1, "swap_x") for v in send]
    recv_cot = recv.pop()

    g = {}

    def make(places, waits, estimate):
        g.update(zip(places, grad_call(places, after(scalars, *waits), mine, recv, recv_cot, estimate)))

    make([(2, 1), (1, 1), (3, 1), (2, 0), (3, 0), (0, 1), (1, 0), (0, 0)], near, 16)
    far = shift(after(g[2, 1], first_sum), 0, 1, 0, "rs_D")
    w[2, 1] = shift(after(w[1, 1], g[2, 0]), -1, 0, 0, "ag_D")
    w[3, 1] = shift(after(w[0, 1], w[2, 0], g[2, 0]), 1, 0, 0, "ag_C")

    near_half, far_half = (0, 1), (3, 2)
    cots = (recv_cot, masked)
    sent0, own0 = half_call(
        near_half, after(scalars, g[0, 0]), recv, mine, cots, norm_gain, w, "half_near"
    )
    got0 = [shift(v, 0, 0, 1, "swap_w0") for v in sent0]
    near_order = [(dz, dy) for dz in near_half for dy in range(NY)]
    far_order = [(dz, dy) for dz in far_half for dy in range(NY)]
    near_sums = gain_call(near_order, after(scalars, sent0[0]), g, w)
    side = shift(after(g[1, 1], sent0[0]), 0, 1, 0, "rs_B")
    left = shift(after(g[3, 1], near_sums, w[2, 1]), -1, 0, 0, "rs_C")
    over = shift(add(g[2, 0], after(far, near_sums)), 1, 0, 0, "rs_A")
    sent1, own1 = half_call(
        far_half, after(scalars, sent0[0], far), recv, mine, cots, norm_gain, w, "half_far"
    )

    partial = gain_call(far_order, after(scalars, sent1[0], second_sum), g, w, near_sums)
    got1 = [shift(after(v, partial), 0, 0, 1, "swap_w1") for v in sent1]
    left, side, over = (after(v, partial) for v in (left, side, over))
    from_next = shift(after(g[3, 0], left), -1, 0, 0, "rs_zm")
    to_side, to_last = relay_call(g[0, 1], left, g[1, 0], side, over)
    from_side = shift(to_side, 0, 1, 0, "rs_y")
    from_last = shift(to_last, 1, 0, 0, "rs_zp")

    values_out, hidden_grad = hidden_call(
        (*near_half, *far_half), after(scalars, left, side, over), hidden, masked, inverse,
        (*own0[:-1], *own1[:-1]), (*got0[:-1], *got1[:-1]),
        (own0[-1], own1[-1], got0[-1], got1[-1]),
    )

    partial = partial + shift(after(partial, to_last), 0, 1, 0, "gain_y")
    partial = partial + flip_z(partial, 1)
    partial = partial + flip_z(partial, 3)
    other = shift(after(partial, hidden_grad), 0, 0, 1, "gain_c")
    new_weight, anchor_out, momentum_out = update_call(
        inner_rate,
        scalars,
        weight,
        (after(g[0, 0], hidden_grad), from_next, from_side, from_last),
        total,
        anchor,
        momentum,
    )
    other = after(other, new_weight)
    even = jnp.where(core == 0, partial, other).reshape(HALF // ROWS, ROWS)
    odd = jnp.where(core == 0, other, partial).reshape(HALF // ROWS, ROWS)
    gain_grad = jnp.stack([even, odd], axis=1).reshape(1, D) / norm_gain
    new_gain = norm_gain - gain_rate * gain_grad

    return (
        values_out[None],
        hidden_grad[None],
        new_weight[None],
        new_gain,
        anchor_out,
        momentum_out,
    )


def solution(mesh):
    placed = (
        P("replica", "fsdp", None),
        P("replica", "fsdp", None),
        P("replica", "fsdp", None),
        P("replica", None),
        P(None, "fsdp", "replica", None),
        P(None, "fsdp", "replica", None),
        P("replica", None),
        P(),
    )
    return jax.shard_map(
        body,
        mesh=mesh,
        in_specs=placed,
        out_specs=(
            P("replica", "fsdp", None),
            P("replica", "fsdp", None),
            P("replica", "fsdp", None),
            P("replica", None),
            P(None, "fsdp", "replica", None),
            P(None, "fsdp", "replica", None),
        ),
        check_vma=False,
    )
```

```python
import functools

import jax
import jax.numpy as jnp
from jax import lax
from jax.experimental import pallas as pl
from jax.experimental.pallas import tpu as pltpu
from jax.sharding import PartitionSpec as P

outer_momentum = 0.9
outer_rate = 0.7
mix_weight = 0.5

ROWS = 512
D = 8192
KV = 1024
HALF = D // 2
WIDE = HALF + KV
VMEM = 62 * 1024 * 1024
NZ, NY, NC = 4, 2, 2
bf16, f32 = jnp.bfloat16, jnp.float32


def params(n):
    return pltpu.CompilerParams(dimension_semantics=("arbitrary",) * n, vmem_limit_bytes=VMEM)


def cost(microseconds):
    return pl.CostEstimate(flops=0, bytes_accessed=int(microseconds * 3.3e6), transcendentals=0)


def shift(x, dz, dy, dc, name="x"):
    pairs = []
    for z in range(NZ):
        for y in range(NY):
            for c in range(NC):
                to = ((z + dz) % NZ, (y + dy) % NY, (c + dc) % NC)
                pairs.append(((z * NY + y) * NC + c, (to[0] * NY + to[1]) * NC + to[2]))
    with jax.named_scope(name):
        return lax.ppermute(x, "fsdp", pairs)


def flip_z(x, mask):
    pairs = [(i, i ^ (mask * NY * NC)) for i in range(NZ * NY * NC)]
    return lax.ppermute(x, "fsdp", pairs)


def flip_replica(x, mask):
    return lax.ppermute(x, "replica", [(i, i ^ mask) for i in range(8)])


Z, Y, CORE, FIRST, FRAG, REPLICA = range(6)
PAIR = 2 * ROWS


def pick(step, values):
    found = values[-1]
    for k, value in enumerate(values[:-1]):
        found = jnp.where(step == k, value, found)
    return found


def block_of(s, step, places):
    dz, dy = pick(step, [p[0] for p in places]), pick(step, [p[1] for p in places])
    return lax.rem(s[Z] + dz, NZ) * NY + lax.rem(s[Y] + dy, NY)


def pair_of(s, step, depths):
    return lax.rem(s[Z] + pick(step, depths), NZ)


def lanes(v, k):
    return v[:, k * 128 : (k + 1) * 128]


def norm_kernel(s_ref, x_ref, cot_ref, gain_ref, excl_ref, mine_ref, *rest):
    sends, (masked_ref, inv_ref) = rest[:NZ], rest[NZ:]
    core = s_ref[CORE]
    rows = x_ref.shape[0]
    position = s_ref[FIRST] + pl.program_id(0) * rows
    position = position + lax.broadcasted_iota(jnp.int32, (rows, 1), 0)
    hits = jnp.where(position == excl_ref[...], 1.0, 0.0)
    kept = 1.0 - jnp.max(hits, axis=1, keepdims=True)
    masked = (cot_ref[...].astype(f32) * kept).astype(bf16)
    mine_ref[:, HALF:] = masked
    masked_ref[...] = masked
    total = jnp.zeros((rows, 128), f32)
    for b in range(D // 128):
        v = x_ref[:, b * 128 : (b + 1) * 128].astype(f32)
        total = total + v * v
    total = jnp.sum(total, axis=1, keepdims=True)
    inverse = jnp.broadcast_to(lax.rsqrt(total / D + 1e-05), inv_ref.shape)
    inv_ref[...] = inverse

    def scaled(at, out, to):
        x = x_ref[:, pl.ds(at, ROWS)].astype(f32)
        gain = gain_ref[:, pl.ds(at, ROWS)]
        for k in range(ROWS // 128):
            v = lanes(x, k) * inverse * lanes(gain, k)
            out[:, to + k * 128 : to + (k + 1) * 128] = v.astype(bf16)

    for j in range(HALF // ROWS):
        scaled(pl.multiple_of((2 * j + core) * ROWS, ROWS), mine_ref, j * ROWS)
    for dz, send_ref in enumerate(sends):
        first = lax.rem(s_ref[Z] + dz, NZ) * NY
        for y in range(NY):
            at = pl.multiple_of((2 * (first + y) + 1 - core) * ROWS, ROWS)
            scaled(at, send_ref, y * ROWS)


def norm_call(scalars, hidden, cot, gain, excl):
    tile = 128
    return pl.pallas_call(
        norm_kernel,
        grid_spec=pltpu.PrefetchScalarGridSpec(
            num_scalar_prefetch=1,
            grid=(ROWS // tile,),
            in_specs=[
                pl.BlockSpec((tile, D), lambda t, s: (t, 0)),
                pl.BlockSpec((tile, KV), lambda t, s: (t, 0)),
                pl.BlockSpec((1, D), lambda t, s: (0, 0)),
                pl.BlockSpec((1, 1024), lambda t, s: (0, 0)),
            ],
            out_specs=[
                pl.BlockSpec((tile, WIDE), lambda t, s: (t, 0)),
                *[pl.BlockSpec((tile, PAIR), lambda t, s: (t, 0))] * NZ,
                pl.BlockSpec((tile, KV), lambda t, s: (t, 0)),
                pl.BlockSpec((tile, 128), lambda t, s: (t, 0)),
            ],
        ),
        out_shape=[
            jax.ShapeDtypeStruct((ROWS, WIDE), bf16),
            *[jax.ShapeDtypeStruct((ROWS, PAIR), bf16)] * NZ,
            jax.ShapeDtypeStruct((ROWS, KV), bf16),
            jax.ShapeDtypeStruct((ROWS, 128), f32),
        ],
        compiler_params=params(1),
        cost_estimate=cost(8),
        name="norm",
    )(scalars, hidden, cot, gain, excl)


def grad_kernel(places, s_ref, x0_ref, c0_ref, c1_ref, *rest):
    count = len(places)
    x1_refs, outs, (x1, x1_sems, held, sems) = rest[:count], rest[count : 2 * count], rest[2 * count :]
    step = pl.program_id(0)
    dims = (((0,), (0,)), ((), ()))
    loads = []
    for k, (_, dy) in enumerate(places):
        at = pl.multiple_of(lax.rem(s_ref[Y] + dy, NY) * ROWS, ROWS)
        loads.append(
            pltpu.make_async_copy(x1_refs[k].at[:, pl.ds(at, ROWS)], x1.at[k], x1_sems.at[k])
        )
    copies = [pltpu.make_async_copy(held.at[k % 2], outs[k], sems.at[k % 2]) for k in range(count)]

    @pl.when(step == 0)
    def _():
        for load in loads:
            load.start()

    total = lax.dot_general(x0_ref[...], c0_ref[...], dims, preferred_element_type=f32)
    for k in range(count):

        @pl.when(step == k)
        def _(k=k):
            loads[k].wait()

    total = total + lax.dot_general(x1[step], c1_ref[...], dims, preferred_element_type=f32)
    total = total.astype(bf16)
    for k in range(count):

        @pl.when(step == k)
        def _(k=k):
            if k >= 2:
                copies[k - 2].wait()
            held[k % 2] = total
            copies[k].start()
            if k == count - 1:
                for copy in copies[max(k - 1, 0) :]:
                    copy.wait()


def grad_call(places, scalars, mine, recv, recv_cot, estimate):
    count = len(places)
    c = pl.BlockSpec((ROWS, KV), lambda t, s: (0, 0))
    return pl.pallas_call(
        functools.partial(grad_kernel, places),
        grid_spec=pltpu.PrefetchScalarGridSpec(
            num_scalar_prefetch=1,
            grid=(count,),
            in_specs=[
                pl.BlockSpec((ROWS, ROWS), lambda t, s: (0, block_of(s, t, places))),
                pl.BlockSpec((ROWS, KV), lambda t, s: (0, HALF // KV)),
                c,
            ]
            + [pl.BlockSpec(memory_space=pltpu.HBM)] * count,
            out_specs=[pl.BlockSpec(memory_space=pltpu.HBM)] * count,
            scratch_shapes=[
                pltpu.VMEM((count, ROWS, ROWS), bf16),
                pltpu.SemaphoreType.DMA((count,)),
                pltpu.VMEM((2, ROWS, KV), bf16),
                pltpu.SemaphoreType.DMA((2,)),
            ],
        ),
        out_shape=[jax.ShapeDtypeStruct((ROWS, KV), bf16)] * count,
        compiler_params=params(1),
        cost_estimate=cost(estimate),
        name="weight_grad_blocks",
    )(scalars, mine, mine, recv_cot, *[recv[dz] for dz, _ in places])


def weight_copies(depths, s_ref, weights, held, sems):
    copies = []
    for k in range(len(depths)):
        for dy in range(NY):
            at = pl.multiple_of(lax.rem(s_ref[Y] + dy, NY) * ROWS, ROWS)
            n = NY * k + dy
            copies.append(
                pltpu.make_async_copy(weights[n], held.at[k, pl.ds(at, ROWS)], sems.at[n])
            )
    return copies


def half_kernel(depths, s_ref, gain_ref, *rest):
    count = len(depths)
    cots, xs, mine_ref, rest = rest[:2], rest[2 : 2 + count], rest[2 + count], rest[3 + count :]
    weights, outs = rest[: NY * count], rest[NY * count : NY * count + 2 * (count + 1)]
    x, cot, held, values, made, in_sems, sems, out_sems = rest[NY * count + 2 * (count + 1) :]
    step = pl.program_id(0)
    copies = weight_copies(depths, s_ref, weights, held, sems)
    loads = []
    for k, ref in enumerate(xs):
        at = pl.multiple_of(lax.rem(s_ref[Z] + depths[k], NZ) * PAIR, PAIR)
        own = mine_ref.at[:, pl.ds(at, PAIR)]
        for n, source in enumerate((ref, own)):
            to = x.at[k, n * ROWS : (n + 1) * ROWS]
            loads.append(pltpu.make_async_copy(source, to, in_sems.at[2 * k + n]))
    for n, ref in enumerate(cots):
        to = cot.at[n * ROWS : (n + 1) * ROWS]
        loads.append(pltpu.make_async_copy(ref, to, in_sems.at[2 * count + n]))
    back = []
    for k in range(count + 1):
        for n in range(2):
            source = made.at[k % 2, n * ROWS : (n + 1) * ROWS]
            back.append(
                pltpu.make_async_copy(source, outs[n * (count + 1) + k], out_sems.at[k % 2, n])
            )

    @pl.when(step == 0)
    def _():
        for k in range(count):
            for copy in (*loads[2 * k : 2 * k + 2], *copies[NY * k : NY * k + NY]):
                copy.start()
            if k == 0:
                for copy in loads[2 * count :]:
                    copy.start()
        for copy in loads[2 * count :]:
            copy.wait()

    for k in range(count):

        @pl.when(step == k)
        def _(k=k):
            for copy in (*loads[2 * k : 2 * k + 2], *copies[NY * k : NY * k + NY]):
                copy.wait()
            if k >= 2:
                back[2 * k - 4].wait()
                back[2 * k - 3].wait()

    w = held[step]
    grad = lax.dot_general(cot[...], w, (((1,), (1,)), ((), ())), preferred_element_type=f32)
    first = lax.rem(s_ref[Z] + pick(step, depths), NZ) * NY
    slot = lax.rem(step, 2)
    for k in range(NY):
        at = pl.multiple_of((2 * (first + k) + s_ref[CORE]) * ROWS, ROWS)
        cols = slice(k * ROWS, (k + 1) * ROWS)
        made[slot, :, cols] = (grad[:, cols] * gain_ref[:, pl.ds(at, ROWS)]).astype(bf16)

    for k in range(count):

        @pl.when(step == k)
        def _(k=k):
            back[2 * k].start()
            back[2 * k + 1].start()

    part = jnp.dot(x[step], w, preferred_element_type=f32)

    @pl.when(step == 0)
    def _():
        values[...] = part

    @pl.when((step > 0) & (step < count - 1))
    def _():
        values[...] += part

    @pl.when(step == count - 1)
    def _():
        if count >= 2:
            back[2 * count - 4].wait()
            back[2 * count - 3].wait()
        made[count % 2] = (values[...] + part).astype(bf16)
        for copy in back[2 * count :]:
            copy.start()
        for copy in back[2 * count - 2 :]:
            copy.wait()


def half_call(depths, scalars, x, mine, cots, gain, w, name):
    count = len(depths)
    weights = [w[dz, dy] for dz in depths for dy in range(NY)]
    made = pl.pallas_call(
        functools.partial(half_kernel, depths),
        grid_spec=pltpu.PrefetchScalarGridSpec(
            num_scalar_prefetch=1,
            grid=(count,),
            in_specs=[pl.BlockSpec((1, D), lambda t, s: (0, 0))]
            + [pl.BlockSpec(memory_space=pltpu.HBM)] * (3 + count + len(weights)),
            out_specs=[pl.BlockSpec(memory_space=pltpu.HBM)] * (2 * (count + 1)),
            scratch_shapes=[
                pltpu.VMEM((count, 2 * ROWS, PAIR), bf16),
                pltpu.VMEM((2 * ROWS, KV), bf16),
                pltpu.VMEM((count, PAIR, KV), bf16),
                pltpu.VMEM((2 * ROWS, KV), f32),
                pltpu.VMEM((2, 2 * ROWS, PAIR), bf16),
                pltpu.SemaphoreType.DMA((2 * count + 2,)),
                pltpu.SemaphoreType.DMA((NY * count,)),
                pltpu.SemaphoreType.DMA((2, 2)),
            ],
        ),
        out_shape=[jax.ShapeDtypeStruct((ROWS, PAIR), bf16)] * (2 * (count + 1)),
        compiler_params=params(1),
        cost_estimate=cost(10),
        name=name,
    )(scalars, gain, *cots, *[x[dz] for dz in depths], mine, *weights)
    return made[: count + 1], made[count + 1 :]


def hidden_kernel(depths, s_ref, x_ref, c_ref, inv_ref, *rest):
    count = len(depths)
    owns, gots, tails = rest[:count], rest[count : 2 * count], rest[2 * count : -2]
    values_ref, out_ref = rest[-2:]
    core = s_ref[CORE]
    values = tails[0][...].astype(f32)
    for tail in tails[1:]:
        values = values + tail[...].astype(f32)
    values_ref[...] = values.astype(bf16)
    mean = jnp.sum(values * c_ref[...].astype(f32), axis=1, keepdims=True) / D
    inverse = inv_ref[...]
    mean = jnp.broadcast_to(mean, inverse.shape) * inverse
    for dz, own_ref, got_ref in zip(depths, owns, gots):
        first = lax.rem(s_ref[Z] + dz, NZ) * NY
        for y in range(NY):
            for parity, w_ref in ((core, own_ref), (1 - core, got_ref)):
                at = pl.multiple_of((2 * (first + y) + parity) * ROWS, ROWS)
                x = x_ref[:, pl.ds(at, ROWS)].astype(f32)
                w = w_ref[:, y * ROWS : (y + 1) * ROWS].astype(f32)
                for n in range(ROWS // 128):
                    v = (lanes(w, n) - lanes(x, n) * mean) * inverse
                    out_ref[:, pl.ds(at + n * 128, 128)] = v.astype(bf16)


def hidden_call(depths, scalars, hidden, cot, inverse, owns, gots, tails):
    tile = 128
    wide = pl.BlockSpec((tile, D), lambda t, s: (t, 0))
    row = pl.BlockSpec((tile, KV), lambda t, s: (t, 0))
    return pl.pallas_call(
        functools.partial(hidden_kernel, depths),
        grid_spec=pltpu.PrefetchScalarGridSpec(
            num_scalar_prefetch=1,
            grid=(ROWS // tile,),
            in_specs=[
                wide,
                row,
                pl.BlockSpec((tile, 128), lambda t, s: (t, 0)),
                *[row] * (2 * len(depths) + len(tails)),
            ],
            out_specs=[row, wide],
        ),
        out_shape=[
            jax.ShapeDtypeStruct((ROWS, KV), bf16),
            jax.ShapeDtypeStruct((ROWS, D), bf16),
        ],
        compiler_params=params(1),
        cost_estimate=cost(100),
        name="hidden_grad",
    )(scalars, hidden, cot, inverse, *owns, *gots, *tails)


def update_kernel(rate, s_ref, w_ref, a_ref, b_ref, c_ref, d_ref, total_ref, *rest):
    anchor_ref, momentum_ref, all_ref, out_ref, anchor_out, momentum_out = rest
    grad = a_ref[...].astype(f32) + b_ref[...].astype(f32)
    grad = grad + (c_ref[...].astype(f32) + d_ref[...].astype(f32))
    out_ref[...] = (w_ref[...].astype(f32) - rate * grad).astype(bf16)
    cols = total_ref.shape[1]
    at = pl.ds(pl.multiple_of(s_ref[FRAG] * cols, cols), cols)
    grad = a_ref[:, at].astype(f32) + b_ref[:, at].astype(f32)
    grad = grad + (c_ref[:, at].astype(f32) + d_ref[:, at].astype(f32))
    now = w_ref[:, at].astype(f32) - rate * grad
    out_ref[:, at] = (mix_weight * total_ref[...] + (1.0 - mix_weight) * now).astype(bf16)

    @pl.when(pl.program_id(0) == 0)
    def _():
        anchor_out[...] = anchor_ref[...]
        momentum_out[...] = momentum_ref[...]
        rows = anchor_ref.shape[2]
        frag = s_ref[FRAG]
        a, m = anchor_ref[frag, 0], momentum_ref[frag, 0]
        at = pl.ds(pl.multiple_of(s_ref[REPLICA] * rows, rows), rows)
        kept = (1.0 - by_delta) * a - by_momentum * m
        delta = a - (all_ref[at, :] - kept) / by_delta
        m_new = outer_momentum * m + delta
        momentum_out[frag, 0] = m_new
        anchor_out[frag, 0] = a - outer_rate * (delta + outer_momentum * m_new)


def update_call(rate, scalars, weight, parts, total, anchor, momentum):
    tile = 256
    row = pl.BlockSpec((tile, KV), lambda t, s: (t, 0))
    whole = pl.BlockSpec(anchor.shape, lambda t, s: (0, 0, 0, 0))
    return pl.pallas_call(
        functools.partial(update_kernel, rate),
        grid_spec=pltpu.PrefetchScalarGridSpec(
            num_scalar_prefetch=1,
            grid=(ROWS // tile,),
            in_specs=[
                *[row] * 5,
                pl.BlockSpec((tile, total.shape[1]), lambda t, s: (t, 0)),
                whole,
                whole,
                pl.BlockSpec(total.shape, lambda t, s: (0, 0)),
            ],
            out_specs=[row, whole, whole],
        ),
        out_shape=[
            jax.ShapeDtypeStruct((ROWS, KV), bf16),
            jax.ShapeDtypeStruct(anchor.shape, f32),
            jax.ShapeDtypeStruct(anchor.shape, f32),
        ],
        compiler_params=params(1),
        cost_estimate=cost(3),
        name="update",
    )(scalars, weight, *parts, total, anchor, momentum, total)


by_delta = outer_rate * (1.0 + outer_momentum)
by_momentum = outer_rate * outer_momentum * outer_momentum


def term_kernel(replicas, s_ref, w_ref, a_ref, m_ref, out_ref):
    rows = a_ref.shape[2]
    out_ref[...] = w_ref[...].astype(f32) * (by_delta / replicas)
    at = pl.ds(pl.multiple_of(s_ref[REPLICA] * rows, rows), rows)
    out_ref[at, :] += (1.0 - by_delta) * a_ref[0, 0] - by_momentum * m_ref[0, 0]


def term_call(replicas, scalars, weight, anchor, momentum):
    _, _, rows, cols = anchor.shape
    state = pl.BlockSpec((1, 1, rows, cols), lambda t, s: (s[FRAG], 0, 0, 0))
    return pl.pallas_call(
        functools.partial(term_kernel, replicas),
        grid_spec=pltpu.PrefetchScalarGridSpec(
            num_scalar_prefetch=1,
            grid=(1,),
            in_specs=[pl.BlockSpec((ROWS, cols), lambda t, s: (0, s[FRAG])), state, state],
            out_specs=pl.BlockSpec((ROWS, cols), lambda t, s: (0, 0)),
        ),
        out_shape=jax.ShapeDtypeStruct((ROWS, cols), f32),
        compiler_params=params(1),
        cost_estimate=cost(1),
        name="outer_term",
    )(scalars, weight, anchor, momentum)


def gain_kernel(places, add, s_ref, *rest):
    count = len(places)
    grads, weights, rest = rest[:count], rest[count : 2 * count], rest[2 * count :]
    out_ref = rest[-1]
    rows = grads[0].shape[0]
    ones = jnp.ones((8, KV), bf16)

    @pl.when(pl.program_id(0) == 0)
    def _():
        out_ref[...] = rest[0][...] if add else jnp.zeros(out_ref.shape, f32)

    for k, (dz, dy) in enumerate(places):
        product = (grads[k][...].astype(f32) * weights[k][...].astype(f32)).astype(bf16)
        sums = lax.dot_general(ones, product, (((1,), (1,)), ((), ())), preferred_element_type=f32)
        block = lax.rem(s_ref[Z] + dz, NZ) * NY + lax.rem(s_ref[Y] + dy, NY)
        at = pl.multiple_of(block * ROWS + pl.program_id(0) * rows, rows)
        out_ref[:, pl.ds(at, rows)] = sums[:1]


def gain_call(places, scalars, g, w, before=None):
    tile = 256
    row = pl.BlockSpec((tile, KV), lambda t, s: (t, 0))
    whole = pl.BlockSpec((1, HALF), lambda t, s: (0, 0))
    extra = [] if before is None else [before]
    return pl.pallas_call(
        functools.partial(gain_kernel, places, before is not None),
        grid_spec=pltpu.PrefetchScalarGridSpec(
            num_scalar_prefetch=1,
            grid=(ROWS // tile,),
            in_specs=[row] * (2 * len(places)) + [whole] * len(extra),
            out_specs=whole,
        ),
        out_shape=jax.ShapeDtypeStruct((1, HALF), f32),
        compiler_params=params(1),
        cost_estimate=cost(0),
        name="gain_grad",
    )(scalars, *[g[p] for p in places], *[w[p] for p in places], *extra)


def relay_kernel(a_ref, b_ref, c_ref, d_ref, e_ref, two_ref, three_ref):
    two_ref[...] = (a_ref[...].astype(f32) + b_ref[...].astype(f32)).astype(bf16)
    three = c_ref[...].astype(f32) + d_ref[...].astype(f32) + e_ref[...].astype(f32)
    three_ref[...] = three.astype(bf16)


def relay_call(*terms):
    row = pl.BlockSpec((ROWS // 4, KV), lambda t: (t, 0))
    return pl.pallas_call(
        relay_kernel,
        grid=(4,),
        in_specs=[row] * 5,
        out_specs=[row] * 2,
        out_shape=[jax.ShapeDtypeStruct((ROWS, KV), bf16)] * 2,
        compiler_params=params(1),
        cost_estimate=cost(3),
        name="relay_sums",
    )(*terms)


def after(x, *others):
    return lax.optimization_barrier((x, *others))[0]


def add(*terms):
    total = terms[0].astype(f32)
    for term in terms[1:]:
        total = total + term.astype(f32)
    return total.astype(bf16)


def body(hidden_in, value_cot, proj_weight, norm_gain, anchor, momentum, excluded, fragment):
    inner_rate = 0.01 / ROWS**0.5
    gain_rate = 0.1 / ROWS**0.5
    hidden, weight = hidden_in[0], proj_weight[0]
    here = lax.axis_index("fsdp")
    replica = lax.axis_index("replica")
    z, y, core = here // (NY * NC), (here // NC) % NY, here % NC
    scalars = jnp.stack([z, y, core, here * ROWS, fragment[0], replica]).astype(jnp.int32)

    w = {(0, 0): weight}
    w[1, 0] = shift(weight, -1, 0, 0, "ag_zm")
    w[0, 1] = shift(weight, 0, 1, 0, "ag_y")
    w[3, 0] = shift(weight, 1, 0, 0, "ag_zp")
    near = (w[0, 1], w[1, 0], w[3, 0])
    w[1, 1] = shift(after(w[0, 1], *near), -1, 0, 0, "ag_B")
    w[2, 0] = shift(after(w[3, 0], *near), 1, 0, 0, "ag_A")

    total = term_call(lax.axis_size("replica"), scalars, weight, anchor, momentum)
    first_term = total
    total = total + flip_replica(after(total, w[0, 1]), 1)
    first_sum = total
    total = total + flip_replica(total, 2)
    second_sum = total
    total = total + flip_replica(total, 6)

    mine, *send, inverse = norm_call(
        after(scalars, first_term), hidden, value_cot[0], norm_gain, excluded
    )
    masked = send[-1]
    recv = [shift(v, 0, 0, 1, "swap_x") for v in send]
    recv_cot = recv.pop()

    g = {}

    def make(places, waits, estimate):
        g.update(zip(places, grad_call(places, after(scalars, *waits), mine, recv, recv_cot, estimate)))

    make([(2, 1), (1, 1), (3, 1), (2, 0), (3, 0), (0, 1), (1, 0), (0, 0)], near, 16)
    far = shift(after(g[2, 1], first_sum), 0, 1, 0, "rs_D")
    w[2, 1] = shift(after(w[1, 1], g[2, 0]), -1, 0, 0, "ag_D")
    w[3, 1] = shift(after(w[0, 1], w[2, 0], g[2, 0]), 1, 0, 0, "ag_C")

    near_half, far_half = (0, 1), (3, 2)
    cots = (recv_cot, masked)
    sent0, own0 = half_call(
        near_half, after(scalars, g[0, 0]), recv, mine, cots, norm_gain, w, "half_near"
    )
    got0 = [shift(v, 0, 0, 1, "swap_w0") for v in sent0]
    near_order = [(dz, dy) for dz in near_half for dy in range(NY)]
    far_order = [(dz, dy) for dz in far_half for dy in range(NY)]
    near_sums = gain_call(near_order, after(scalars, sent0[0]), g, w)
    side = shift(after(g[1, 1], near_sums, w[2, 1]), 0, 1, 0, "rs_B")
    left = shift(after(g[3, 1], near_sums, w[2, 1]), -1, 0, 0, "rs_C")
    over = shift(add(g[2, 0], after(far, near_sums)), 1, 0, 0, "rs_A")
    partial = gain_call(far_order, after(scalars, near_sums, second_sum), g, w, near_sums)
    sent1, own1 = half_call(
        far_half, after(scalars, sent0[0], far, partial), recv, mine, cots, norm_gain, w, "half_far"
    )
    got1 = [shift(v, 0, 0, 1, "swap_w1") for v in sent1]

    partial = partial + shift(partial, 0, 1, 0, "gain_y")
    partial = partial + flip_z(after(partial, sent1[0]), 1)
    from_next = shift(after(g[3, 0], left), -1, 0, 0, "rs_zm")
    to_side, to_last = relay_call(g[0, 1], left, g[1, 0], side, over)
    from_side = shift(to_side, 0, 1, 0, "rs_y")
    from_last = shift(to_last, 1, 0, 0, "rs_zp")

    values_out, hidden_grad = hidden_call(
        (*near_half, *far_half), after(scalars, left, side, over), hidden, masked, inverse,
        (*own0[:-1], *own1[:-1]), (*got0[:-1], *got1[:-1]),
        (own0[-1], own1[-1], got0[-1], got1[-1]),
    )

    partial = partial + flip_z(after(partial, to_last), 3)
    other = shift(after(partial, hidden_grad), 0, 0, 1, "gain_c")
    new_weight, anchor_out, momentum_out = update_call(
        inner_rate,
        scalars,
        weight,
        (after(g[0, 0], hidden_grad), from_next, from_side, from_last),
        total,
        anchor,
        momentum,
    )
    other = after(other, new_weight)
    even = jnp.where(core == 0, partial, other).reshape(HALF // ROWS, ROWS)
    odd = jnp.where(core == 0, other, partial).reshape(HALF // ROWS, ROWS)
    gain_grad = jnp.stack([even, odd], axis=1).reshape(1, D) / norm_gain
    new_gain = norm_gain - gain_rate * gain_grad

    return (
        values_out[None],
        hidden_grad[None],
        new_weight[None],
        new_gain,
        anchor_out,
        momentum_out,
    )


def solution(mesh):
    placed = (
        P("replica", "fsdp", None),
        P("replica", "fsdp", None),
        P("replica", "fsdp", None),
        P("replica", None),
        P(None, "fsdp", "replica", None),
        P(None, "fsdp", "replica", None),
        P("replica", None),
        P(),
    )
    return jax.shard_map(
        body,
        mesh=mesh,
        in_specs=placed,
        out_specs=(
            P("replica", "fsdp", None),
            P("replica", "fsdp", None),
            P("replica", "fsdp", None),
            P("replica", None),
            P(None, "fsdp", "replica", None),
            P(None, "fsdp", "replica", None),
        ),
        check_vma=False,
    )
```

```python
import functools

import jax
import jax.numpy as jnp
from jax import lax
from jax.experimental import pallas as pl
from jax.experimental.pallas import tpu as pltpu
from jax.sharding import PartitionSpec as P

outer_momentum = 0.9
outer_rate = 0.7
mix_weight = 0.5

ROWS = 512
D = 8192
KV = 1024
HALF = D // 2
WIDE = HALF + KV
VMEM = 62 * 1024 * 1024
NZ, NY, NC = 4, 2, 2
bf16, f32 = jnp.bfloat16, jnp.float32


def params(n):
    return pltpu.CompilerParams(dimension_semantics=("arbitrary",) * n, vmem_limit_bytes=VMEM)


def cost(microseconds):
    return pl.CostEstimate(flops=0, bytes_accessed=int(microseconds * 3.3e6), transcendentals=0)


def shift(x, dz, dy, dc, name="x"):
    pairs = []
    for z in range(NZ):
        for y in range(NY):
            for c in range(NC):
                to = ((z + dz) % NZ, (y + dy) % NY, (c + dc) % NC)
                pairs.append(((z * NY + y) * NC + c, (to[0] * NY + to[1]) * NC + to[2]))
    with jax.named_scope(name):
        return lax.ppermute(x, "fsdp", pairs)


def flip_z(x, mask):
    pairs = [(i, i ^ (mask * NY * NC)) for i in range(NZ * NY * NC)]
    return lax.ppermute(x, "fsdp", pairs)


def flip_replica(x, mask):
    return lax.ppermute(x, "replica", [(i, i ^ mask) for i in range(8)])


Z, Y, CORE, FIRST, FRAG, REPLICA = range(6)
PAIR = 2 * ROWS


def pick(step, values):
    found = values[-1]
    for k, value in enumerate(values[:-1]):
        found = jnp.where(step == k, value, found)
    return found


def block_of(s, step, places):
    dz, dy = pick(step, [p[0] for p in places]), pick(step, [p[1] for p in places])
    return lax.rem(s[Z] + dz, NZ) * NY + lax.rem(s[Y] + dy, NY)


def pair_of(s, step, depths):
    return lax.rem(s[Z] + pick(step, depths), NZ)


def lanes(v, k):
    return v[:, k * 128 : (k + 1) * 128]


def norm_kernel(s_ref, x_ref, cot_ref, gain_ref, excl_ref, mine_ref, *rest):
    sends, (masked_ref, inv_ref) = rest[:NZ], rest[NZ:]
    core = s_ref[CORE]
    rows = x_ref.shape[0]
    position = s_ref[FIRST] + pl.program_id(0) * rows
    position = position + lax.broadcasted_iota(jnp.int32, (rows, 1), 0)
    hits = jnp.where(position == excl_ref[...], 1.0, 0.0)
    kept = 1.0 - jnp.max(hits, axis=1, keepdims=True)
    masked = (cot_ref[...].astype(f32) * kept).astype(bf16)
    mine_ref[:, HALF:] = masked
    masked_ref[...] = masked
    total = jnp.zeros((rows, 128), f32)
    for b in range(D // 128):
        v = x_ref[:, b * 128 : (b + 1) * 128].astype(f32)
        total = total + v * v
    total = jnp.sum(total, axis=1, keepdims=True)
    inverse = jnp.broadcast_to(lax.rsqrt(total / D + 1e-05), inv_ref.shape)
    inv_ref[...] = inverse

    def scaled(at, out, to):
        x = x_ref[:, pl.ds(at, ROWS)].astype(f32)
        gain = gain_ref[:, pl.ds(at, ROWS)]
        for k in range(ROWS // 128):
            v = lanes(x, k) * inverse * lanes(gain, k)
            out[:, to + k * 128 : to + (k + 1) * 128] = v.astype(bf16)

    for j in range(HALF // ROWS):
        scaled(pl.multiple_of((2 * j + core) * ROWS, ROWS), mine_ref, j * ROWS)
    for dz, send_ref in enumerate(sends):
        first = lax.rem(s_ref[Z] + dz, NZ) * NY
        for y in range(NY):
            at = pl.multiple_of((2 * (first + y) + 1 - core) * ROWS, ROWS)
            scaled(at, send_ref, y * ROWS)


def norm_call(scalars, hidden, cot, gain, excl):
    tile = 128
    return pl.pallas_call(
        norm_kernel,
        grid_spec=pltpu.PrefetchScalarGridSpec(
            num_scalar_prefetch=1,
            grid=(ROWS // tile,),
            in_specs=[
                pl.BlockSpec((tile, D), lambda t, s: (t, 0)),
                pl.BlockSpec((tile, KV), lambda t, s: (t, 0)),
                pl.BlockSpec((1, D), lambda t, s: (0, 0)),
                pl.BlockSpec((1, 1024), lambda t, s: (0, 0)),
            ],
            out_specs=[
                pl.BlockSpec((tile, WIDE), lambda t, s: (t, 0)),
                *[pl.BlockSpec((tile, PAIR), lambda t, s: (t, 0))] * NZ,
                pl.BlockSpec((tile, KV), lambda t, s: (t, 0)),
                pl.BlockSpec((tile, 128), lambda t, s: (t, 0)),
            ],
        ),
        out_shape=[
            jax.ShapeDtypeStruct((ROWS, WIDE), bf16),
            *[jax.ShapeDtypeStruct((ROWS, PAIR), bf16)] * NZ,
            jax.ShapeDtypeStruct((ROWS, KV), bf16),
            jax.ShapeDtypeStruct((ROWS, 128), f32),
        ],
        compiler_params=params(1),
        cost_estimate=cost(8),
        name="norm",
    )(scalars, hidden, cot, gain, excl)


def grad_kernel(places, s_ref, x0_ref, c0_ref, c1_ref, *rest):
    count = len(places)
    x1_refs, outs, (x1, x1_sems, held, sems) = rest[:count], rest[count : 2 * count], rest[2 * count :]
    step = pl.program_id(0)
    dims = (((0,), (0,)), ((), ()))
    loads = []
    for k, (_, dy) in enumerate(places):
        at = pl.multiple_of(lax.rem(s_ref[Y] + dy, NY) * ROWS, ROWS)
        loads.append(
            pltpu.make_async_copy(x1_refs[k].at[:, pl.ds(at, ROWS)], x1.at[k], x1_sems.at[k])
        )
    copies = [pltpu.make_async_copy(held.at[k % 2], outs[k], sems.at[k % 2]) for k in range(count)]

    @pl.when(step == 0)
    def _():
        for load in loads:
            load.start()

    total = lax.dot_general(x0_ref[...], c0_ref[...], dims, preferred_element_type=f32)
    for k in range(count):

        @pl.when(step == k)
        def _(k=k):
            loads[k].wait()

    total = total + lax.dot_general(x1[step], c1_ref[...], dims, preferred_element_type=f32)
    total = total.astype(bf16)
    for k in range(count):

        @pl.when(step == k)
        def _(k=k):
            if k >= 2:
                copies[k - 2].wait()
            held[k % 2] = total
            copies[k].start()
            if k == count - 1:
                for copy in copies[max(k - 1, 0) :]:
                    copy.wait()


def grad_call(places, scalars, mine, recv, recv_cot, estimate):
    count = len(places)
    c = pl.BlockSpec((ROWS, KV), lambda t, s: (0, 0))
    return pl.pallas_call(
        functools.partial(grad_kernel, places),
        grid_spec=pltpu.PrefetchScalarGridSpec(
            num_scalar_prefetch=1,
            grid=(count,),
            in_specs=[
                pl.BlockSpec((ROWS, ROWS), lambda t, s: (0, block_of(s, t, places))),
                pl.BlockSpec((ROWS, KV), lambda t, s: (0, HALF // KV)),
                c,
            ]
            + [pl.BlockSpec(memory_space=pltpu.HBM)] * count,
            out_specs=[pl.BlockSpec(memory_space=pltpu.HBM)] * count,
            scratch_shapes=[
                pltpu.VMEM((count, ROWS, ROWS), bf16),
                pltpu.SemaphoreType.DMA((count,)),
                pltpu.VMEM((2, ROWS, KV), bf16),
                pltpu.SemaphoreType.DMA((2,)),
            ],
        ),
        out_shape=[jax.ShapeDtypeStruct((ROWS, KV), bf16)] * count,
        compiler_params=params(1),
        cost_estimate=cost(estimate),
        name="weight_grad_blocks",
    )(scalars, mine, mine, recv_cot, *[recv[dz] for dz, _ in places])


def weight_copies(depths, s_ref, weights, held, sems):
    copies = []
    for k in range(len(depths)):
        for dy in range(NY):
            at = pl.multiple_of(lax.rem(s_ref[Y] + dy, NY) * ROWS, ROWS)
            n = NY * k + dy
            copies.append(
                pltpu.make_async_copy(weights[n], held.at[k, pl.ds(at, ROWS)], sems.at[n])
            )
    return copies


def half_kernel(depths, s_ref, gain_ref, *rest):
    count = len(depths)
    cots, xs, mine_ref, rest = rest[:2], rest[2 : 2 + count], rest[2 + count], rest[3 + count :]
    weights, outs = rest[: NY * count], rest[NY * count : NY * count + 2 * (count + 1)]
    x, cot, held, values, made, in_sems, sems, out_sems = rest[NY * count + 2 * (count + 1) :]
    step = pl.program_id(0)
    copies = weight_copies(depths, s_ref, weights, held, sems)
    loads = []
    for k, ref in enumerate(xs):
        at = pl.multiple_of(lax.rem(s_ref[Z] + depths[k], NZ) * PAIR, PAIR)
        own = mine_ref.at[:, pl.ds(at, PAIR)]
        for n, source in enumerate((ref, own)):
            to = x.at[k, n * ROWS : (n + 1) * ROWS]
            loads.append(pltpu.make_async_copy(source, to, in_sems.at[2 * k + n]))
    for n, ref in enumerate(cots):
        to = cot.at[n * ROWS : (n + 1) * ROWS]
        loads.append(pltpu.make_async_copy(ref, to, in_sems.at[2 * count + n]))
    back = []
    for k in range(count + 1):
        for n in range(2):
            source = made.at[k % 2, n * ROWS : (n + 1) * ROWS]
            back.append(
                pltpu.make_async_copy(source, outs[n * (count + 1) + k], out_sems.at[k % 2, n])
            )

    @pl.when(step == 0)
    def _():
        for k in range(count):
            for copy in (*loads[2 * k : 2 * k + 2], *copies[NY * k : NY * k + NY]):
                copy.start()
            if k == 0:
                for copy in loads[2 * count :]:
                    copy.start()
        for copy in loads[2 * count :]:
            copy.wait()

    for k in range(count):

        @pl.when(step == k)
        def _(k=k):
            for copy in (*loads[2 * k : 2 * k + 2], *copies[NY * k : NY * k + NY]):
                copy.wait()
            if k >= 2:
                back[2 * k - 4].wait()
                back[2 * k - 3].wait()

    w = held[step]
    grad = lax.dot_general(cot[...], w, (((1,), (1,)), ((), ())), preferred_element_type=f32)
    first = lax.rem(s_ref[Z] + pick(step, depths), NZ) * NY
    slot = lax.rem(step, 2)
    for k in range(NY):
        at = pl.multiple_of((2 * (first + k) + s_ref[CORE]) * ROWS, ROWS)
        cols = slice(k * ROWS, (k + 1) * ROWS)
        made[slot, :, cols] = (grad[:, cols] * gain_ref[:, pl.ds(at, ROWS)]).astype(bf16)

    for k in range(count):

        @pl.when(step == k)
        def _(k=k):
            back[2 * k].start()
            back[2 * k + 1].start()

    part = jnp.dot(x[step], w, preferred_element_type=f32)

    @pl.when(step == 0)
    def _():
        values[...] = part

    @pl.when((step > 0) & (step < count - 1))
    def _():
        values[...] += part

    @pl.when(step == count - 1)
    def _():
        if count >= 2:
            back[2 * count - 4].wait()
            back[2 * count - 3].wait()
        made[count % 2] = (values[...] + part).astype(bf16)
        for copy in back[2 * count :]:
            copy.start()
        for copy in back[2 * count - 2 :]:
            copy.wait()


def half_call(depths, scalars, x, mine, cots, gain, w, name):
    count = len(depths)
    weights = [w[dz, dy] for dz in depths for dy in range(NY)]
    made = pl.pallas_call(
        functools.partial(half_kernel, depths),
        grid_spec=pltpu.PrefetchScalarGridSpec(
            num_scalar_prefetch=1,
            grid=(count,),
            in_specs=[pl.BlockSpec((1, D), lambda t, s: (0, 0))]
            + [pl.BlockSpec(memory_space=pltpu.HBM)] * (3 + count + len(weights)),
            out_specs=[pl.BlockSpec(memory_space=pltpu.HBM)] * (2 * (count + 1)),
            scratch_shapes=[
                pltpu.VMEM((count, 2 * ROWS, PAIR), bf16),
                pltpu.VMEM((2 * ROWS, KV), bf16),
                pltpu.VMEM((count, PAIR, KV), bf16),
                pltpu.VMEM((2 * ROWS, KV), f32),
                pltpu.VMEM((2, 2 * ROWS, PAIR), bf16),
                pltpu.SemaphoreType.DMA((2 * count + 2,)),
                pltpu.SemaphoreType.DMA((NY * count,)),
                pltpu.SemaphoreType.DMA((2, 2)),
            ],
        ),
        out_shape=[jax.ShapeDtypeStruct((ROWS, PAIR), bf16)] * (2 * (count + 1)),
        compiler_params=params(1),
        cost_estimate=cost(10),
        name=name,
    )(scalars, gain, *cots, *[x[dz] for dz in depths], mine, *weights)
    return made[: count + 1], made[count + 1 :]


def hidden_kernel(depths, s_ref, x_ref, c_ref, inv_ref, *rest):
    count = len(depths)
    owns, gots, tails = rest[:count], rest[count : 2 * count], rest[2 * count : -2]
    values_ref, out_ref = rest[-2:]
    core = s_ref[CORE]
    values = tails[0][...].astype(f32)
    for tail in tails[1:]:
        values = values + tail[...].astype(f32)
    values_ref[...] = values.astype(bf16)
    mean = jnp.sum(values * c_ref[...].astype(f32), axis=1, keepdims=True) / D
    inverse = inv_ref[...]
    mean = jnp.broadcast_to(mean, inverse.shape) * inverse
    for dz, own_ref, got_ref in zip(depths, owns, gots):
        first = lax.rem(s_ref[Z] + dz, NZ) * NY
        for y in range(NY):
            for parity, w_ref in ((core, own_ref), (1 - core, got_ref)):
                at = pl.multiple_of((2 * (first + y) + parity) * ROWS, ROWS)
                x = x_ref[:, pl.ds(at, ROWS)].astype(f32)
                w = w_ref[:, y * ROWS : (y + 1) * ROWS].astype(f32)
                for n in range(ROWS // 128):
                    v = (lanes(w, n) - lanes(x, n) * mean) * inverse
                    out_ref[:, pl.ds(at + n * 128, 128)] = v.astype(bf16)


def hidden_call(depths, scalars, hidden, cot, inverse, owns, gots, tails):
    tile = 128
    wide = pl.BlockSpec((tile, D), lambda t, s: (t, 0))
    row = pl.BlockSpec((tile, KV), lambda t, s: (t, 0))
    return pl.pallas_call(
        functools.partial(hidden_kernel, depths),
        grid_spec=pltpu.PrefetchScalarGridSpec(
            num_scalar_prefetch=1,
            grid=(ROWS // tile,),
            in_specs=[
                wide,
                row,
                pl.BlockSpec((tile, 128), lambda t, s: (t, 0)),
                *[row] * (2 * len(depths) + len(tails)),
            ],
            out_specs=[row, wide],
        ),
        out_shape=[
            jax.ShapeDtypeStruct((ROWS, KV), bf16),
            jax.ShapeDtypeStruct((ROWS, D), bf16),
        ],
        compiler_params=params(1),
        cost_estimate=cost(100),
        name="hidden_grad",
    )(scalars, hidden, cot, inverse, *owns, *gots, *tails)


def update_kernel(rate, s_ref, w_ref, a_ref, b_ref, c_ref, d_ref, total_ref, *rest):
    anchor_ref, momentum_ref, all_ref, out_ref, anchor_out, momentum_out = rest
    grad = a_ref[...].astype(f32) + b_ref[...].astype(f32)
    grad = grad + (c_ref[...].astype(f32) + d_ref[...].astype(f32))
    out_ref[...] = (w_ref[...].astype(f32) - rate * grad).astype(bf16)
    cols = total_ref.shape[1]
    at = pl.ds(pl.multiple_of(s_ref[FRAG] * cols, cols), cols)
    grad = a_ref[:, at].astype(f32) + b_ref[:, at].astype(f32)
    grad = grad + (c_ref[:, at].astype(f32) + d_ref[:, at].astype(f32))
    now = w_ref[:, at].astype(f32) - rate * grad
    out_ref[:, at] = (mix_weight * total_ref[...] + (1.0 - mix_weight) * now).astype(bf16)

    @pl.when(pl.program_id(0) == 0)
    def _():
        anchor_out[...] = anchor_ref[...]
        momentum_out[...] = momentum_ref[...]
        rows = anchor_ref.shape[2]
        frag = s_ref[FRAG]
        a, m = anchor_ref[frag, 0], momentum_ref[frag, 0]
        at = pl.ds(pl.multiple_of(s_ref[REPLICA] * rows, rows), rows)
        kept = (1.0 - by_delta) * a - by_momentum * m
        delta = a - (all_ref[at, :] - kept) / by_delta
        m_new = outer_momentum * m + delta
        momentum_out[frag, 0] = m_new
        anchor_out[frag, 0] = a - outer_rate * (delta + outer_momentum * m_new)


def update_call(rate, scalars, weight, parts, total, anchor, momentum):
    tile = 256
    row = pl.BlockSpec((tile, KV), lambda t, s: (t, 0))
    whole = pl.BlockSpec(anchor.shape, lambda t, s: (0, 0, 0, 0))
    return pl.pallas_call(
        functools.partial(update_kernel, rate),
        grid_spec=pltpu.PrefetchScalarGridSpec(
            num_scalar_prefetch=1,
            grid=(ROWS // tile,),
            in_specs=[
                *[row] * 5,
                pl.BlockSpec((tile, total.shape[1]), lambda t, s: (t, 0)),
                whole,
                whole,
                pl.BlockSpec(total.shape, lambda t, s: (0, 0)),
            ],
            out_specs=[row, whole, whole],
        ),
        out_shape=[
            jax.ShapeDtypeStruct((ROWS, KV), bf16),
            jax.ShapeDtypeStruct(anchor.shape, f32),
            jax.ShapeDtypeStruct(anchor.shape, f32),
        ],
        compiler_params=params(1),
        cost_estimate=cost(3),
        name="update",
    )(scalars, weight, *parts, total, anchor, momentum, total)


by_delta = outer_rate * (1.0 + outer_momentum)
by_momentum = outer_rate * outer_momentum * outer_momentum


def term_kernel(replicas, s_ref, w_ref, a_ref, m_ref, out_ref):
    rows = a_ref.shape[2]
    out_ref[...] = w_ref[...].astype(f32) * (by_delta / replicas)
    at = pl.ds(pl.multiple_of(s_ref[REPLICA] * rows, rows), rows)
    out_ref[at, :] += (1.0 - by_delta) * a_ref[0, 0] - by_momentum * m_ref[0, 0]


def term_call(replicas, scalars, weight, anchor, momentum):
    _, _, rows, cols = anchor.shape
    state = pl.BlockSpec((1, 1, rows, cols), lambda t, s: (s[FRAG], 0, 0, 0))
    return pl.pallas_call(
        functools.partial(term_kernel, replicas),
        grid_spec=pltpu.PrefetchScalarGridSpec(
            num_scalar_prefetch=1,
            grid=(1,),
            in_specs=[pl.BlockSpec((ROWS, cols), lambda t, s: (0, s[FRAG])), state, state],
            out_specs=pl.BlockSpec((ROWS, cols), lambda t, s: (0, 0)),
        ),
        out_shape=jax.ShapeDtypeStruct((ROWS, cols), f32),
        compiler_params=params(1),
        cost_estimate=cost(1),
        name="outer_term",
    )(scalars, weight, anchor, momentum)


def gain_kernel(places, add, s_ref, *rest):
    count = len(places)
    grads, weights, rest = rest[:count], rest[count : 2 * count], rest[2 * count :]
    out_ref = rest[-1]
    rows = grads[0].shape[0]
    ones = jnp.ones((8, KV), bf16)

    @pl.when(pl.program_id(0) == 0)
    def _():
        out_ref[...] = rest[0][...] if add else jnp.zeros(out_ref.shape, f32)

    for k, (dz, dy) in enumerate(places):
        product = (grads[k][...].astype(f32) * weights[k][...].astype(f32)).astype(bf16)
        sums = lax.dot_general(ones, product, (((1,), (1,)), ((), ())), preferred_element_type=f32)
        block = lax.rem(s_ref[Z] + dz, NZ) * NY + lax.rem(s_ref[Y] + dy, NY)
        at = pl.multiple_of(block * ROWS + pl.program_id(0) * rows, rows)
        out_ref[:, pl.ds(at, rows)] = sums[:1]


def gain_call(places, scalars, g, w, before=None):
    tile = 256
    row = pl.BlockSpec((tile, KV), lambda t, s: (t, 0))
    whole = pl.BlockSpec((1, HALF), lambda t, s: (0, 0))
    extra = [] if before is None else [before]
    return pl.pallas_call(
        functools.partial(gain_kernel, places, before is not None),
        grid_spec=pltpu.PrefetchScalarGridSpec(
            num_scalar_prefetch=1,
            grid=(ROWS // tile,),
            in_specs=[row] * (2 * len(places)) + [whole] * len(extra),
            out_specs=whole,
        ),
        out_shape=jax.ShapeDtypeStruct((1, HALF), f32),
        compiler_params=params(1),
        cost_estimate=cost(0),
        name="gain_grad",
    )(scalars, *[g[p] for p in places], *[w[p] for p in places], *extra)


def relay_kernel(a_ref, b_ref, c_ref, d_ref, e_ref, two_ref, three_ref):
    two_ref[...] = (a_ref[...].astype(f32) + b_ref[...].astype(f32)).astype(bf16)
    three = c_ref[...].astype(f32) + d_ref[...].astype(f32) + e_ref[...].astype(f32)
    three_ref[...] = three.astype(bf16)


def relay_call(*terms):
    row = pl.BlockSpec((ROWS // 4, KV), lambda t: (t, 0))
    return pl.pallas_call(
        relay_kernel,
        grid=(4,),
        in_specs=[row] * 5,
        out_specs=[row] * 2,
        out_shape=[jax.ShapeDtypeStruct((ROWS, KV), bf16)] * 2,
        compiler_params=params(1),
        cost_estimate=cost(3),
        name="relay_sums",
    )(*terms)


def after(x, *others):
    return lax.optimization_barrier((x, *others))[0]


def add(*terms):
    total = terms[0].astype(f32)
    for term in terms[1:]:
        total = total + term.astype(f32)
    return total.astype(bf16)


def body(hidden_in, value_cot, proj_weight, norm_gain, anchor, momentum, excluded, fragment):
    inner_rate = 0.01 / ROWS**0.5
    gain_rate = 0.1 / ROWS**0.5
    hidden, weight = hidden_in[0], proj_weight[0]
    here = lax.axis_index("fsdp")
    replica = lax.axis_index("replica")
    z, y, core = here // (NY * NC), (here // NC) % NY, here % NC
    scalars = jnp.stack([z, y, core, here * ROWS, fragment[0], replica]).astype(jnp.int32)

    w = {(0, 0): weight}
    w[1, 0] = shift(weight, -1, 0, 0, "ag_zm")
    w[0, 1] = shift(weight, 0, 1, 0, "ag_y")
    w[3, 0] = shift(weight, 1, 0, 0, "ag_zp")
    near = (w[0, 1], w[1, 0], w[3, 0])
    w[1, 1] = shift(after(w[0, 1], *near), -1, 0, 0, "ag_B")
    w[2, 0] = shift(after(w[3, 0], *near), 1, 0, 0, "ag_A")

    total = term_call(lax.axis_size("replica"), scalars, weight, anchor, momentum)
    first_term = total
    total = total + flip_replica(after(total, w[0, 1]), 1)
    first_sum = total
    total = total + flip_replica(total, 2)
    second_sum = total
    total = total + flip_replica(total, 6)

    mine, *send, inverse = norm_call(
        after(scalars, first_term), hidden, value_cot[0], norm_gain, excluded
    )
    masked = send[-1]
    recv = [shift(v, 0, 0, 1, "swap_x") for v in send]
    recv_cot = recv.pop()

    g = {}

    def make(places, waits, estimate):
        g.update(zip(places, grad_call(places, after(scalars, *waits), mine, recv, recv_cot, estimate)))

    make([(2, 1), (1, 1), (3, 1), (2, 0), (3, 0), (0, 1), (1, 0), (0, 0)], near, 16)
    far = shift(after(g[2, 1], first_sum), 0, 1, 0, "rs_D")
    w[2, 1] = shift(after(w[1, 1], g[2, 0]), -1, 0, 0, "ag_D")
    w[3, 1] = shift(after(w[0, 1], w[2, 0], g[2, 0]), 1, 0, 0, "ag_C")

    near_half, far_half = (0, 1), (3, 2)
    cots = (recv_cot, masked)
    sent0, own0 = half_call(
        near_half, after(scalars, g[0, 0]), recv, mine, cots, norm_gain, w, "half_near"
    )
    got0 = [shift(v, 0, 0, 1, "swap_w0") for v in sent0]
    near_order = [(dz, dy) for dz in near_half for dy in range(NY)]
    far_order = [(dz, dy) for dz in far_half for dy in range(NY)]
    near_sums = gain_call(near_order, after(scalars, sent0[0], second_sum), g, w)
    side = shift(after(g[1, 1], near_sums, w[2, 1]), 0, 1, 0, "rs_B")
    left = shift(after(g[3, 1], near_sums, w[2, 1]), -1, 0, 0, "rs_C")
    over = shift(add(g[2, 0], after(far, near_sums)), 1, 0, 0, "rs_A")
    partial = gain_call(far_order, after(scalars, near_sums), g, w, near_sums)
    sent1, own1 = half_call(
        far_half, after(scalars, sent0[0], far, partial), recv, mine, cots, norm_gain, w, "half_far"
    )
    got1 = [shift(v, 0, 0, 1, "swap_w1") for v in sent1]

    partial = partial + shift(partial, 0, 1, 0, "gain_y")
    partial = partial + flip_z(after(partial, sent1[0]), 1)
    from_next = shift(after(g[3, 0], left), -1, 0, 0, "rs_zm")
    to_side, to_last = relay_call(g[0, 1], left, g[1, 0], side, over)
    from_side = shift(to_side, 0, 1, 0, "rs_y")
    from_last = shift(to_last, 1, 0, 0, "rs_zp")

    values_out, hidden_grad = hidden_call(
        (*near_half, *far_half), after(scalars, left, side, over), hidden, masked, inverse,
        (*own0[:-1], *own1[:-1]), (*got0[:-1], *got1[:-1]),
        (own0[-1], own1[-1], got0[-1], got1[-1]),
    )

    partial = partial + flip_z(after(partial, to_last), 3)
    other = shift(after(partial, hidden_grad), 0, 0, 1, "gain_c")
    new_weight, anchor_out, momentum_out = update_call(
        inner_rate,
        scalars,
        weight,
        (after(g[0, 0], hidden_grad), from_next, from_side, from_last),
        total,
        anchor,
        momentum,
    )
    other = after(other, new_weight)
    even = jnp.where(core == 0, partial, other).reshape(HALF // ROWS, ROWS)
    odd = jnp.where(core == 0, other, partial).reshape(HALF // ROWS, ROWS)
    gain_grad = jnp.stack([even, odd], axis=1).reshape(1, D) / norm_gain
    new_gain = norm_gain - gain_rate * gain_grad

    return (
        values_out[None],
        hidden_grad[None],
        new_weight[None],
        new_gain,
        anchor_out,
        momentum_out,
    )


def solution(mesh):
    placed = (
        P("replica", "fsdp", None),
        P("replica", "fsdp", None),
        P("replica", "fsdp", None),
        P("replica", None),
        P(None, "fsdp", "replica", None),
        P(None, "fsdp", "replica", None),
        P("replica", None),
        P(),
    )
    return jax.shard_map(
        body,
        mesh=mesh,
        in_specs=placed,
        out_specs=(
            P("replica", "fsdp", None),
            P("replica", "fsdp", None),
            P("replica", "fsdp", None),
            P("replica", None),
            P(None, "fsdp", "replica", None),
            P(None, "fsdp", "replica", None),
        ),
        check_vma=False,
    )
```

```python
import functools

import jax
import jax.numpy as jnp
from jax import lax
from jax.experimental import pallas as pl
from jax.experimental.pallas import tpu as pltpu
from jax.sharding import PartitionSpec as P

outer_momentum = 0.9
outer_rate = 0.7
mix_weight = 0.5

ROWS = 512
D = 8192
KV = 1024
HALF = D // 2
WIDE = HALF + KV
VMEM = 62 * 1024 * 1024
NZ, NY, NC = 4, 2, 2
bf16, f32 = jnp.bfloat16, jnp.float32


def params(n):
    return pltpu.CompilerParams(dimension_semantics=("arbitrary",) * n, vmem_limit_bytes=VMEM)


def cost(microseconds):
    return pl.CostEstimate(flops=0, bytes_accessed=int(microseconds * 3.3e6), transcendentals=0)


def shift(x, dz, dy, dc, name="x"):
    pairs = []
    for z in range(NZ):
        for y in range(NY):
            for c in range(NC):
                to = ((z + dz) % NZ, (y + dy) % NY, (c + dc) % NC)
                pairs.append(((z * NY + y) * NC + c, (to[0] * NY + to[1]) * NC + to[2]))
    with jax.named_scope(name):
        return lax.ppermute(x, "fsdp", pairs)


def flip_z(x, mask):
    pairs = [(i, i ^ (mask * NY * NC)) for i in range(NZ * NY * NC)]
    return lax.ppermute(x, "fsdp", pairs)


def flip_replica(x, mask):
    return lax.ppermute(x, "replica", [(i, i ^ mask) for i in range(8)])


Z, Y, CORE, FIRST, FRAG, REPLICA = range(6)
PAIR = 2 * ROWS


def pick(step, values):
    found = values[-1]
    for k, value in enumerate(values[:-1]):
        found = jnp.where(step == k, value, found)
    return found


def block_of(s, step, places):
    dz, dy = pick(step, [p[0] for p in places]), pick(step, [p[1] for p in places])
    return lax.rem(s[Z] + dz, NZ) * NY + lax.rem(s[Y] + dy, NY)


def pair_of(s, step, depths):
    return lax.rem(s[Z] + pick(step, depths), NZ)


def lanes(v, k):
    return v[:, k * 128 : (k + 1) * 128]


def norm_kernel(s_ref, x_ref, cot_ref, gain_ref, excl_ref, mine_ref, *rest):
    sends, (masked_ref, inv_ref) = rest[:NZ], rest[NZ:]
    core = s_ref[CORE]
    rows = x_ref.shape[0]
    position = s_ref[FIRST] + pl.program_id(0) * rows
    position = position + lax.broadcasted_iota(jnp.int32, (rows, 1), 0)
    hits = jnp.where(position == excl_ref[...], 1.0, 0.0)
    kept = 1.0 - jnp.max(hits, axis=1, keepdims=True)
    masked = (cot_ref[...].astype(f32) * kept).astype(bf16)
    mine_ref[:, HALF:] = masked
    masked_ref[...] = masked
    total = jnp.zeros((rows, 128), f32)
    for b in range(D // 128):
        v = x_ref[:, b * 128 : (b + 1) * 128].astype(f32)
        total = total + v * v
    total = jnp.sum(total, axis=1, keepdims=True)
    inverse = jnp.broadcast_to(lax.rsqrt(total / D + 1e-05), inv_ref.shape)
    inv_ref[...] = inverse

    def scaled(at, out, to):
        x = x_ref[:, pl.ds(at, ROWS)].astype(f32)
        gain = gain_ref[:, pl.ds(at, ROWS)]
        for k in range(ROWS // 128):
            v = lanes(x, k) * inverse * lanes(gain, k)
            out[:, to + k * 128 : to + (k + 1) * 128] = v.astype(bf16)

    for j in range(HALF // ROWS):
        scaled(pl.multiple_of((2 * j + core) * ROWS, ROWS), mine_ref, j * ROWS)
    for dz, send_ref in enumerate(sends):
        first = lax.rem(s_ref[Z] + dz, NZ) * NY
        for y in range(NY):
            at = pl.multiple_of((2 * (first + y) + 1 - core) * ROWS, ROWS)
            scaled(at, send_ref, y * ROWS)


def norm_call(scalars, hidden, cot, gain, excl):
    tile = 128
    return pl.pallas_call(
        norm_kernel,
        grid_spec=pltpu.PrefetchScalarGridSpec(
            num_scalar_prefetch=1,
            grid=(ROWS // tile,),
            in_specs=[
                pl.BlockSpec((tile, D), lambda t, s: (t, 0)),
                pl.BlockSpec((tile, KV), lambda t, s: (t, 0)),
                pl.BlockSpec((1, D), lambda t, s: (0, 0)),
                pl.BlockSpec((1, 1024), lambda t, s: (0, 0)),
            ],
            out_specs=[
                pl.BlockSpec((tile, WIDE), lambda t, s: (t, 0)),
                *[pl.BlockSpec((tile, PAIR), lambda t, s: (t, 0))] * NZ,
                pl.BlockSpec((tile, KV), lambda t, s: (t, 0)),
                pl.BlockSpec((tile, 128), lambda t, s: (t, 0)),
            ],
        ),
        out_shape=[
            jax.ShapeDtypeStruct((ROWS, WIDE), bf16),
            *[jax.ShapeDtypeStruct((ROWS, PAIR), bf16)] * NZ,
            jax.ShapeDtypeStruct((ROWS, KV), bf16),
            jax.ShapeDtypeStruct((ROWS, 128), f32),
        ],
        compiler_params=params(1),
        cost_estimate=cost(8),
        name="norm",
    )(scalars, hidden, cot, gain, excl)


def grad_kernel(places, s_ref, x0_ref, c0_ref, c1_ref, *rest):
    count = len(places)
    x1_refs, outs, (x1, x1_sems, held, sems) = rest[:count], rest[count : 2 * count], rest[2 * count :]
    step = pl.program_id(0)
    dims = (((0,), (0,)), ((), ()))
    loads = []
    for k, (_, dy) in enumerate(places):
        at = pl.multiple_of(lax.rem(s_ref[Y] + dy, NY) * ROWS, ROWS)
        loads.append(
            pltpu.make_async_copy(x1_refs[k].at[:, pl.ds(at, ROWS)], x1.at[k], x1_sems.at[k])
        )
    copies = [pltpu.make_async_copy(held.at[k % 2], outs[k], sems.at[k % 2]) for k in range(count)]

    @pl.when(step == 0)
    def _():
        for load in loads:
            load.start()

    total = lax.dot_general(x0_ref[...], c0_ref[...], dims, preferred_element_type=f32)
    for k in range(count):

        @pl.when(step == k)
        def _(k=k):
            loads[k].wait()

    total = total + lax.dot_general(x1[step], c1_ref[...], dims, preferred_element_type=f32)
    total = total.astype(bf16)
    for k in range(count):

        @pl.when(step == k)
        def _(k=k):
            if k >= 2:
                copies[k - 2].wait()
            held[k % 2] = total
            copies[k].start()
            if k == count - 1:
                for copy in copies[max(k - 1, 0) :]:
                    copy.wait()


def grad_call(places, scalars, mine, recv, recv_cot, estimate):
    count = len(places)
    c = pl.BlockSpec((ROWS, KV), lambda t, s: (0, 0))
    return pl.pallas_call(
        functools.partial(grad_kernel, places),
        grid_spec=pltpu.PrefetchScalarGridSpec(
            num_scalar_prefetch=1,
            grid=(count,),
            in_specs=[
                pl.BlockSpec((ROWS, ROWS), lambda t, s: (0, block_of(s, t, places))),
                pl.BlockSpec((ROWS, KV), lambda t, s: (0, HALF // KV)),
                c,
            ]
            + [pl.BlockSpec(memory_space=pltpu.HBM)] * count,
            out_specs=[pl.BlockSpec(memory_space=pltpu.HBM)] * count,
            scratch_shapes=[
                pltpu.VMEM((count, ROWS, ROWS), bf16),
                pltpu.SemaphoreType.DMA((count,)),
                pltpu.VMEM((2, ROWS, KV), bf16),
                pltpu.SemaphoreType.DMA((2,)),
            ],
        ),
        out_shape=[jax.ShapeDtypeStruct((ROWS, KV), bf16)] * count,
        compiler_params=params(1),
        cost_estimate=cost(estimate),
        name="weight_grad_blocks",
    )(scalars, mine, mine, recv_cot, *[recv[dz] for dz, _ in places])


def weight_copies(depths, s_ref, weights, held, sems):
    copies = []
    for k in range(len(depths)):
        for dy in range(NY):
            at = pl.multiple_of(lax.rem(s_ref[Y] + dy, NY) * ROWS, ROWS)
            n = NY * k + dy
            copies.append(
                pltpu.make_async_copy(weights[n], held.at[k, pl.ds(at, ROWS)], sems.at[n])
            )
    return copies


def half_kernel(depths, s_ref, gain_ref, *rest):
    count = len(depths)
    cots, xs, mine_ref, rest = rest[:2], rest[2 : 2 + count], rest[2 + count], rest[3 + count :]
    weights, outs = rest[: NY * count], rest[NY * count : NY * count + 2 * (count + 1)]
    x, cot, held, values, made, in_sems, sems, out_sems = rest[NY * count + 2 * (count + 1) :]
    step = pl.program_id(0)
    copies = weight_copies(depths, s_ref, weights, held, sems)
    loads = []
    for k, ref in enumerate(xs):
        at = pl.multiple_of(lax.rem(s_ref[Z] + depths[k], NZ) * PAIR, PAIR)
        own = mine_ref.at[:, pl.ds(at, PAIR)]
        for n, source in enumerate((ref, own)):
            to = x.at[k, n * ROWS : (n + 1) * ROWS]
            loads.append(pltpu.make_async_copy(source, to, in_sems.at[2 * k + n]))
    for n, ref in enumerate(cots):
        to = cot.at[n * ROWS : (n + 1) * ROWS]
        loads.append(pltpu.make_async_copy(ref, to, in_sems.at[2 * count + n]))
    back = []
    for k in range(count + 1):
        for n in range(2):
            source = made.at[k % 2, n * ROWS : (n + 1) * ROWS]
            back.append(
                pltpu.make_async_copy(source, outs[n * (count + 1) + k], out_sems.at[k % 2, n])
            )

    @pl.when(step == 0)
    def _():
        for k in range(count):
            for copy in (*loads[2 * k : 2 * k + 2], *copies[NY * k : NY * k + NY]):
                copy.start()
            if k == 0:
                for copy in loads[2 * count :]:
                    copy.start()
        for copy in loads[2 * count :]:
            copy.wait()

    for k in range(count):

        @pl.when(step == k)
        def _(k=k):
            for copy in (*loads[2 * k : 2 * k + 2], *copies[NY * k : NY * k + NY]):
                copy.wait()
            if k >= 2:
                back[2 * k - 4].wait()
                back[2 * k - 3].wait()

    w = held[step]
    grad = lax.dot_general(cot[...], w, (((1,), (1,)), ((), ())), preferred_element_type=f32)
    first = lax.rem(s_ref[Z] + pick(step, depths), NZ) * NY
    slot = lax.rem(step, 2)
    for k in range(NY):
        at = pl.multiple_of((2 * (first + k) + s_ref[CORE]) * ROWS, ROWS)
        cols = slice(k * ROWS, (k + 1) * ROWS)
        made[slot, :, cols] = (grad[:, cols] * gain_ref[:, pl.ds(at, ROWS)]).astype(bf16)

    for k in range(count):

        @pl.when(step == k)
        def _(k=k):
            back[2 * k].start()
            back[2 * k + 1].start()

    part = jnp.dot(x[step], w, preferred_element_type=f32)

    @pl.when(step == 0)
    def _():
        values[...] = part

    @pl.when((step > 0) & (step < count - 1))
    def _():
        values[...] += part

    @pl.when(step == count - 1)
    def _():
        if count >= 2:
            back[2 * count - 4].wait()
            back[2 * count - 3].wait()
        made[count % 2] = (values[...] + part).astype(bf16)
        for copy in back[2 * count :]:
            copy.start()
        for copy in back[2 * count - 2 :]:
            copy.wait()


def half_call(depths, scalars, x, mine, cots, gain, w, name):
    count = len(depths)
    weights = [w[dz, dy] for dz in depths for dy in range(NY)]
    made = pl.pallas_call(
        functools.partial(half_kernel, depths),
        grid_spec=pltpu.PrefetchScalarGridSpec(
            num_scalar_prefetch=1,
            grid=(count,),
            in_specs=[pl.BlockSpec((1, D), lambda t, s: (0, 0))]
            + [pl.BlockSpec(memory_space=pltpu.HBM)] * (3 + count + len(weights)),
            out_specs=[pl.BlockSpec(memory_space=pltpu.HBM)] * (2 * (count + 1)),
            scratch_shapes=[
                pltpu.VMEM((count, 2 * ROWS, PAIR), bf16),
                pltpu.VMEM((2 * ROWS, KV), bf16),
                pltpu.VMEM((count, PAIR, KV), bf16),
                pltpu.VMEM((2 * ROWS, KV), f32),
                pltpu.VMEM((2, 2 * ROWS, PAIR), bf16),
                pltpu.SemaphoreType.DMA((2 * count + 2,)),
                pltpu.SemaphoreType.DMA((NY * count,)),
                pltpu.SemaphoreType.DMA((2, 2)),
            ],
        ),
        out_shape=[jax.ShapeDtypeStruct((ROWS, PAIR), bf16)] * (2 * (count + 1)),
        compiler_params=params(1),
        cost_estimate=cost(10),
        name=name,
    )(scalars, gain, *cots, *[x[dz] for dz in depths], mine, *weights)
    return made[: count + 1], made[count + 1 :]


def hidden_kernel(depths, s_ref, x_ref, c_ref, inv_ref, *rest):
    count = len(depths)
    owns, gots, tails = rest[:count], rest[count : 2 * count], rest[2 * count : -2]
    values_ref, out_ref = rest[-2:]
    core = s_ref[CORE]
    values = tails[0][...].astype(f32)
    for tail in tails[1:]:
        values = values + tail[...].astype(f32)
    values_ref[...] = values.astype(bf16)
    mean = jnp.sum(values * c_ref[...].astype(f32), axis=1, keepdims=True) / D
    inverse = inv_ref[...]
    mean = jnp.broadcast_to(mean, inverse.shape) * inverse
    for dz, own_ref, got_ref in zip(depths, owns, gots):
        first = lax.rem(s_ref[Z] + dz, NZ) * NY
        for y in range(NY):
            for parity, w_ref in ((core, own_ref), (1 - core, got_ref)):
                at = pl.multiple_of((2 * (first + y) + parity) * ROWS, ROWS)
                x = x_ref[:, pl.ds(at, ROWS)].astype(f32)
                w = w_ref[:, y * ROWS : (y + 1) * ROWS].astype(f32)
                for n in range(ROWS // 128):
                    v = (lanes(w, n) - lanes(x, n) * mean) * inverse
                    out_ref[:, pl.ds(at + n * 128, 128)] = v.astype(bf16)


def hidden_call(depths, scalars, hidden, cot, inverse, owns, gots, tails):
    tile = 128
    wide = pl.BlockSpec((tile, D), lambda t, s: (t, 0))
    row = pl.BlockSpec((tile, KV), lambda t, s: (t, 0))
    return pl.pallas_call(
        functools.partial(hidden_kernel, depths),
        grid_spec=pltpu.PrefetchScalarGridSpec(
            num_scalar_prefetch=1,
            grid=(ROWS // tile,),
            in_specs=[
                wide,
                row,
                pl.BlockSpec((tile, 128), lambda t, s: (t, 0)),
                *[row] * (2 * len(depths) + len(tails)),
            ],
            out_specs=[row, wide],
        ),
        out_shape=[
            jax.ShapeDtypeStruct((ROWS, KV), bf16),
            jax.ShapeDtypeStruct((ROWS, D), bf16),
        ],
        compiler_params=params(1),
        cost_estimate=cost(100),
        name="hidden_grad",
    )(scalars, hidden, cot, inverse, *owns, *gots, *tails)


def update_kernel(rate, s_ref, w_ref, a_ref, b_ref, c_ref, d_ref, total_ref, *rest):
    anchor_ref, momentum_ref, all_ref, out_ref, anchor_out, momentum_out = rest
    grad = a_ref[...].astype(f32) + b_ref[...].astype(f32)
    grad = grad + (c_ref[...].astype(f32) + d_ref[...].astype(f32))
    out_ref[...] = (w_ref[...].astype(f32) - rate * grad).astype(bf16)
    cols = total_ref.shape[1]
    at = pl.ds(pl.multiple_of(s_ref[FRAG] * cols, cols), cols)
    grad = a_ref[:, at].astype(f32) + b_ref[:, at].astype(f32)
    grad = grad + (c_ref[:, at].astype(f32) + d_ref[:, at].astype(f32))
    now = w_ref[:, at].astype(f32) - rate * grad
    out_ref[:, at] = (mix_weight * total_ref[...] + (1.0 - mix_weight) * now).astype(bf16)

    @pl.when(pl.program_id(0) == 0)
    def _():
        anchor_out[...] = anchor_ref[...]
        momentum_out[...] = momentum_ref[...]
        rows = anchor_ref.shape[2]
        frag = s_ref[FRAG]
        a, m = anchor_ref[frag, 0], momentum_ref[frag, 0]
        at = pl.ds(pl.multiple_of(s_ref[REPLICA] * rows, rows), rows)
        kept = (1.0 - by_delta) * a - by_momentum * m
        delta = a - (all_ref[at, :] - kept) / by_delta
        m_new = outer_momentum * m + delta
        momentum_out[frag, 0] = m_new
        anchor_out[frag, 0] = a - outer_rate * (delta + outer_momentum * m_new)


def update_call(rate, scalars, weight, parts, total, anchor, momentum):
    tile = 256
    row = pl.BlockSpec((tile, KV), lambda t, s: (t, 0))
    whole = pl.BlockSpec(anchor.shape, lambda t, s: (0, 0, 0, 0))
    return pl.pallas_call(
        functools.partial(update_kernel, rate),
        grid_spec=pltpu.PrefetchScalarGridSpec(
            num_scalar_prefetch=1,
            grid=(ROWS // tile,),
            in_specs=[
                *[row] * 5,
                pl.BlockSpec((tile, total.shape[1]), lambda t, s: (t, 0)),
                whole,
                whole,
                pl.BlockSpec(total.shape, lambda t, s: (0, 0)),
            ],
            out_specs=[row, whole, whole],
        ),
        out_shape=[
            jax.ShapeDtypeStruct((ROWS, KV), bf16),
            jax.ShapeDtypeStruct(anchor.shape, f32),
            jax.ShapeDtypeStruct(anchor.shape, f32),
        ],
        compiler_params=params(1),
        cost_estimate=cost(3),
        name="update",
    )(scalars, weight, *parts, total, anchor, momentum, total)


by_delta = outer_rate * (1.0 + outer_momentum)
by_momentum = outer_rate * outer_momentum * outer_momentum


def term_kernel(replicas, s_ref, w_ref, a_ref, m_ref, out_ref):
    rows = a_ref.shape[2]
    out_ref[...] = w_ref[...].astype(f32) * (by_delta / replicas)
    at = pl.ds(pl.multiple_of(s_ref[REPLICA] * rows, rows), rows)
    out_ref[at, :] += (1.0 - by_delta) * a_ref[0, 0] - by_momentum * m_ref[0, 0]


def term_call(replicas, scalars, weight, anchor, momentum):
    _, _, rows, cols = anchor.shape
    state = pl.BlockSpec((1, 1, rows, cols), lambda t, s: (s[FRAG], 0, 0, 0))
    return pl.pallas_call(
        functools.partial(term_kernel, replicas),
        grid_spec=pltpu.PrefetchScalarGridSpec(
            num_scalar_prefetch=1,
            grid=(1,),
            in_specs=[pl.BlockSpec((ROWS, cols), lambda t, s: (0, s[FRAG])), state, state],
            out_specs=pl.BlockSpec((ROWS, cols), lambda t, s: (0, 0)),
        ),
        out_shape=jax.ShapeDtypeStruct((ROWS, cols), f32),
        compiler_params=params(1),
        cost_estimate=cost(1),
        name="outer_term",
    )(scalars, weight, anchor, momentum)


def gain_kernel(places, add, s_ref, *rest):
    count = len(places)
    grads, weights, rest = rest[:count], rest[count : 2 * count], rest[2 * count :]
    out_ref = rest[-1]
    rows = grads[0].shape[0]
    ones = jnp.ones((8, KV), bf16)

    @pl.when(pl.program_id(0) == 0)
    def _():
        out_ref[...] = rest[0][...] if add else jnp.zeros(out_ref.shape, f32)

    for k, (dz, dy) in enumerate(places):
        product = (grads[k][...].astype(f32) * weights[k][...].astype(f32)).astype(bf16)
        sums = lax.dot_general(ones, product, (((1,), (1,)), ((), ())), preferred_element_type=f32)
        block = lax.rem(s_ref[Z] + dz, NZ) * NY + lax.rem(s_ref[Y] + dy, NY)
        at = pl.multiple_of(block * ROWS + pl.program_id(0) * rows, rows)
        out_ref[:, pl.ds(at, rows)] = sums[:1]


def gain_call(places, scalars, g, w, before=None):
    tile = 256
    row = pl.BlockSpec((tile, KV), lambda t, s: (t, 0))
    whole = pl.BlockSpec((1, HALF), lambda t, s: (0, 0))
    extra = [] if before is None else [before]
    return pl.pallas_call(
        functools.partial(gain_kernel, places, before is not None),
        grid_spec=pltpu.PrefetchScalarGridSpec(
            num_scalar_prefetch=1,
            grid=(ROWS // tile,),
            in_specs=[row] * (2 * len(places)) + [whole] * len(extra),
            out_specs=whole,
        ),
        out_shape=jax.ShapeDtypeStruct((1, HALF), f32),
        compiler_params=params(1),
        cost_estimate=cost(0),
        name="gain_grad",
    )(scalars, *[g[p] for p in places], *[w[p] for p in places], *extra)


def relay_kernel(a_ref, b_ref, c_ref, d_ref, e_ref, two_ref, three_ref):
    two_ref[...] = (a_ref[...].astype(f32) + b_ref[...].astype(f32)).astype(bf16)
    three = c_ref[...].astype(f32) + d_ref[...].astype(f32) + e_ref[...].astype(f32)
    three_ref[...] = three.astype(bf16)


def relay_call(*terms):
    row = pl.BlockSpec((ROWS // 4, KV), lambda t: (t, 0))
    return pl.pallas_call(
        relay_kernel,
        grid=(4,),
        in_specs=[row] * 5,
        out_specs=[row] * 2,
        out_shape=[jax.ShapeDtypeStruct((ROWS, KV), bf16)] * 2,
        compiler_params=params(1),
        cost_estimate=cost(3),
        name="relay_sums",
    )(*terms)


def after(x, *others):
    return lax.optimization_barrier((x, *others))[0]


def add(*terms):
    total = terms[0].astype(f32)
    for term in terms[1:]:
        total = total + term.astype(f32)
    return total.astype(bf16)


def body(hidden_in, value_cot, proj_weight, norm_gain, anchor, momentum, excluded, fragment):
    inner_rate = 0.01 / ROWS**0.5
    gain_rate = 0.1 / ROWS**0.5
    hidden, weight = hidden_in[0], proj_weight[0]
    here = lax.axis_index("fsdp")
    replica = lax.axis_index("replica")
    z, y, core = here // (NY * NC), (here // NC) % NY, here % NC
    scalars = jnp.stack([z, y, core, here * ROWS, fragment[0], replica]).astype(jnp.int32)

    w = {(0, 0): weight}
    w[1, 0] = shift(weight, -1, 0, 0, "ag_zm")
    w[0, 1] = shift(weight, 0, 1, 0, "ag_y")
    w[3, 0] = shift(weight, 1, 0, 0, "ag_zp")
    near = (w[0, 1], w[1, 0], w[3, 0])
    w[1, 1] = shift(after(w[0, 1], *near), -1, 0, 0, "ag_B")
    w[2, 0] = shift(after(w[3, 0], *near), 1, 0, 0, "ag_A")

    total = term_call(lax.axis_size("replica"), scalars, weight, anchor, momentum)
    first_term = total
    total = total + flip_replica(after(total, w[0, 1]), 1)
    first_sum = total
    total = total + flip_replica(total, 2)
    second_sum = total
    total = total + flip_replica(total, 6)

    mine, *send, inverse = norm_call(
        after(scalars, first_term), hidden, value_cot[0], norm_gain, excluded
    )
    masked = send[-1]
    recv = [shift(v, 0, 0, 1, "swap_x") for v in send]
    recv_cot = recv.pop()

    g = {}

    def make(places, waits, estimate):
        g.update(zip(places, grad_call(places, after(scalars, *waits), mine, recv, recv_cot, estimate)))

    make([(2, 1), (1, 1), (3, 1), (2, 0), (3, 0), (0, 1), (1, 0), (0, 0)], near, 16)
    far = shift(after(g[2, 1], first_sum), 0, 1, 0, "rs_D")
    w[2, 1] = shift(after(w[1, 1], g[2, 0]), -1, 0, 0, "ag_D")
    w[3, 1] = shift(after(w[0, 1], w[2, 0], g[2, 0]), 1, 0, 0, "ag_C")

    near_half, far_half = (0, 1), (3, 2)
    cots = (recv_cot, masked)
    sent0, own0 = half_call(
        near_half, after(scalars, g[0, 0]), recv, mine, cots, norm_gain, w, "half_near"
    )
    got0 = [shift(v, 0, 0, 1, "swap_w0") for v in sent0]
    near_order = [(dz, dy) for dz in near_half for dy in range(NY)]
    far_order = [(dz, dy) for dz in far_half for dy in range(NY)]
    near_sums = gain_call(near_order, after(scalars, sent0[0], second_sum), g, w)
    side = shift(after(g[1, 1], near_sums, w[2, 1]), 0, 1, 0, "rs_B")
    left = shift(after(g[3, 1], near_sums, w[2, 1]), -1, 0, 0, "rs_C")
    over = shift(add(g[2, 0], after(far, near_sums)), 1, 0, 0, "rs_A")
    partial = gain_call(far_order, after(scalars, near_sums), g, w, near_sums)
    sent1, own1 = half_call(
        far_half, after(scalars, sent0[0], far, partial), recv, mine, cots, norm_gain, w, "half_far"
    )
    got1 = [shift(v, 0, 0, 1, "swap_w1") for v in sent1]

    partial = partial + shift(partial, 0, 1, 0, "gain_y")
    partial = partial + flip_z(after(partial, sent1[0]), 1)
    from_next = shift(after(g[3, 0], left), -1, 0, 0, "rs_zm")
    to_side, to_last = relay_call(g[0, 1], left, g[1, 0], side, over)
    from_side = shift(to_side, 0, 1, 0, "rs_y")
    from_last = shift(to_last, 1, 0, 0, "rs_zp")

    values_out, hidden_grad = hidden_call(
        (*near_half, *far_half), after(scalars, left, side, over), hidden, masked, inverse,
        (*own0[:-1], *own1[:-1]), (*got0[:-1], *got1[:-1]),
        (own0[-1], own1[-1], got0[-1], got1[-1]),
    )

    partial = partial + flip_z(after(partial, to_last), 3)
    other = shift(after(partial, hidden_grad), 0, 0, 1, "gain_c")
    new_weight, anchor_out, momentum_out = update_call(
        inner_rate,
        scalars,
        weight,
        (after(g[0, 0], hidden_grad), from_last, from_side, from_next),
        total,
        anchor,
        momentum,
    )
    other = after(other, new_weight)
    even = jnp.where(core == 0, partial, other).reshape(HALF // ROWS, ROWS)
    odd = jnp.where(core == 0, other, partial).reshape(HALF // ROWS, ROWS)
    gain_grad = jnp.stack([even, odd], axis=1).reshape(1, D) / norm_gain
    new_gain = norm_gain - gain_rate * gain_grad

    return (
        values_out[None],
        hidden_grad[None],
        new_weight[None],
        new_gain,
        anchor_out,
        momentum_out,
    )


def solution(mesh):
    placed = (
        P("replica", "fsdp", None),
        P("replica", "fsdp", None),
        P("replica", "fsdp", None),
        P("replica", None),
        P(None, "fsdp", "replica", None),
        P(None, "fsdp", "replica", None),
        P("replica", None),
        P(),
    )
    return jax.shard_map(
        body,
        mesh=mesh,
        in_specs=placed,
        out_specs=(
            P("replica", "fsdp", None),
            P("replica", "fsdp", None),
            P("replica", "fsdp", None),
            P("replica", None),
            P(None, "fsdp", "replica", None),
            P(None, "fsdp", "replica", None),
        ),
        check_vma=False,
    )
```
